128 devices in a mesh: dp: 16 (over y, x), segment: 4 (over z), mp: 2 (over core).
Axes of the slice: x: 4, y: 4, z: 4, core: 2. Of those that a mesh axis runs over, the one named last changes fastest.
Arguments:
- trunk_in: bfloat16 [4096, 2560], P('dp', 'mp'), may hold values from -6 to 6
- norm_gain: bfloat16 [4, 2560], P('segment'), may hold values from 0.5 to 1.5
- w_gate: bfloat16 [4, 2560, 3584], P('segment', 'dp', 'mp'), may hold values from -0.125 to 0.125
- w_up: bfloat16 [4, 2560, 3584], P('segment', 'dp', 'mp'), may hold values from -0.125 to 0.125
- w_down: bfloat16 [4, 3584, 2560], P('segment', 'mp', 'dp'), may hold values from -0.09375 to 0.09375
- w_cond: bfloat16 [2560, 512], P('mp'), may hold values from -0.125 to 0.125
- w_time: bfloat16 [256, 512], replicated, may hold values from -0.375 to 0.375
- w_in: bfloat16 [70, 256], replicated, may hold values from -0.75 to 0.75
- w_mid: bfloat16 [1280, 256], replicated, may hold values from -0.15625 to 0.15625
- w_res: bfloat16 [14, 256], replicated, may hold values from -1.5 to 1.5
- w_out: bfloat16 [256, 14], replicated, may hold values from -0.375 to 0.375
- tsteps: int32 [256, 8], P('dp'), may hold values from 0 to 99
- advantage: float32 [256, 8], P('dp'), may hold values from -4 to 4
- actions: bfloat16 [256, 64, 14], P('dp'), may hold values from -6 to 6
- noise: bfloat16 [256, 8, 64, 14], P('dp'), may hold values from -6 to 6
Outputs:
- grad_w_in: float32 [70, 256], P(None, 'segment')
- grad_w_mid: float32 [1280, 256], P(None, 'segment')
- grad_w_res: float32 [14, 256], P(None, 'segment')
- grad_w_out: float32 [256, 14], P('segment')
- grad_w_time: float32 [256, 512], P(None, 'segment')
- grad_w_cond: float32 [2560, 512], P('mp', 'segment')
- grad_cond: float32 [256, 2560], P(('dp', 'segment'), 'mp')
- loss: float32 [1], replicated
The draws below stay inside these ranges and needn't reach their ends.
All inputs are finite; a program needn't handle non-finite values.
Results may differ from the reference program's by a relative error of at most 0.035.
Values may be sent and summed in bfloat16 or wider, within the bound.
A program may use at most 128 MiB of HBM per device.

```python
import math
import jax
import jax.numpy as jnp
from jax import lax

D = 2560
FF = 3584
C = 256
DSED = 256
H = 64
A = 14
GROUPS = 8
TSTEPS = 100
TPS = 16
SPD = 16
LEV = 8
SAMPLES = 256
TOKENS = 4096
N_DP = 16
N_SEGMENT = 4


def plant(values, own_key, least, largest):
    longest = values.shape.index(max(values.shape))
    spots = []
    for shift in (0, 1):
        where = [jax.random.randint(jax.random.fold_in(own_key, axis), (), 0, length) for axis, length in enumerate(values.shape)]
        where[longest] = (where[longest] + shift) % values.shape[longest]
        spots.append(tuple(where))
    return values.at[spots[0]].set(least).at[spots[1]].set(largest)


def block_levels(stream_key, shape, cuts, least, top_value):
    def one(axis_at, shards_of):
        steps = jax.random.uniform(jax.random.fold_in(jax.random.fold_in(stream_key, 6), axis_at), (shards_of,), jnp.float32, least / len(cuts), top_value / len(cuts))
        return jnp.repeat(jnp.exp(steps), shape[axis_at] // shards_of).reshape((-1,) + (1,) * (len(shape) - axis_at - 1))

    gain = one(*cuts[0])
    for cut in cuts[1:]:
        gain = gain * one(*cut)
    return gain


def centred(rng, dims, deviation, most, shards=(), kind=jnp.bfloat16):
    level = block_levels(rng, dims, shards, -0.22, 0.18) if shards else 1.0
    entries = jax.random.normal(rng, dims, jnp.float32) * deviation * level
    return jnp.minimum(jnp.maximum(entries, -most), most).astype(kind)


def setup_inputs(seed: int = 0) -> dict:
    seeds = jax.random.split(jax.random.key(seed), 16)
    trunk_in = centred(seeds[0], (TOKENS, D), 1.0, 6.0, ((0, 16), (1, 2)))
    norm_gain = jnp.clip(1.0 + 0.1 * jax.random.normal(seeds[1], (N_SEGMENT, D), jnp.float32), 0.5, 1.5).astype(jnp.bfloat16)
    w_gate = centred(seeds[2], (N_SEGMENT, D, FF), D ** -0.5, 0.125, ((0, 4), (1, 16), (2, 2)))
    w_up = centred(seeds[3], (N_SEGMENT, D, FF), D ** -0.5, 0.125, ((0, 4), (1, 16), (2, 2)))
    w_down = centred(seeds[4], (N_SEGMENT, FF, D), FF ** -0.5, 0.09375, ((0, 4), (1, 2), (2, 16)))
    w_cond = centred(seeds[5], (D, 2 * C), D ** -0.5, 0.125, ((0, 2),))
    w_time = centred(seeds[6], (DSED, 2 * C), DSED ** -0.5, 0.375)
    w_in = centred(seeds[7], (5 * A, C), (5 * A) ** -0.5, 0.75)
    w_mid = centred(seeds[8], (5 * C, C), (5 * C) ** -0.5, 0.15625)
    w_res = centred(seeds[9], (A, C), A ** -0.5, 1.5)
    w_out = centred(seeds[10], (C, A), C ** -0.5, 0.375)
    tsteps = plant(jax.random.randint(seeds[11], (SAMPLES, LEV), 0, TSTEPS), jax.random.fold_in(seeds[11], 1), 0, TSTEPS - 1).astype(jnp.int32)
    advantage = centred(seeds[12], (SAMPLES, LEV), 1.0, 4.0, ((0, 16),), jnp.float32)
    actions = centred(seeds[13], (SAMPLES, H, A), 1.0, 6.0, ((0, 16),))
    noise = centred(seeds[14], (SAMPLES, LEV, H, A), 1.0, 6.0, ((0, 16),))
    return {"trunk_in": trunk_in, "norm_gain": norm_gain, "w_gate": w_gate, "w_up": w_up, "w_down": w_down, "w_cond": w_cond, "w_time": w_time, "w_in": w_in, "w_mid": w_mid, "w_res": w_res, "w_out": w_out, "tsteps": tsteps, "advantage": advantage, "actions": actions, "noise": noise}


def mish_value(values):
    return values * jnp.tanh(jax.nn.softplus(values))

def mish_slope(values):
    soft = jnp.tanh(jax.nn.softplus(values))
    return soft + values * jax.nn.sigmoid(values) * (1.0 - soft * soft)

def contract(form, left, right):
    return jnp.einsum(form, left.astype(jnp.float32), right.astype(jnp.float32))

def alpha_table():
    grid = jnp.arange(TSTEPS + 1, dtype=jnp.float32) / TSTEPS
    curve = jnp.cos((grid + 0.008) / 1.008 * math.pi / 2.0) ** 2
    betas = jnp.minimum(1.0 - curve[1:] / curve[:-1], 0.999)
    return jnp.cumprod(1.0 - betas)

def norm_act(values):
    rows, steps, channels = values.shape
    grouped = values.reshape(rows, steps, GROUPS, channels // GROUPS)
    center = lax.optimization_barrier(jnp.mean(grouped, axis=(1, 3), keepdims=True))
    spread = lax.optimization_barrier(jnp.mean((grouped - center) ** 2, axis=(1, 3), keepdims=True))
    normed = (grouped - center) * lax.rsqrt(spread + 1e-05)
    return mish_value(normed.reshape(rows, steps, channels))

def columns(values):
    steps = values.shape[1]
    padded = jnp.pad(values, ((0, 0), (2, 2), (0, 0)))
    return jnp.concatenate([padded[:, tap:tap + steps] for tap in range(5)], axis=2)

def columns_adjoint(grads, width):
    total = 0.0
    for tap in range(5):
        piece = grads[:, :, tap * width:(tap + 1) * width]
        total = total + jnp.pad(piece, ((0, 0), (tap, 4 - tap), (0, 0)))
    return total[:, 2:-2]

def denoise(film_cond, tsteps, advantage, actions, noise, w_in, w_mid, w_res, w_out, w_time, product):
    row_count, levels = tsteps.shape
    horizon, action_dims = (actions.shape[1], actions.shape[2])
    channels = w_mid.shape[1]
    flat = row_count * levels
    matches = (tsteps[:, :, None] == jnp.arange(TSTEPS, dtype=jnp.int32)[None, None, :]).astype(jnp.float32)
    alpha = lax.optimization_barrier(jnp.sum(matches * alpha_table()[None, None, :], axis=2))
    keep_root = jnp.sqrt(alpha)[:, :, None, None]
    noise_root = jnp.sqrt(1.0 - alpha)[:, :, None, None]
    noisy_act = (keep_root * actions.astype(jnp.float32)[:, None] + noise_root * noise.astype(jnp.float32)).astype(jnp.bfloat16)
    noisy_act = noisy_act.reshape(flat, horizon, action_dims)
    half_dim = w_time.shape[0] // 2
    frequencies = jnp.exp(-math.log(10000.0) * jnp.arange(half_dim, dtype=jnp.float32) / (half_dim - 1))
    angles = tsteps.astype(jnp.float32)[:, :, None] * frequencies[None, None, :]
    embedded = jnp.concatenate([jnp.sin(angles), jnp.cos(angles)], axis=2)
    time_act = mish_value(embedded).astype(jnp.bfloat16).reshape(flat, 2 * half_dim)
    film = film_cond[:, None, :] + product('rld,dc->rlc', time_act.reshape(row_count, levels, -1), w_time)
    film = film.reshape(flat, 2 * channels)
    film_scale = film[:, None, :channels]
    film_shift = film[:, None, channels:]
    columns_in = columns(noisy_act)
    pre_first = product('mhk,kc->mhc', columns_in, w_in)
    act_first, first_back = jax.vjp(norm_act, pre_first)
    modulated = (film_scale * act_first + film_shift).astype(jnp.bfloat16)
    columns_mid = columns(modulated)
    pre_second = product('mhk,kc->mhc', columns_mid, w_mid)
    act_second, second_back = jax.vjp(norm_act, pre_second)
    block_out = (act_second + product('mha,ac->mhc', noisy_act, w_res)).astype(jnp.bfloat16)
    predicted = product('mhc,ca->mha', block_out, w_out)
    errors = predicted - noise.reshape(flat, horizon, action_dims).astype(jnp.float32)
    err_sum = jnp.sum(errors * errors) / (horizon * action_dims)
    weights = advantage.reshape(flat, 1, 1)
    d_pred = (2.0 * weights * errors / (horizon * action_dims)).astype(jnp.bfloat16)
    grad_out = product('mhc,mha->ca', block_out, d_pred)
    d_block = product('mha,ca->mhc', d_pred, w_out)
    grad_res = product('mha,mhc->ac', noisy_act, d_block.astype(jnp.bfloat16))
    d_second = second_back(d_block)[0].astype(jnp.bfloat16)
    grad_mid = product('mhk,mhc->kc', columns_mid, d_second)
    d_columns = product('mhc,kc->mhk', d_second, w_mid)
    d_modulated = columns_adjoint(d_columns, channels)
    d_film = jnp.concatenate([lax.optimization_barrier(jnp.sum(d_modulated * act_first, axis=1)), lax.optimization_barrier(jnp.sum(d_modulated, axis=1))], axis=1)
    d_first = first_back(film_scale * d_modulated)[0].astype(jnp.bfloat16)
    grad_in = product('mhk,mhc->kc', columns_in, d_first)
    grad_time = product('md,mc->dc', time_act, d_film.astype(jnp.bfloat16))
    d_film_cond = lax.optimization_barrier(jnp.sum(d_film.reshape(row_count, levels, -1), axis=1))
    return (err_sum, grad_in, grad_mid, grad_res, grad_out, grad_time, d_film_cond)

def reference(trunk_in, norm_gain, w_gate, w_up, w_down, w_cond, w_time, w_in, w_mid, w_res, w_out, tsteps, advantage, actions, noise):
    hidden_state = trunk_in
    for section in range(N_SEGMENT):
        widened = hidden_state.astype(jnp.float32)
        factor = lax.rsqrt(lax.optimization_barrier(jnp.mean(widened * widened, axis=1, keepdims=True)) + 1e-05)
        normed = (widened * factor * norm_gain[section].astype(jnp.float32)).astype(jnp.bfloat16)
        gate_out = jnp.dot(normed, w_gate[section], preferred_element_type=jnp.float32)
        up_out = jnp.dot(normed, w_up[section], preferred_element_type=jnp.float32)
        hidden = (jax.nn.silu(gate_out) * up_out).astype(jnp.bfloat16)
        hidden_state = (widened + jnp.dot(hidden, w_down[section], preferred_element_type=jnp.float32)).astype(jnp.bfloat16)
    cond = lax.optimization_barrier(jnp.mean(hidden_state.reshape(SAMPLES, TPS, D).astype(jnp.float32), axis=1)).astype(jnp.bfloat16)
    cond_act = mish_value(cond.astype(jnp.float32)).astype(jnp.bfloat16)
    film_cond = jnp.dot(cond_act, w_cond, preferred_element_type=jnp.float32)

    def per_group(pieces):
        return denoise(pieces[0], pieces[1], pieces[2], pieces[3], pieces[4], w_in, w_mid, w_res, w_out, w_time, contract)
    grouped = (film_cond.reshape(N_DP, SPD, -1), tsteps.reshape(N_DP, SPD, LEV), advantage.reshape(N_DP, SPD, LEV), actions.reshape(N_DP, SPD, H, A), noise.reshape(N_DP, SPD, LEV, H, A))
    outcome = lax.map(per_group, grouped)
    err_sum = jnp.sum(outcome[0])
    grad_w_in = lax.optimization_barrier(jnp.sum(outcome[1], axis=0))
    grad_w_mid = lax.optimization_barrier(jnp.sum(outcome[2], axis=0))
    grad_w_res = lax.optimization_barrier(jnp.sum(outcome[3], axis=0))
    grad_w_out = lax.optimization_barrier(jnp.sum(outcome[4], axis=0))
    grad_w_time = lax.optimization_barrier(jnp.sum(outcome[5], axis=0))
    d_film_cond = outcome[6].reshape(SAMPLES, -1).astype(jnp.bfloat16)
    grad_w_cond = contract('sd,sc->dc', cond_act, d_film_cond)
    grad_cond = contract('sc,dc->sd', d_film_cond, w_cond) * mish_slope(cond.astype(jnp.float32))
    loss = (err_sum / (SAMPLES * LEV)).reshape(1)
    return (grad_w_in, grad_w_mid, grad_w_res, grad_w_out, grad_w_time, grad_w_cond, grad_cond, loss)
```

```python
import functools
import math

import jax
import jax.numpy as jnp
import numpy as np
from jax import lax
from jax.experimental import pallas as pl
from jax.experimental.pallas import tpu as pltpu
from jax.sharding import PartitionSpec as P

MESH = pl.DeviceIdType.MESH
GROUPS = 8
TSTEPS = 100
SIDE = 4
MICRO = 4
ROWS = 32
D = 2560
HALF = 1280
FH = 1792
SHARD = 160
CUT = 80
TILE = 256


def schedule():
    grid = np.arange(TSTEPS + 1, dtype=np.float64) / TSTEPS
    curve = np.cos((grid + 0.008) / 1.008 * math.pi / 2.0) ** 2
    betas = np.minimum(1.0 - curve[1:] / curve[:-1], 0.999)
    return np.cumprod(1.0 - betas)


def trunk_kernel(
    x_ref, gain_ref, wg_ref, wu_ref, wd_ref, wc_ref,
    cond_ref, wcond_ref,
    weights, first, arrived, leaving, normed, hidden, partial, share, other,
    own_sem, gs_sem, gr_sem, ms_sem, mr_sem, zs_sem, zr_sem, cs_sem, cr_sem,
):
    dp, seg, core = lax.axis_index("dp"), lax.axis_index("segment"), lax.axis_index("mp")
    y, x = dp // SIDE, dp % SIDE
    sibling = 1 - core

    def at(axis, delta):
        if axis == "x":
            return y * SIDE + (x + delta + SIDE) % SIDE
        return ((y + delta + SIDE) % SIDE) * SIDE + x

    barrier = pltpu.get_barrier_semaphore()
    for axis in ("x", "y"):
        for delta in (1, -1):
            pl.semaphore_signal(barrier, inc=1, device_id={"dp": at(axis, delta)}, device_id_type=MESH)
    pl.semaphore_signal(barrier, inc=1, device_id={"mp": sibling}, device_id_type=MESH)
    for step in range(1, 4):
        pl.semaphore_signal(barrier, inc=1, device_id={"segment": (seg + step) % 4}, device_id_type=MESH)
    pl.semaphore_wait(barrier, 8)

    sources = (wg_ref, wu_ref, wd_ref)
    chunks = [(which, part) for which in range(3) for part in range(2)]

    def spot(which, part, px, py, begin=0, size=CUT):
        row = (py * SIDE + px) * SHARD + part * CUT + begin
        return weights.at[which, pl.ds(pl.multiple_of(row, 16), size), :]

    def place(chunk, p_off, q_off, begin=0, size=CUT):
        which, part = chunk
        dx, dy = (p_off, q_off) if part == 0 else (q_off, p_off)
        return spot(which, part, (x + dx + SIDE) % SIDE, (y + dy + SIDE) % SIDE, begin, size)

    def axes(chunk):
        return ("x", "y") if chunk[1] == 0 else ("y", "x")

    def piece(chunk, kind):
        return (0, 48) if kind == 0 else (48, 32)

    def make(chunk, number, src, dst, axis, delta):
        q = chunks.index(chunk)
        return pltpu.make_async_remote_copy(
            src_ref=src, dst_ref=dst, send_sem=gs_sem.at[q, number], recv_sem=gr_sem.at[q, number],
            device_id={"dp": at(axis, delta)}, device_id_type=MESH,
        )

    OFF = (0, -1, 1, 2)

    def spec(chunk, number):
        p_axis, q_axis = axes(chunk)
        if number < 4:
            delta = 1 if number % 2 == 0 else -1
            if number < 2:
                return p_axis, delta, 0, 0, 0, CUT
            begin, size = piece(chunk, number - 2)
            return p_axis, delta, -delta, 0, begin, size
        slot, kind = divmod(number - 4, 4)
        delta = 1 if kind % 2 == 0 else -1
        if kind < 2:
            return q_axis, delta, OFF[slot], 0, 0, CUT
        begin, size = piece(chunk, kind - 2)
        return q_axis, delta, OFF[slot], -delta, begin, size

    def source_of(chunk, number):
        _, _, p_off, q_off, begin, size = spec(chunk, number)
        if p_off == 0 and q_off == 0:
            return sources[chunk[0]].at[pl.ds(chunk[1] * CUT + begin, size), :]
        return place(chunk, p_off, q_off, begin, size)

    def send(chunk, number):
        axis, delta, p_off, q_off, begin, size = spec(chunk, number)
        make(chunk, number, source_of(chunk, number), place(chunk, p_off, q_off, begin, size), axis, delta).start()

    def receive(chunk, number):
        axis, delta, p_off, q_off, begin, size = spec(chunk, number)
        if number < 4:
            p_off = p_off - delta
        else:
            q_off = q_off - delta
        spot_here = place(chunk, p_off, q_off, begin, size)
        make(chunk, number, spot_here, spot_here, axis, delta).wait_recv()

    def sent(chunk, number):
        axis, delta, p_off, q_off, begin, size = spec(chunk, number)
        make(chunk, number, source_of(chunk, number), place(chunk, p_off, q_off, begin, size), axis, delta).wait_send()

    own = []
    for chunk in chunks:
        for number in (0, 1, 4, 5):
            send(chunk, number)
    for which in range(3):
        keep = pltpu.make_async_copy(
            sources[which], weights.at[which, pl.ds(pl.multiple_of(dp * SHARD, 16), SHARD), :], own_sem.at[which]
        )
        keep.start()
        own.append(keep)

    def sibling_copy(number, src, dst):
        return pltpu.make_async_remote_copy(
            src_ref=src, dst_ref=dst, send_sem=ms_sem.at[number], recv_sem=mr_sem.at[number],
            device_id={"mp": sibling}, device_id_type=MESH,
        )

    here = pl.ds(pl.multiple_of(core * HALF, 128), HALF)
    there = pl.ds(pl.multiple_of(sibling * HALF, 128), HALF)
    for j in range(MICRO):
        src = x_ref.at[pl.ds(pl.multiple_of(64 * j + 32 * sibling, 16), ROWS), :]
        sibling_copy(j, src, first.at[j, :, here]).start()
        kept = pltpu.make_async_copy(
            x_ref.at[pl.ds(pl.multiple_of(64 * j + 32 * core, 16), ROWS), :], first.at[j, :, here], own_sem.at[3 + j]
        )
        kept.start()
        own.append(kept)
    here_rows = wcond_ref.at[pl.ds(pl.multiple_of(core * HALF, 16), HALF), :]
    there_rows = wcond_ref.at[pl.ds(pl.multiple_of(sibling * HALF, 16), HALF), :]
    sibling_copy(4, wc_ref, here_rows).start()
    kept = pltpu.make_async_copy(wc_ref, here_rows, own_sem.at[7])
    kept.start()
    own.append(kept)
    cond_ref[...] = jnp.zeros_like(cond_ref)

    for chunk in chunks:
        for number in (0, 1):
            receive(chunk, number)
            send(chunk, 2 + number)
            slot = 1 + number
            send(chunk, 4 + 4 * slot)
            send(chunk, 5 + 4 * slot)
        for kind in (0, 1):
            receive(chunk, 4 + kind)
            send(chunk, 6 + kind)
    for chunk in chunks:
        for number in (2, 3):
            receive(chunk, number)
        send(chunk, 16)
        send(chunk, 17)
        for slot in (1, 2):
            for kind in (0, 1):
                receive(chunk, 4 + 4 * slot + kind)
                send(chunk, 6 + 4 * slot + kind)
    for chunk in chunks:
        for kind in (0, 1):
            receive(chunk, 16 + kind)
            send(chunk, 18 + kind)
    for j in range(MICRO):
        sibling_copy(j, first.at[j, :, there], first.at[j, :, there]).wait_recv()
    for chunk in chunks:
        for slot in range(4):
            for kind in (2, 3):
                receive(chunk, 4 + 4 * slot + kind)
    for keep in own:
        keep.wait()

    def z_copy(j):
        return pltpu.make_async_remote_copy(
            src_ref=leaving.at[j], dst_ref=arrived.at[j], send_sem=zs_sem.at[j], recv_sem=zr_sem.at[j],
            device_id={"segment": (seg + 1) % 4}, device_id_type=MESH,
        )

    def cond_copy(j, target):
        return pltpu.make_async_remote_copy(
            src_ref=cond_ref.at[j], dst_ref=cond_ref.at[j], send_sem=cs_sem.at[j, target], recv_sem=cr_sem.at[j],
            device_id={"segment": target}, device_id_type=MESH,
        )

    gain = gain_ref[...].astype(jnp.float32)

    def micro(j, carry):
        @pl.when(seg == 0)
        def _():
            arrived[j] = first[j]

        @pl.when(seg > 0)
        def _():
            z_copy(j).wait_recv()

        state = arrived[j].astype(jnp.float32)
        factor = lax.rsqrt(jnp.mean(state * state, axis=1, keepdims=True) + 1e-05)
        normed[j, 0:ROWS] = (state * factor * gain).astype(jnp.bfloat16)
        swap = sibling_copy(5 + j, normed.at[j, pl.ds(0, ROWS)], normed.at[j, pl.ds(ROWS, ROWS)])
        swap.start()
        swap.wait_recv()

        def up(n, carry):
            cols = pl.ds(pl.multiple_of(n * TILE, TILE), TILE)
            rows = normed[j]
            gate = jnp.dot(rows, weights[0, :, cols], preferred_element_type=jnp.float32)
            lift = jnp.dot(rows, weights[1, :, cols], preferred_element_type=jnp.float32)
            hidden[:, cols] = (gate / (1.0 + jnp.exp(-gate)) * lift).astype(jnp.bfloat16)
            return carry

        lax.fori_loop(0, FH // TILE, up, 0)

        def down(n, carry):
            cols = pl.ds(pl.multiple_of(n * TILE, TILE), TILE)
            out = lax.dot_general(
                hidden[...], weights[2, cols, :], (((1,), (1,)), ((), ())), preferred_element_type=jnp.float32
            )
            partial[:, cols] = out[0:ROWS]
            share[j, :, cols] = out[ROWS:].astype(jnp.bfloat16)
            return carry

        lax.fori_loop(0, D // TILE, down, 0)
        back = sibling_copy(9 + j, share.at[j], other.at[j])
        back.start()
        back.wait_recv()
        result = (arrived[j].astype(jnp.float32) + (partial[...] + other[j].astype(jnp.float32))).astype(jnp.bfloat16)

        @pl.when(seg < 3)
        def _():
            leaving[j] = result
            z_copy(j).start()

        @pl.when(seg == 3)
        def _():
            mean = jnp.mean(result.astype(jnp.float32).reshape(2, 16, D), axis=1)
            cond_ref[j, 0:2] = mean.astype(jnp.bfloat16).astype(jnp.float32)
            for target in range(3):
                cond_copy(j, target).start()

        return carry

    lax.fori_loop(0, MICRO, micro, 0)

    for chunk in chunks:
        for number in range(20):
            sent(chunk, number)
    for j in range(MICRO):
        sibling_copy(j, x_ref.at[pl.ds(0, ROWS), :], first.at[j, :, there]).wait_send()
        sibling_copy(5 + j, normed.at[j, pl.ds(0, ROWS)], normed.at[j, pl.ds(ROWS, ROWS)]).wait_send()
        sibling_copy(9 + j, share.at[j], other.at[j]).wait_send()

        @pl.when(seg < 3)
        def _(j=j):
            z_copy(j).wait_send()
            cond_copy(j, 0).wait_recv()

        @pl.when(seg == 3)
        def _(j=j):
            for target in range(3):
                cond_copy(j, target).wait_send()

    last = sibling_copy(4, wc_ref, there_rows)
    last.wait_recv()
    last.wait_send()


def trunk(trunk_in, norm_gain, w_gate, w_up, w_down_t, w_cond):
    anywhere = pl.BlockSpec(memory_space=pl.ANY)
    vmem = pl.BlockSpec(memory_space=pltpu.VMEM)
    dma = pltpu.SemaphoreType.DMA
    bf16 = jnp.bfloat16
    return pl.pallas_call(
        trunk_kernel,
        out_shape=(
            jax.ShapeDtypeStruct((MICRO, 8, D), jnp.float32),
            jax.ShapeDtypeStruct((D, w_cond.shape[1]), bf16),
        ),
        in_specs=[anywhere, vmem, anywhere, anywhere, anywhere, anywhere],
        out_specs=(vmem, anywhere),
        scratch_shapes=[
            pltpu.VMEM((3, D, FH), bf16),
            pltpu.VMEM((MICRO, ROWS, D), bf16),
            pltpu.VMEM((MICRO, ROWS, D), bf16),
            pltpu.VMEM((MICRO, ROWS, D), bf16),
            pltpu.VMEM((MICRO, 2 * ROWS, D), bf16),
            pltpu.VMEM((2 * ROWS, FH), bf16),
            pltpu.VMEM((ROWS, D), jnp.float32),
            pltpu.VMEM((MICRO, ROWS, D), bf16),
            pltpu.VMEM((MICRO, ROWS, D), bf16),
            dma((8,)),
            dma((6, 20)),
            dma((6, 20)),
            dma((13,)),
            dma((13,)),
            dma((MICRO,)),
            dma((MICRO,)),
            dma((MICRO, 3)),
            dma((MICRO,)),
        ],
        compiler_params=pltpu.CompilerParams(
            collective_id=0, has_side_effects=True, vmem_limit_bytes=52 * 2**20
        ),
    )(trunk_in, norm_gain, w_gate, w_up, w_down_t, w_cond)


def mish_parts(values):
    small = jnp.exp(-jnp.abs(values))
    right = values > 0
    top = jnp.where(right, 1.0 + 2.0 * small, small * (small + 2.0))
    rest = jnp.where(right, 2.0 * small * small, 2.0)
    return small, right, top, rest


def mish_value(values):
    _, _, top, rest = mish_parts(values)
    return values * (top / (top + rest))


def mish_slope(values):
    small, right, top, rest = mish_parts(values)
    inverse = 1.0 / (top + rest)
    logistic = jnp.where(right, 1.0, small) / (1.0 + small)
    return top * inverse + values * logistic * (rest * (2.0 * top + rest)) * (inverse * inverse)


def collect_kernel(
    cond_ref, film_ref, grads_ref, wc_ref,
    total_ref, gwc_ref, gcond_ref,
    cond_sib, act_all, film_sib, film_out, film_z, film_all,
    mp_in, z_out, z_in, x_out, x_in, y_out, y_in, full,
    ms_sem, mr_sem, zs_sem, zr_sem, xs_sem, xr_sem, ys_sem, yr_sem,
):
    dp, seg, core = lax.axis_index("dp"), lax.axis_index("segment"), lax.axis_index("mp")
    y, x = dp // SIDE, dp % SIDE
    sibling = 1 - core

    def x_peer(step):
        return {"dp": y * SIDE + (x + step) % SIDE}

    def y_peer(step):
        return {"dp": ((y + step) % SIDE) * SIDE + x}

    def z_peer(step):
        return {"segment": (seg + step) % SIDE}

    barrier = pltpu.get_barrier_semaphore()
    pl.semaphore_signal(barrier, inc=1, device_id={"mp": sibling}, device_id_type=MESH)
    for step in range(1, SIDE):
        for peer in (x_peer, y_peer, z_peer):
            pl.semaphore_signal(barrier, inc=1, device_id=peer(step), device_id_type=MESH)
    pl.semaphore_wait(barrier, 10)

    def copy(src, dst, out_sem, in_sem, peer):
        return pltpu.make_async_remote_copy(
            src_ref=src, dst_ref=dst, send_sem=out_sem, recv_sem=in_sem, device_id=peer, device_id_type=MESH
        )

    started = []

    def launch(src, dst, out_sem, in_sem, peer):
        one = copy(src, dst, out_sem, in_sem, peer)
        one.start()
        started.append(one)

    def arrive(dst, in_sem):
        copy(dst, dst, ms_sem.at[0], in_sem, {"mp": sibling}).wait_recv()

    def to_sibling(number, src, dst):
        launch(src, dst, ms_sem.at[number], mr_sem.at[number], {"mp": sibling})

    def scatter(out_sem, in_sem, number, src, dst, me, peer):
        for step in range(1, SIDE):
            launch(
                src.at[(me + step) % SIDE], dst.at[me], out_sem.at[number, step - 1], in_sem.at[number, step - 1], peer(step)
            )

    def spread(out_sem, in_sem, number, slots, me, peer):
        for step in range(1, SIDE):
            launch(slots.at[me], slots.at[me], out_sem.at[number, step - 1], in_sem.at[number, step - 1], peer(step))

    def gathered(in_sem, number, slots, me):
        for step in range(1, SIDE):
            arrive(slots.at[(me - step + SIDE) % SIDE], in_sem.at[number, step - 1])

    def added(slots):
        pieces = [slots[k].astype(jnp.float32) for k in range(SIDE)]
        return (pieces[0] + pieces[1]) + (pieces[2] + pieces[3])

    here = pl.ds(pl.multiple_of(core * HALF, 128), HALF)
    there = pl.ds(pl.multiple_of(sibling * HALF, 128), HALF)
    mine = pl.ds(pl.multiple_of(core * 512, 128), 512)
    others = pl.ds(pl.multiple_of(sibling * 512, 128), 512)

    to_sibling(0, film_ref, film_sib)
    to_sibling(1, grads_ref.at[:, others, :], mp_in)
    to_sibling(2, cond_ref.at[:, :, there], cond_sib)

    arrive(film_sib, mr_sem.at[0])
    film_out[...] = jnp.zeros_like(film_out)
    for s in range(SIDE):
        film_out[s, 0:2] = film_ref[0:2, 128 * s : 128 * (s + 1)]
        film_out[s, 2:4] = film_sib[0:2, 128 * s : 128 * (s + 1)]
    scatter(zs_sem, zr_sem, 0, film_out, film_z, seg, z_peer)
    film_z[seg] = film_out[seg]

    arrive(mp_in, mr_sem.at[1])
    z_out[...] = (grads_ref[:, mine, :].astype(jnp.float32) + mp_in[...].astype(jnp.float32)).astype(jnp.bfloat16)
    scatter(zs_sem, zr_sem, 1, z_out, z_in, seg, z_peer)
    z_in[seg] = z_out[seg]

    arrive(cond_sib, mr_sem.at[2])
    rows = [cond_ref[j, 0:2, here] for j in range(MICRO)] + [cond_sib[j, 0:2] for j in range(MICRO)]
    act_all[y, x] = mish_value(jnp.concatenate(rows, axis=0)).astype(jnp.bfloat16)
    spread(xs_sem, xr_sem, 0, act_all.at[y], x, x_peer)

    gathered(zr_sem, 0, film_z, seg)
    rows = [film_z[j, 0:2] for j in range(MICRO)] + [film_z[j, 2:4] for j in range(MICRO)]
    film_all[y, x] = jnp.concatenate(rows, axis=0).astype(jnp.bfloat16)
    spread(xs_sem, xr_sem, 1, film_all.at[y], x, x_peer)

    low = jnp.where(core == 0, film_ref[0:2], film_sib[0:2])
    high = jnp.where(core == 0, film_sib[0:2], film_ref[0:2])
    film_rows = jnp.concatenate([low, high, jnp.zeros((12, 512), jnp.float32)], axis=0).astype(jnp.bfloat16)
    own_cond, sib_cond = cond_ref[seg, 0:2, here], cond_sib[seg, 0:2]
    cond_rows = jnp.concatenate(
        [jnp.where(core == 0, own_cond, sib_cond), jnp.where(core == 0, sib_cond, own_cond)], axis=0
    )
    back = lax.dot_general(film_rows, wc_ref[...], (((1,), (1,)), ((), ())), preferred_element_type=jnp.float32)
    gcond_ref[...] = back[0:4] * mish_slope(cond_rows)

    gathered(zr_sem, 1, z_in, seg)
    x_out[...] = added(z_in).astype(jnp.bfloat16).reshape(x_out.shape)
    scatter(xs_sem, xr_sem, 2, x_out, x_in, x, x_peer)
    x_in[x] = x_out[x]

    gathered(xr_sem, 0, act_all.at[y], x)
    spread(ys_sem, yr_sem, 0, act_all, y, y_peer)
    gathered(xr_sem, 1, film_all.at[y], x)
    spread(ys_sem, yr_sem, 1, film_all, y, y_peer)

    gathered(xr_sem, 2, x_in, x)
    y_out[...] = added(x_in).astype(jnp.bfloat16).reshape(y_out.shape)
    scatter(ys_sem, yr_sem, 2, y_out, y_in, y, y_peer)
    y_in[y] = y_out[y]
    gathered(yr_sem, 2, y_in, y)
    full[core, x, y] = added(y_in).astype(jnp.bfloat16)
    spread(ys_sem, yr_sem, 3, full.at[core, x], y, y_peer)
    gathered(yr_sem, 3, full.at[core, x], y)
    spread(xs_sem, xr_sem, 3, full.at[core], x, x_peer)

    gathered(yr_sem, 0, act_all, y)
    gathered(yr_sem, 1, film_all, y)

    gathered(xr_sem, 3, full.at[core], x)
    to_sibling(3, full.at[core], full.at[core])
    gwc_ref[...] = lax.dot_general(
        act_all[...].reshape(256, HALF), film_all[...].reshape(256, 128), (((0,), (0,)), ((), ())),
        preferred_element_type=jnp.float32,
    )
    arrive(full.at[sibling], mr_sem.at[3])
    total_ref[...] = full[...].astype(jnp.float32).reshape(total_ref.shape)
    for one in started:
        one.wait_send()


def collect(cond, film, grads, w_cond):
    vmem = pl.BlockSpec(memory_space=pltpu.VMEM)
    dma = pltpu.SemaphoreType.DMA
    bf16, f32 = jnp.bfloat16, jnp.float32
    return pl.pallas_call(
        collect_kernel,
        out_shape=(
            jax.ShapeDtypeStruct((1024, 128), f32),
            jax.ShapeDtypeStruct((HALF, 128), f32),
            jax.ShapeDtypeStruct((4, HALF), f32),
        ),
        in_specs=[vmem] * 4,
        out_specs=(vmem, vmem, vmem),
        scratch_shapes=[
            pltpu.VMEM((MICRO, 8, HALF), f32),
            pltpu.VMEM((SIDE, SIDE, 16, HALF), bf16),
            pltpu.VMEM((8, 512), f32),
            pltpu.VMEM((SIDE, 8, 128), f32),
            pltpu.VMEM((SIDE, 8, 128), f32),
            pltpu.VMEM((SIDE, SIDE, 16, 128), bf16),
            pltpu.VMEM((SIDE, 512, 128), bf16),
            pltpu.VMEM((SIDE, 512, 128), bf16),
            pltpu.VMEM((SIDE, 512, 128), bf16),
            pltpu.VMEM((SIDE, 128, 128), bf16),
            pltpu.VMEM((SIDE, 128, 128), bf16),
            pltpu.VMEM((SIDE, 32, 128), bf16),
            pltpu.VMEM((SIDE, 32, 128), bf16),
            pltpu.VMEM((2, SIDE, SIDE, 32, 128), bf16),
            dma((4,)), dma((4,)),
            dma((2, 3)), dma((2, 3)),
            dma((4, 3)), dma((4, 3)),
            dma((4, 3)), dma((4, 3)),
        ],
        compiler_params=pltpu.CompilerParams(
            collective_id=1, has_side_effects=True, vmem_limit_bytes=32 * 2**20
        ),
    )(cond, film, grads, w_cond)


def contract(form, left, right):
    return jnp.einsum(form, left, right, preferred_element_type=jnp.float32)


def norm_act(values):
    rows, steps, channels = values.shape
    grouped = values.reshape(rows, steps, GROUPS, channels // GROUPS)
    center = jnp.mean(grouped, axis=(1, 3), keepdims=True)
    spread = jnp.mean((grouped - center) ** 2, axis=(1, 3), keepdims=True)
    normed = (grouped - center) * lax.rsqrt(spread + 1e-05)
    return mish_value(normed.reshape(rows, steps, channels))


def columns(values):
    steps = values.shape[1]
    padded = jnp.pad(values, ((0, 0), (2, 2), (0, 0)))
    return jnp.concatenate([padded[:, tap : tap + steps] for tap in range(5)], axis=2)


def columns_adjoint(grads, width):
    total = 0.0
    for tap in range(5):
        piece = grads[:, :, tap * width : (tap + 1) * width]
        total = total + jnp.pad(piece, ((0, 0), (tap, 4 - tap), (0, 0)))
    return total[:, 2:-2]


def denoise(
    film_cond, tsteps, advantage, actions, noise, w_in, w_mid, w_res, w_out, w_time, product
):
    row_count, levels = tsteps.shape
    horizon, action_dims = (actions.shape[1], actions.shape[2])
    channels = w_mid.shape[1]
    flat = row_count * levels
    matches = (tsteps[:, :, None] == jnp.arange(TSTEPS, dtype=jnp.int32)[None, None, :]).astype(
        jnp.float32
    )
    alpha = jnp.sum(matches * jnp.asarray(schedule(), jnp.float32)[None, None, :], axis=2)
    keep_root = jnp.sqrt(alpha)[:, :, None, None]
    noise_root = jnp.sqrt(1.0 - alpha)[:, :, None, None]
    noisy_act = (
        keep_root * actions.astype(jnp.float32)[:, None] + noise_root * noise.astype(jnp.float32)
    ).astype(jnp.bfloat16)
    noisy_act = noisy_act.reshape(flat, horizon, action_dims)
    half_dim = w_time.shape[0] // 2
    frequencies = jnp.exp(
        -math.log(10000.0) * jnp.arange(half_dim, dtype=jnp.float32) / (half_dim - 1)
    )
    angles = tsteps.astype(jnp.float32)[:, :, None] * frequencies[None, None, :]
    embedded = jnp.concatenate([jnp.sin(angles), jnp.cos(angles)], axis=2)
    time_act = mish_value(embedded).astype(jnp.bfloat16).reshape(flat, 2 * half_dim)
    film = film_cond[:, None, :] + product(
        "rld,dc->rlc", time_act.reshape(row_count, levels, -1), w_time
    )
    film = film.reshape(flat, 2 * channels)
    film_scale = film[:, None, :channels]
    film_shift = film[:, None, channels:]
    columns_in = columns(noisy_act)
    pre_first = product("mhk,kc->mhc", columns_in, w_in)
    act_first, first_back = jax.vjp(norm_act, pre_first)
    modulated = (film_scale * act_first + film_shift).astype(jnp.bfloat16)
    columns_mid = columns(modulated)
    pre_second = product("mhk,kc->mhc", columns_mid, w_mid)
    act_second, second_back = jax.vjp(norm_act, pre_second)
    block_out = (act_second + product("mha,ac->mhc", noisy_act, w_res)).astype(jnp.bfloat16)
    predicted = product("mhc,ca->mha", block_out, w_out)
    errors = predicted - noise.reshape(flat, horizon, action_dims).astype(jnp.float32)
    err_sum = jnp.sum(errors * errors) / (horizon * action_dims)
    weights = advantage.reshape(flat, 1, 1)
    d_pred = (2.0 * weights * errors / (horizon * action_dims)).astype(jnp.bfloat16)
    grad_out = product("mhc,mha->ca", block_out, d_pred)
    d_block = product("mha,ca->mhc", d_pred, w_out)
    grad_res = product("mha,mhc->ac", noisy_act, d_block.astype(jnp.bfloat16))
    d_second = second_back(d_block)[0].astype(jnp.bfloat16)
    grad_mid = product("mhk,mhc->kc", columns_mid, d_second)
    d_columns = product("mhc,kc->mhk", d_second, w_mid)
    d_modulated = columns_adjoint(d_columns, channels)
    d_film = jnp.concatenate(
        [jnp.sum(d_modulated * act_first, axis=1), jnp.sum(d_modulated, axis=1)], axis=1
    )
    d_first = first_back(film_scale * d_modulated)[0].astype(jnp.bfloat16)
    grad_in = product("mhk,mhc->kc", columns_in, d_first)
    grad_time = product("md,mc->dc", time_act, d_film.astype(jnp.bfloat16))
    d_film_cond = jnp.sum(d_film.reshape(row_count, levels, -1), axis=1)
    return (err_sum, grad_in, grad_mid, grad_res, grad_out, grad_time, d_film_cond)


def body(
    trunk_in, norm_gain, w_gate, w_up, w_down, w_cond, w_time, w_in, w_mid, w_res, w_out,
    tsteps, advantage, actions, noise,
):
    seg, core = lax.axis_index("segment"), lax.axis_index("mp")
    cond_all, w_cond_full = trunk(trunk_in, norm_gain, w_gate[0], w_up[0], w_down[0].T, w_cond)
    cond = lax.dynamic_index_in_dim(cond_all, seg, 0, keepdims=False)[0:2]
    cond_act = mish_value(cond).astype(jnp.bfloat16)
    film_cond = jnp.dot(cond_act, w_cond_full, preferred_element_type=jnp.float32)
    begin = 4 * seg + 2 * core

    def own(values):
        return lax.dynamic_slice_in_dim(values, begin, 2, 0)

    err_sum, grad_in, grad_mid, grad_res, grad_out, grad_time, d_film_cond = denoise(
        film_cond, own(tsteps), own(advantage), own(actions), own(noise), w_in, w_mid, w_res, w_out, w_time, contract
    )
    blocks = []
    for s in range(4):
        part = slice(64 * s, 64 * (s + 1))
        upper = jnp.concatenate([grad_mid[:640, part], grad_mid[640:, part]], axis=1)
        low = jnp.concatenate(
            [grad_res[:, part], jnp.zeros((2, 64)), grad_out[part].T, jnp.zeros((2, 64)), jnp.full((48, 64), err_sum)], axis=0
        )
        middle = jnp.concatenate([jnp.pad(grad_in[:, part], ((0, 10), (0, 0))), low], axis=1)
        blocks.append(
            jnp.concatenate([upper, middle, grad_time[:, 128 * s : 128 * (s + 1)], jnp.zeros((48, 128))], axis=0)
        )
    packed = jnp.stack(blocks).astype(jnp.bfloat16)
    film_pad = jnp.pad(d_film_cond, ((0, 6), (0, 0)))
    total, grad_w_cond, grad_cond = collect(cond_all, film_pad, packed, w_cond)
    side = total[640:720, 64:]
    return (
        total[640:710, :64],
        jnp.concatenate([total[:640, :64], total[:640, 64:]], axis=0),
        side[0:14],
        side[16:30].T,
        total[720:976],
        grad_w_cond,
        grad_cond,
        side[32, 0:1] / 2048.0,
    )


def solution(mesh):
    in_specs = (
        P("dp", "mp"),
        P("segment", None),
        P("segment", "dp", "mp"),
        P("segment", "dp", "mp"),
        P("segment", "mp", "dp"),
        P("mp", None),
        P(),
        P(),
        P(),
        P(),
        P(),
        P("dp", None),
        P("dp", None),
        P("dp", None, None),
        P("dp", None, None, None),
    )
    out_specs = (
        P(None, "segment"),
        P(None, "segment"),
        P(None, "segment"),
        P("segment", None),
        P(None, "segment"),
        P("mp", "segment"),
        P(("dp", "segment"), "mp"),
        P(),
    )
    return jax.shard_map(body, mesh=mesh, in_specs=in_specs, out_specs=out_specs, check_vma=False)
```

```python
import functools
import math

import jax
import jax.numpy as jnp
import numpy as np
from jax import lax
from jax.experimental import pallas as pl
from jax.experimental.pallas import tpu as pltpu
from jax.sharding import PartitionSpec as P

MESH = pl.DeviceIdType.MESH
TSTEPS = 100
SIDE = 4
MICRO = 4
ROWS = 32
D = 2560
HALF = 1280
FH = 1792
SHARD = 160
CUT = 80
TILE = 256


def schedule():
    grid = np.arange(TSTEPS + 1, dtype=np.float64) / TSTEPS
    curve = np.cos((grid + 0.008) / 1.008 * math.pi / 2.0) ** 2
    betas = np.minimum(1.0 - curve[1:] / curve[:-1], 0.999)
    return np.cumprod(1.0 - betas)


def trunk_kernel(
    x_ref, gain_ref, wg_ref, wu_ref, wd_ref, wc_ref,
    cond_ref, wcond_ref,
    weights, first, arrived, leaving, normed, hidden, partial, share, other,
    own_sem, gs_sem, gr_sem, ms_sem, mr_sem, zs_sem, zr_sem, cs_sem, cr_sem,
):
    dp, seg, core = lax.axis_index("dp"), lax.axis_index("segment"), lax.axis_index("mp")
    y, x = dp // SIDE, dp % SIDE
    sibling = 1 - core

    def at(axis, delta):
        if axis == "x":
            return y * SIDE + (x + delta + SIDE) % SIDE
        return ((y + delta + SIDE) % SIDE) * SIDE + x

    barrier = pltpu.get_barrier_semaphore()
    for axis in ("x", "y"):
        for delta in (1, -1):
            pl.semaphore_signal(barrier, inc=1, device_id={"dp": at(axis, delta)}, device_id_type=MESH)
    pl.semaphore_signal(barrier, inc=1, device_id={"mp": sibling}, device_id_type=MESH)
    for step in range(1, 4):
        pl.semaphore_signal(barrier, inc=1, device_id={"segment": (seg + step) % 4}, device_id_type=MESH)
    pl.semaphore_wait(barrier, 8)

    sources = (wg_ref, wu_ref, wd_ref)
    chunks = [(which, part) for which in range(3) for part in range(2)]

    def spot(which, part, px, py, begin=0, size=CUT):
        row = (py * SIDE + px) * SHARD + part * CUT + begin
        return weights.at[which, pl.ds(pl.multiple_of(row, 16), size), :]

    def place(chunk, p_off, q_off, begin=0, size=CUT):
        which, part = chunk
        dx, dy = (p_off, q_off) if part == 0 else (q_off, p_off)
        return spot(which, part, (x + dx + SIDE) % SIDE, (y + dy + SIDE) % SIDE, begin, size)

    def axes(chunk):
        return ("x", "y") if chunk[1] == 0 else ("y", "x")

    def piece(chunk, kind):
        return (0, 48) if kind == 0 else (48, 32)

    def make(chunk, number, src, dst, axis, delta):
        q = chunks.index(chunk)
        return pltpu.make_async_remote_copy(
            src_ref=src, dst_ref=dst, send_sem=gs_sem.at[q, number], recv_sem=gr_sem.at[q, number],
            device_id={"dp": at(axis, delta)}, device_id_type=MESH,
        )

    OFF = (0, -1, 1, 2)

    def spec(chunk, number):
        p_axis, q_axis = axes(chunk)
        if number < 4:
            delta = 1 if number % 2 == 0 else -1
            if number < 2:
                return p_axis, delta, 0, 0, 0, CUT
            begin, size = piece(chunk, number - 2)
            return p_axis, delta, -delta, 0, begin, size
        slot, kind = divmod(number - 4, 4)
        delta = 1 if kind % 2 == 0 else -1
        if kind < 2:
            return q_axis, delta, OFF[slot], 0, 0, CUT
        begin, size = piece(chunk, kind - 2)
        return q_axis, delta, OFF[slot], -delta, begin, size

    def source_of(chunk, number):
        _, _, p_off, q_off, begin, size = spec(chunk, number)
        if p_off == 0 and q_off == 0:
            return sources[chunk[0]].at[pl.ds(chunk[1] * CUT + begin, size), :]
        return place(chunk, p_off, q_off, begin, size)

    def send(chunk, number):
        axis, delta, p_off, q_off, begin, size = spec(chunk, number)
        make(chunk, number, source_of(chunk, number), place(chunk, p_off, q_off, begin, size), axis, delta).start()

    def receive(chunk, number):
        axis, delta, p_off, q_off, begin, size = spec(chunk, number)
        if number < 4:
            p_off = p_off - delta
        else:
            q_off = q_off - delta
        spot_here = place(chunk, p_off, q_off, begin, size)
        make(chunk, number, spot_here, spot_here, axis, delta).wait_recv()

    def sent(chunk, number):
        axis, delta, p_off, q_off, begin, size = spec(chunk, number)
        make(chunk, number, source_of(chunk, number), place(chunk, p_off, q_off, begin, size), axis, delta).wait_send()

    own = []
    for chunk in chunks:
        for number in (0, 1, 4, 5):
            send(chunk, number)
    for which in range(3):
        keep = pltpu.make_async_copy(
            sources[which], weights.at[which, pl.ds(pl.multiple_of(dp * SHARD, 16), SHARD), :], own_sem.at[which]
        )
        keep.start()
        own.append(keep)

    def sibling_copy(number, src, dst):
        return pltpu.make_async_remote_copy(
            src_ref=src, dst_ref=dst, send_sem=ms_sem.at[number], recv_sem=mr_sem.at[number],
            device_id={"mp": sibling}, device_id_type=MESH,
        )

    here = pl.ds(pl.multiple_of(core * HALF, 128), HALF)
    there = pl.ds(pl.multiple_of(sibling * HALF, 128), HALF)
    for j in range(MICRO):
        src = x_ref.at[pl.ds(pl.multiple_of(64 * j + 32 * sibling, 16), ROWS), :]
        sibling_copy(j, src, first.at[j, :, here]).start()
        kept = pltpu.make_async_copy(
            x_ref.at[pl.ds(pl.multiple_of(64 * j + 32 * core, 16), ROWS), :], first.at[j, :, here], own_sem.at[3 + j]
        )
        kept.start()
        own.append(kept)
    here_rows = wcond_ref.at[pl.ds(pl.multiple_of(core * HALF, 16), HALF), :]
    there_rows = wcond_ref.at[pl.ds(pl.multiple_of(sibling * HALF, 16), HALF), :]
    sibling_copy(4, wc_ref, here_rows).start()
    kept = pltpu.make_async_copy(wc_ref, here_rows, own_sem.at[7])
    kept.start()
    own.append(kept)
    cond_ref[...] = jnp.zeros_like(cond_ref)

    for chunk in chunks:
        for number in (0, 1):
            receive(chunk, number)
            send(chunk, 2 + number)
            slot = 1 + number
            send(chunk, 4 + 4 * slot)
            send(chunk, 5 + 4 * slot)
        for kind in (0, 1):
            receive(chunk, 4 + kind)
            send(chunk, 6 + kind)
    for chunk in chunks:
        for number in (2, 3):
            receive(chunk, number)
        send(chunk, 16)
        send(chunk, 17)
        for slot in (1, 2):
            for kind in (0, 1):
                receive(chunk, 4 + 4 * slot + kind)
                send(chunk, 6 + 4 * slot + kind)
    for chunk in chunks:
        for kind in (0, 1):
            receive(chunk, 16 + kind)
            send(chunk, 18 + kind)
    for j in range(MICRO):
        sibling_copy(j, first.at[j, :, there], first.at[j, :, there]).wait_recv()
    for chunk in chunks:
        for slot in range(4):
            for kind in (2, 3):
                receive(chunk, 4 + 4 * slot + kind)
    for keep in own:
        keep.wait()

    def z_copy(j):
        return pltpu.make_async_remote_copy(
            src_ref=leaving.at[j], dst_ref=arrived.at[j], send_sem=zs_sem.at[j], recv_sem=zr_sem.at[j],
            device_id={"segment": (seg + 1) % 4}, device_id_type=MESH,
        )

    def cond_copy(j, target):
        return pltpu.make_async_remote_copy(
            src_ref=cond_ref.at[j], dst_ref=cond_ref.at[j], send_sem=cs_sem.at[j, target], recv_sem=cr_sem.at[j],
            device_id={"segment": target}, device_id_type=MESH,
        )

    gain = gain_ref[...].astype(jnp.float32)

    def micro(j, carry):
        @pl.when(seg == 0)
        def _():
            arrived[j] = first[j]

        @pl.when(seg > 0)
        def _():
            z_copy(j).wait_recv()

        state = arrived[j].astype(jnp.float32)
        factor = lax.rsqrt(jnp.mean(state * state, axis=1, keepdims=True) + 1e-05)
        normed[j, 0:ROWS] = (state * factor * gain).astype(jnp.bfloat16)
        swap = sibling_copy(5 + j, normed.at[j, pl.ds(0, ROWS)], normed.at[j, pl.ds(ROWS, ROWS)])
        swap.start()
        swap.wait_recv()

        def up(n, carry):
            cols = pl.ds(pl.multiple_of(n * TILE, TILE), TILE)
            rows = normed[j]
            gate = jnp.dot(rows, weights[0, :, cols], preferred_element_type=jnp.float32)
            lift = jnp.dot(rows, weights[1, :, cols], preferred_element_type=jnp.float32)
            hidden[:, cols] = (gate / (1.0 + jnp.exp(-gate)) * lift).astype(jnp.bfloat16)
            return carry

        lax.fori_loop(0, FH // TILE, up, 0)

        def down(n, carry):
            cols = pl.ds(pl.multiple_of(n * TILE, TILE), TILE)
            out = lax.dot_general(
                hidden[...], weights[2, cols, :], (((1,), (1,)), ((), ())), preferred_element_type=jnp.float32
            )
            partial[:, cols] = out[0:ROWS]
            share[j, :, cols] = out[ROWS:].astype(jnp.bfloat16)
            return carry

        lax.fori_loop(0, D // TILE, down, 0)
        back = sibling_copy(9 + j, share.at[j], other.at[j])
        back.start()
        back.wait_recv()
        result = (arrived[j].astype(jnp.float32) + (partial[...] + other[j].astype(jnp.float32))).astype(jnp.bfloat16)

        @pl.when(seg < 3)
        def _():
            leaving[j] = result
            z_copy(j).start()

        @pl.when(seg == 3)
        def _():
            mean = jnp.mean(result.astype(jnp.float32).reshape(2, 16, D), axis=1)
            cond_ref[j, 0:2] = mean.astype(jnp.bfloat16).astype(jnp.float32)
            for target in range(3):
                cond_copy(j, target).start()

        return carry

    lax.fori_loop(0, MICRO, micro, 0)

    for chunk in chunks:
        for number in range(20):
            sent(chunk, number)
    for j in range(MICRO):
        sibling_copy(j, x_ref.at[pl.ds(0, ROWS), :], first.at[j, :, there]).wait_send()
        sibling_copy(5 + j, normed.at[j, pl.ds(0, ROWS)], normed.at[j, pl.ds(ROWS, ROWS)]).wait_send()
        sibling_copy(9 + j, share.at[j], other.at[j]).wait_send()

        @pl.when(seg < 3)
        def _(j=j):
            z_copy(j).wait_send()
            cond_copy(j, 0).wait_recv()

        @pl.when(seg == 3)
        def _(j=j):
            for target in range(3):
                cond_copy(j, target).wait_send()

    last = sibling_copy(4, wc_ref, there_rows)
    last.wait_recv()
    last.wait_send()


def trunk(trunk_in, norm_gain, w_gate, w_up, w_down_t, w_cond):
    anywhere = pl.BlockSpec(memory_space=pl.ANY)
    vmem = pl.BlockSpec(memory_space=pltpu.VMEM)
    dma = pltpu.SemaphoreType.DMA
    bf16 = jnp.bfloat16
    return pl.pallas_call(
        trunk_kernel,
        out_shape=(
            jax.ShapeDtypeStruct((MICRO, 8, D), jnp.float32),
            jax.ShapeDtypeStruct((D, w_cond.shape[1]), bf16),
        ),
        in_specs=[anywhere, vmem, anywhere, anywhere, anywhere, anywhere],
        out_specs=(vmem, anywhere),
        scratch_shapes=[
            pltpu.VMEM((3, D, FH), bf16),
            pltpu.VMEM((MICRO, ROWS, D), bf16),
            pltpu.VMEM((MICRO, ROWS, D), bf16),
            pltpu.VMEM((MICRO, ROWS, D), bf16),
            pltpu.VMEM((MICRO, 2 * ROWS, D), bf16),
            pltpu.VMEM((2 * ROWS, FH), bf16),
            pltpu.VMEM((ROWS, D), jnp.float32),
            pltpu.VMEM((MICRO, ROWS, D), bf16),
            pltpu.VMEM((MICRO, ROWS, D), bf16),
            dma((8,)),
            dma((6, 20)),
            dma((6, 20)),
            dma((13,)),
            dma((13,)),
            dma((MICRO,)),
            dma((MICRO,)),
            dma((MICRO, 3)),
            dma((MICRO,)),
        ],
        compiler_params=pltpu.CompilerParams(
            collective_id=0, has_side_effects=True, vmem_limit_bytes=52 * 2**20
        ),
    )(trunk_in, norm_gain, w_gate, w_up, w_down_t, w_cond)


def mish_parts(values):
    small = jnp.exp(-jnp.abs(values))
    right = values > 0
    top = jnp.where(right, 1.0 + 2.0 * small, small * (small + 2.0))
    rest = jnp.where(right, 2.0 * small * small, 2.0)
    return small, right, top, rest


def mish_value(values):
    _, _, top, rest = mish_parts(values)
    return values * (top / (top + rest))


def mish_slope(values):
    small, right, top, rest = mish_parts(values)
    inverse = 1.0 / (top + rest)
    logistic = jnp.where(right, 1.0, small) / (1.0 + small)
    return top * inverse + values * logistic * (rest * (2.0 * top + rest)) * (inverse * inverse)


def collect_kernel(
    cond_ref, film_ref, grads_ref, wc_ref,
    total_ref, gwc_ref, gcond_ref,
    cond_sib, act_all, film_sib, film_out, film_z, film_all,
    mp_in, z_out, z_in, x_out, x_in, y_out, y_in, full,
    ms_sem, mr_sem, zs_sem, zr_sem, xs_sem, xr_sem, ys_sem, yr_sem,
):
    dp, seg, core = lax.axis_index("dp"), lax.axis_index("segment"), lax.axis_index("mp")
    y, x = dp // SIDE, dp % SIDE
    sibling = 1 - core

    def x_peer(step):
        return {"dp": y * SIDE + (x + step) % SIDE}

    def y_peer(step):
        return {"dp": ((y + step) % SIDE) * SIDE + x}

    def z_peer(step):
        return {"segment": (seg + step) % SIDE}

    barrier = pltpu.get_barrier_semaphore()
    pl.semaphore_signal(barrier, inc=1, device_id={"mp": sibling}, device_id_type=MESH)
    for step in range(1, SIDE):
        for peer in (x_peer, y_peer, z_peer):
            pl.semaphore_signal(barrier, inc=1, device_id=peer(step), device_id_type=MESH)
    pl.semaphore_wait(barrier, 10)

    def copy(src, dst, out_sem, in_sem, peer):
        return pltpu.make_async_remote_copy(
            src_ref=src, dst_ref=dst, send_sem=out_sem, recv_sem=in_sem, device_id=peer, device_id_type=MESH
        )

    started = []

    def launch(src, dst, out_sem, in_sem, peer):
        one = copy(src, dst, out_sem, in_sem, peer)
        one.start()
        started.append(one)

    def arrive(dst, in_sem):
        copy(dst, dst, ms_sem.at[0], in_sem, {"mp": sibling}).wait_recv()

    def to_sibling(number, src, dst):
        launch(src, dst, ms_sem.at[number], mr_sem.at[number], {"mp": sibling})

    def scatter(out_sem, in_sem, number, src, dst, me, peer):
        for step in range(1, SIDE):
            launch(
                src.at[(me + step) % SIDE], dst.at[me], out_sem.at[number, step - 1], in_sem.at[number, step - 1], peer(step)
            )

    def spread(out_sem, in_sem, number, slots, me, peer):
        for step in range(1, SIDE):
            launch(slots.at[me], slots.at[me], out_sem.at[number, step - 1], in_sem.at[number, step - 1], peer(step))

    def gathered(in_sem, number, slots, me):
        for step in range(1, SIDE):
            arrive(slots.at[(me - step + SIDE) % SIDE], in_sem.at[number, step - 1])

    def added(slots):
        pieces = [slots[k].astype(jnp.float32) for k in range(SIDE)]
        return (pieces[0] + pieces[1]) + (pieces[2] + pieces[3])

    here = pl.ds(pl.multiple_of(core * HALF, 128), HALF)
    there = pl.ds(pl.multiple_of(sibling * HALF, 128), HALF)
    mine = pl.ds(pl.multiple_of(core * 512, 128), 512)
    others = pl.ds(pl.multiple_of(sibling * 512, 128), 512)

    to_sibling(0, film_ref, film_sib)
    to_sibling(1, grads_ref.at[:, others, :], mp_in)
    to_sibling(2, cond_ref.at[:, :, there], cond_sib)

    arrive(film_sib, mr_sem.at[0])
    film_out[...] = jnp.zeros_like(film_out)
    for s in range(SIDE):
        film_out[s, 0:2] = film_ref[0:2, 128 * s : 128 * (s + 1)]
        film_out[s, 2:4] = film_sib[0:2, 128 * s : 128 * (s + 1)]
    scatter(zs_sem, zr_sem, 0, film_out, film_z, seg, z_peer)
    film_z[seg] = film_out[seg]

    arrive(mp_in, mr_sem.at[1])
    z_out[...] = (grads_ref[:, mine, :].astype(jnp.float32) + mp_in[...].astype(jnp.float32)).astype(jnp.bfloat16)
    scatter(zs_sem, zr_sem, 1, z_out, z_in, seg, z_peer)
    z_in[seg] = z_out[seg]

    arrive(cond_sib, mr_sem.at[2])
    rows = [cond_ref[j, 0:2, here] for j in range(MICRO)] + [cond_sib[j, 0:2] for j in range(MICRO)]
    act_all[y, x] = mish_value(jnp.concatenate(rows, axis=0)).astype(jnp.bfloat16)
    spread(xs_sem, xr_sem, 0, act_all.at[y], x, x_peer)

    gathered(zr_sem, 0, film_z, seg)
    rows = [film_z[j, 0:2] for j in range(MICRO)] + [film_z[j, 2:4] for j in range(MICRO)]
    film_all[y, x] = jnp.concatenate(rows, axis=0).astype(jnp.bfloat16)
    spread(xs_sem, xr_sem, 1, film_all.at[y], x, x_peer)

    low = jnp.where(core == 0, film_ref[0:2], film_sib[0:2])
    high = jnp.where(core == 0, film_sib[0:2], film_ref[0:2])
    film_rows = jnp.concatenate([low, high, jnp.zeros((12, 512), jnp.float32)], axis=0).astype(jnp.bfloat16)
    own_cond, sib_cond = cond_ref[seg, 0:2, here], cond_sib[seg, 0:2]
    cond_rows = jnp.concatenate(
        [jnp.where(core == 0, own_cond, sib_cond), jnp.where(core == 0, sib_cond, own_cond)], axis=0
    )
    back = lax.dot_general(film_rows, wc_ref[...], (((1,), (1,)), ((), ())), preferred_element_type=jnp.float32)
    gcond_ref[...] = back[0:4] * mish_slope(cond_rows)

    gathered(zr_sem, 1, z_in, seg)
    x_out[...] = added(z_in).astype(jnp.bfloat16).reshape(x_out.shape)
    scatter(xs_sem, xr_sem, 2, x_out, x_in, x, x_peer)
    x_in[x] = x_out[x]

    gathered(xr_sem, 0, act_all.at[y], x)
    spread(ys_sem, yr_sem, 0, act_all, y, y_peer)
    gathered(xr_sem, 1, film_all.at[y], x)
    spread(ys_sem, yr_sem, 1, film_all, y, y_peer)

    gathered(xr_sem, 2, x_in, x)
    y_out[...] = added(x_in).astype(jnp.bfloat16).reshape(y_out.shape)
    scatter(ys_sem, yr_sem, 2, y_out, y_in, y, y_peer)
    y_in[y] = y_out[y]
    gathered(yr_sem, 2, y_in, y)
    full[core, x, y] = added(y_in).astype(jnp.bfloat16)
    spread(ys_sem, yr_sem, 3, full.at[core, x], y, y_peer)
    gathered(yr_sem, 3, full.at[core, x], y)
    spread(xs_sem, xr_sem, 3, full.at[core], x, x_peer)

    gathered(yr_sem, 0, act_all, y)
    gathered(yr_sem, 1, film_all, y)

    gathered(xr_sem, 3, full.at[core], x)
    to_sibling(3, full.at[core], full.at[core])
    gwc_ref[...] = lax.dot_general(
        act_all[...].reshape(256, HALF), film_all[...].reshape(256, 128), (((0,), (0,)), ((), ())),
        preferred_element_type=jnp.float32,
    )
    arrive(full.at[sibling], mr_sem.at[3])
    total_ref[...] = full[...].astype(jnp.float32).reshape(total_ref.shape)
    for one in started:
        one.wait_send()


def collect(cond, film, grads, w_cond):
    vmem = pl.BlockSpec(memory_space=pltpu.VMEM)
    dma = pltpu.SemaphoreType.DMA
    bf16, f32 = jnp.bfloat16, jnp.float32
    return pl.pallas_call(
        collect_kernel,
        out_shape=(
            jax.ShapeDtypeStruct((1024, 128), f32),
            jax.ShapeDtypeStruct((HALF, 128), f32),
            jax.ShapeDtypeStruct((4, HALF), f32),
        ),
        in_specs=[vmem] * 4,
        out_specs=(vmem, vmem, vmem),
        scratch_shapes=[
            pltpu.VMEM((MICRO, 8, HALF), f32),
            pltpu.VMEM((SIDE, SIDE, 16, HALF), bf16),
            pltpu.VMEM((8, 512), f32),
            pltpu.VMEM((SIDE, 8, 128), f32),
            pltpu.VMEM((SIDE, 8, 128), f32),
            pltpu.VMEM((SIDE, SIDE, 16, 128), bf16),
            pltpu.VMEM((SIDE, 512, 128), bf16),
            pltpu.VMEM((SIDE, 512, 128), bf16),
            pltpu.VMEM((SIDE, 512, 128), bf16),
            pltpu.VMEM((SIDE, 128, 128), bf16),
            pltpu.VMEM((SIDE, 128, 128), bf16),
            pltpu.VMEM((SIDE, 32, 128), bf16),
            pltpu.VMEM((SIDE, 32, 128), bf16),
            pltpu.VMEM((2, SIDE, SIDE, 32, 128), bf16),
            dma((4,)), dma((4,)),
            dma((2, 3)), dma((2, 3)),
            dma((4, 3)), dma((4, 3)),
            dma((4, 3)), dma((4, 3)),
        ],
        compiler_params=pltpu.CompilerParams(
            collective_id=1, has_side_effects=True, vmem_limit_bytes=32 * 2**20
        ),
    )(cond, film, grads, w_cond)


FLATS = 16
STEPS = 64
C = 256
BLOCK = 256


def denoise_kernel(
    film_cond_ref, noise_ref, actions_ref, keep_ref, blend_ref, adv_ref, time_ref,
    win_ref, wres_ref, wmid_ref, wmid_t_ref, wout_ref, wout_t_ref, wtime_ref,
    packed_ref, film_ref,
    npad, cols, pad, mid, back, pre, res, unit1, act1, slope1, unit2, slope2, block, d_block, d_pred,
    d_second, d_first, film, d_film, sum1, sum2, inv1, inv2, mean1, mean2,
):
    bf16, f32 = jnp.bfloat16, jnp.float32

    def rows_of(f, size=STEPS):
        return pl.ds(pl.multiple_of(f * size, size), size)

    def one(f):
        return pl.ds(f, 1)

    def each(body, count=FLATS):
        def step(f, carry):
            body(f)
            return carry

        lax.fori_loop(0, count, step, 0)

    lanes = lax.broadcasted_iota(jnp.int32, (C, C), 1)
    row_ids = lax.broadcasted_iota(jnp.int32, (C, C), 0)
    same = jnp.where(lanes // 32 == row_ids // 32, 1.0 / 2048.0, 0.0).astype(f32)

    def group_mean(values):
        return jnp.dot(values, same, preferred_element_type=f32, precision=lax.Precision.HIGHEST)

    def dot(left, right):
        return jnp.dot(left, right, preferred_element_type=f32)

    npad[...] = jnp.zeros_like(npad)
    pad[...] = jnp.zeros_like(pad)

    def make_cols(f):
        sample = rows_of(f // 8)
        noisy = keep_ref[one(f)] * actions_ref[sample].astype(f32) + blend_ref[one(f)] * noise_ref[rows_of(f)].astype(f32)
        noisy = noisy.astype(bf16).astype(f32)
        npad[f, 8:72] = noisy
        total = pltpu.roll(noisy, 114, 1)
        for tap in range(5):
            total = total + pltpu.roll(npad[f, 6 + tap : 70 + tap], 44 + 14 * tap, 1)
        cols[rows_of(f)] = total.astype(bf16)

    each(make_cols)

    time_film = dot(time_ref[...], wtime_ref[...])
    top = jnp.broadcast_to(film_cond_ref[0:1], (8, 2 * C))
    low = jnp.broadcast_to(film_cond_ref[1:2], (8, 2 * C))
    film[...] = jnp.concatenate([top, low], axis=0) + time_film

    def first_conv(b):
        rows = rows_of(b, BLOCK)
        out = dot(cols[rows], win_ref[...])
        pre[rows] = out
        res[rows] = dot(cols[rows], wres_ref[...])

    each(first_conv, 4)

    def centre(inverse):
        def total(f):
            sum1[one(f)] = jnp.sum(pre[rows_of(f)], axis=0, keepdims=True)

        each(total)
        mean1[...] = group_mean(sum1[...])

        def moved(f):
            left = pre[rows_of(f)] - mean1[one(f)]
            pre[rows_of(f)] = left
            sum1[one(f)] = jnp.sum(left * left, axis=0, keepdims=True)

        each(moved)
        inverse[...] = lax.rsqrt(group_mean(sum1[...]) + 1e-05)

    def mish_both(values):
        small, right, above, rest = mish_parts(values)
        inverse = 1.0 / (above + rest)
        logistic = jnp.where(right, 1.0, small) / (1.0 + small)
        ratio = above * inverse
        value = values * ratio
        return value, ratio + values * logistic * (rest * (2.0 * above + rest)) * (inverse * inverse)

    centre(inv1)

    def first_act(f):
        unit = pre[rows_of(f)] * inv1[one(f)]
        value, slope = mish_both(unit)
        unit1[rows_of(f)] = unit
        act1[rows_of(f)] = value
        slope1[rows_of(f)] = slope
        changed = film[one(f), 0:C] * value + film[one(f), C:]
        pad[f, 8:72] = changed.astype(bf16).astype(f32)
        for tap in range(5):
            mid[rows_of(f), C * tap : C * (tap + 1)] = pad[f, 6 + tap : 70 + tap].astype(bf16)

    each(first_act)

    def second_conv(b):
        rows = rows_of(b, BLOCK)
        pre[rows] = dot(mid[rows], wmid_ref[...])

    each(second_conv, 4)
    centre(inv2)

    def second_act(f):
        unit = pre[rows_of(f)] * inv2[one(f)]
        value, slope = mish_both(unit)
        unit2[rows_of(f)] = unit
        slope2[rows_of(f)] = slope
        block[rows_of(f)] = (value + res[rows_of(f)]).astype(bf16)

    each(second_act)

    def errors(f, total):
        rows = rows_of(f)
        error = dot(block[rows], wout_ref[...]) - noise_ref[rows].astype(f32)
        d_pred[rows] = (adv_ref[one(f)] * error * (2.0 / 896.0)).astype(bf16)
        return total + error * error

    err = lax.fori_loop(0, FLATS, errors, jnp.zeros((STEPS, 128), f32))
    err_sum = jnp.sum(err) * (1.0 / 896.0)

    def from_pred(b):
        rows = rows_of(b, BLOCK)
        out = dot(d_pred[rows], wout_t_ref[...])
        pre[rows] = out
        d_block[rows] = out.astype(bf16)

    each(from_pred, 4)

    def act_back(scale, unit, slope):
        def totals(f):
            grad = scale(f) * slope[rows_of(f)]
            pre[rows_of(f)] = grad
            sum1[one(f)] = jnp.sum(grad, axis=0, keepdims=True)
            sum2[one(f)] = jnp.sum(grad * unit[rows_of(f)], axis=0, keepdims=True)

        each(totals)
        mean1[...] = group_mean(sum1[...])
        mean2[...] = group_mean(sum2[...])

    act_back(lambda f: pre[rows_of(f)], unit2, slope2)

    def second_back(f):
        grad = inv2[one(f)] * (pre[rows_of(f)] - mean1[one(f)] - unit2[rows_of(f)] * mean2[one(f)])
        rounded = grad.astype(bf16)
        d_second[rows_of(f)] = rounded
        pad[f, 8:72] = rounded.astype(f32)
        for tap in range(5):
            back[rows_of(f), C * tap : C * (tap + 1)] = pad[f, 10 - tap : 74 - tap].astype(bf16)

    each(second_back)

    def mid_back(b):
        rows = rows_of(b, BLOCK)
        pre[rows] = dot(back[rows], wmid_t_ref[...])

    each(mid_back, 4)

    def film_back(f):
        grad = pre[rows_of(f)]
        d_film[one(f), 0:C] = jnp.sum(grad * act1[rows_of(f)], axis=0, keepdims=True)
        d_film[one(f), C:] = jnp.sum(grad, axis=0, keepdims=True)

    each(film_back)
    film_ref[...] = jnp.zeros_like(film_ref)
    film_ref[0:1] = jnp.sum(d_film[0:8], axis=0, keepdims=True)
    film_ref[1:2] = jnp.sum(d_film[8:16], axis=0, keepdims=True)

    act_back(lambda f: pre[rows_of(f)] * film[one(f), 0:C], unit1, slope1)

    def first_back(f):
        grad = inv1[one(f)] * (pre[rows_of(f)] - mean1[one(f)] - unit1[rows_of(f)] * mean2[one(f)])
        d_first[rows_of(f)] = grad.astype(bf16)

    each(first_back)

    def over_rows(left, right):
        return lax.dot_general(left, right, (((0,), (0,)), ((), ())), preferred_element_type=f32)

    for tap in range(5):
        grad = over_rows(d_second[...], mid[:, C * tap : C * (tap + 1)]).astype(bf16)
        for s in range(4):
            for half in range(2):
                begin = 64 * (2 * tap + half)
                packed_ref[s, begin : begin + 64] = grad[64 * s : 64 * (s + 1), 128 * half : 128 * (half + 1)]
    lane = lax.broadcasted_iota(jnp.int32, (C, 128), 1)
    inner = over_rows(d_first[...], cols[...])
    skip = over_rows(d_block[...], cols[...])
    out = over_rows(block[...], d_pred[...])
    joined = jnp.where(lane < 70, inner, jnp.where(lane < 84, skip, jnp.where(lane < 98, out, err_sum))).astype(bf16)
    timed = over_rows(time_ref[...], d_film[...].astype(bf16)).astype(bf16)
    for s in range(4):
        packed_ref[s, 640:704] = joined[64 * s : 64 * (s + 1)]
        packed_ref[s, 704:960] = timed[:, 128 * s : 128 * (s + 1)]
        packed_ref[s, 960:1024] = jnp.zeros((64, 128), bf16)


def denoise(film_cond, tsteps, advantage, actions, noise, w_time, w_in, w_mid, w_res, w_out):
    bf16, f32 = jnp.bfloat16, jnp.float32
    flat = tsteps.reshape(FLATS, 1)
    table = schedule()
    picked = (flat == jnp.arange(TSTEPS, dtype=jnp.int32)[None]).astype(f32)
    keep = jnp.sum(picked * jnp.asarray(np.sqrt(table), f32)[None], axis=1, keepdims=True)
    blend = jnp.sum(picked * jnp.asarray(np.sqrt(1.0 - table), f32)[None], axis=1, keepdims=True)

    def wide(values):
        return jnp.broadcast_to(values, (FLATS, 128))

    half_dim = w_time.shape[0] // 2
    frequencies = jnp.exp(-math.log(10000.0) * jnp.arange(half_dim, dtype=f32) / (half_dim - 1))
    angles = flat.astype(f32) * frequencies[None]
    time_act = mish_value(jnp.concatenate([jnp.sin(angles), jnp.cos(angles)], axis=1)).astype(bf16)
    noise_lanes = jnp.pad(noise.reshape(FLATS * STEPS, 14), ((0, 0), (84, 30)))
    action_lanes = jnp.pad(actions.reshape(2 * STEPS, 14), ((0, 0), (84, 30)))
    w_mid_t = w_mid.reshape(5, C, C).transpose(0, 2, 1).reshape(5 * C, C)
    vmem = pl.BlockSpec(memory_space=pltpu.VMEM)
    flat_rows = FLATS * STEPS
    big, small = pltpu.VMEM((flat_rows, C), f32), pltpu.VMEM((FLATS, C), f32)
    big16 = pltpu.VMEM((flat_rows, C), bf16)
    return pl.pallas_call(
        denoise_kernel,
        out_shape=(jax.ShapeDtypeStruct((4, 1024, 128), bf16), jax.ShapeDtypeStruct((8, 2 * C), f32)),
        in_specs=[vmem] * 14,
        out_specs=(vmem, vmem),
        scratch_shapes=[
            pltpu.VMEM((FLATS, 80, 128), f32),
            pltpu.VMEM((flat_rows, 128), bf16),
            pltpu.VMEM((FLATS, 80, C), f32),
            pltpu.VMEM((flat_rows, 5 * C), bf16),
            pltpu.VMEM((flat_rows, 5 * C), bf16),
            big, big, big, big, big, big, big,
            big16, big16,
            pltpu.VMEM((flat_rows, 128), bf16),
            big16, big16,
            pltpu.VMEM((FLATS, 2 * C), f32),
            pltpu.VMEM((FLATS, 2 * C), f32),
            small, small, small, small, small, small,
        ],
        compiler_params=pltpu.CompilerParams(vmem_limit_bytes=48 * 2**20),
    )(
        film_cond, noise_lanes, action_lanes, wide(keep), wide(blend), wide(advantage.reshape(FLATS, 1)), time_act,
        jnp.pad(w_in, ((0, 58), (0, 0))), jnp.pad(w_res, ((70, 44), (0, 0))), w_mid, w_mid_t,
        jnp.pad(w_out, ((0, 0), (84, 30))), jnp.pad(w_out.T, ((84, 30), (0, 0))), w_time,
    )


def body(
    trunk_in, norm_gain, w_gate, w_up, w_down, w_cond, w_time, w_in, w_mid, w_res, w_out,
    tsteps, advantage, actions, noise,
):
    seg, core = lax.axis_index("segment"), lax.axis_index("mp")
    cond_all, w_cond_full = trunk(trunk_in, norm_gain, w_gate[0], w_up[0], w_down[0].T, w_cond)
    cond = lax.dynamic_index_in_dim(cond_all, seg, 0, keepdims=False)[0:2]
    cond_act = mish_value(cond).astype(jnp.bfloat16)
    film_cond = jnp.dot(cond_act, w_cond_full, preferred_element_type=jnp.float32)
    begin = 4 * seg + 2 * core

    def own(values):
        return lax.dynamic_slice_in_dim(values, begin, 2, 0)

    packed, d_film_cond = denoise(
        film_cond, own(tsteps), own(advantage), own(actions), own(noise), w_time, w_in, w_mid, w_res, w_out
    )
    total, grad_w_cond, grad_cond = collect(cond_all, d_film_cond, packed, w_cond)
    joined = total[640:704]
    return (
        joined[:, 0:70].T,
        total[0:640].reshape(10, 64, 128).transpose(0, 2, 1).reshape(1280, 64),
        joined[:, 70:84].T,
        joined[:, 84:98],
        total[704:960],
        grad_w_cond,
        grad_cond,
        joined[0, 98:99] / 2048.0,
    )


def solution(mesh):
    in_specs = (
        P("dp", "mp"),
        P("segment", None),
        P("segment", "dp", "mp"),
        P("segment", "dp", "mp"),
        P("segment", "mp", "dp"),
        P("mp", None),
        P(),
        P(),
        P(),
        P(),
        P(),
        P("dp", None),
        P("dp", None),
        P("dp", None, None),
        P("dp", None, None, None),
    )
    out_specs = (
        P(None, "segment"),
        P(None, "segment"),
        P(None, "segment"),
        P("segment", None),
        P(None, "segment"),
        P("mp", "segment"),
        P(("dp", "segment"), "mp"),
        P(),
    )
    return jax.shard_map(body, mesh=mesh, in_specs=in_specs, out_specs=out_specs, check_vma=False)
```

```python
import functools
import math

import jax
import jax.numpy as jnp
import numpy as np
from jax import lax
from jax.experimental import pallas as pl
from jax.experimental.pallas import tpu as pltpu
from jax.sharding import PartitionSpec as P

MESH = pl.DeviceIdType.MESH
TSTEPS = 100
SIDE = 4
MICRO = 4
ROWS = 32
BATCHES = 2
OWN = 64
PART = 512
PARTS = 5
D = 2560
HALF = 1280
FH = 1792
SHARD = 160
CUT = 80
TILE = 256


def schedule():
    grid = np.arange(TSTEPS + 1, dtype=np.float64) / TSTEPS
    curve = np.cos((grid + 0.008) / 1.008 * math.pi / 2.0) ** 2
    betas = np.minimum(1.0 - curve[1:] / curve[:-1], 0.999)
    return np.cumprod(1.0 - betas)


def trunk_kernel(
    x_ref, gain_ref, wg_ref, wu_ref, wd_ref, wc_ref,
    cond_ref, wcond_ref,
    weights, first, arrived, leaving, normed, hidden, partial, share, other,
    own_sem, gs_sem, gr_sem, ms_sem, mr_sem, ps_sem, pr_sem, zs_sem, zr_sem, cs_sem, cr_sem,
):
    dp, seg, core = lax.axis_index("dp"), lax.axis_index("segment"), lax.axis_index("mp")
    y, x = dp // SIDE, dp % SIDE
    sibling = 1 - core

    def at(axis, delta):
        if axis == "x":
            return y * SIDE + (x + delta + SIDE) % SIDE
        return ((y + delta + SIDE) % SIDE) * SIDE + x

    barrier = pltpu.get_barrier_semaphore()
    for axis in ("x", "y"):
        for delta in (1, -1):
            pl.semaphore_signal(barrier, inc=1, device_id={"dp": at(axis, delta)}, device_id_type=MESH)
    pl.semaphore_signal(barrier, inc=1, device_id={"mp": sibling}, device_id_type=MESH)
    for step in range(1, 4):
        pl.semaphore_signal(barrier, inc=1, device_id={"segment": (seg + step) % 4}, device_id_type=MESH)
    pl.semaphore_wait(barrier, 8)

    sources = (wg_ref, wu_ref, wd_ref)
    chunks = [(which, part) for which in range(3) for part in range(2)]

    def spot(which, part, px, py, begin=0, size=CUT):
        row = (py * SIDE + px) * SHARD + part * CUT + begin
        return weights.at[which, pl.ds(pl.multiple_of(row, 16), size), :]

    def place(chunk, p_off, q_off, begin=0, size=CUT):
        which, part = chunk
        dx, dy = (p_off, q_off) if part == 0 else (q_off, p_off)
        return spot(which, part, (x + dx + SIDE) % SIDE, (y + dy + SIDE) % SIDE, begin, size)

    def axes(chunk):
        return ("x", "y") if chunk[1] == 0 else ("y", "x")

    def piece(chunk, kind):
        return (0, 48) if kind == 0 else (48, 32)

    def make(chunk, number, src, dst, axis, delta):
        q = chunks.index(chunk)
        return pltpu.make_async_remote_copy(
            src_ref=src, dst_ref=dst, send_sem=gs_sem.at[q, number], recv_sem=gr_sem.at[q, number],
            device_id={"dp": at(axis, delta)}, device_id_type=MESH,
        )

    OFF = (0, -1, 1, 2)

    def spec(chunk, number):
        p_axis, q_axis = axes(chunk)
        if number < 4:
            delta = 1 if number % 2 == 0 else -1
            if number < 2:
                return p_axis, delta, 0, 0, 0, CUT
            begin, size = piece(chunk, number - 2)
            return p_axis, delta, -delta, 0, begin, size
        slot, kind = divmod(number - 4, 4)
        delta = 1 if kind % 2 == 0 else -1
        if kind < 2:
            return q_axis, delta, OFF[slot], 0, 0, CUT
        begin, size = piece(chunk, kind - 2)
        return q_axis, delta, OFF[slot], -delta, begin, size

    def source_of(chunk, number):
        _, _, p_off, q_off, begin, size = spec(chunk, number)
        if p_off == 0 and q_off == 0:
            return sources[chunk[0]].at[pl.ds(chunk[1] * CUT + begin, size), :]
        return place(chunk, p_off, q_off, begin, size)

    def send(chunk, number):
        axis, delta, p_off, q_off, begin, size = spec(chunk, number)
        make(chunk, number, source_of(chunk, number), place(chunk, p_off, q_off, begin, size), axis, delta).start()

    def receive(chunk, number):
        axis, delta, p_off, q_off, begin, size = spec(chunk, number)
        if number < 4:
            p_off = p_off - delta
        else:
            q_off = q_off - delta
        spot_here = place(chunk, p_off, q_off, begin, size)
        make(chunk, number, spot_here, spot_here, axis, delta).wait_recv()

    def sent(chunk, number):
        axis, delta, p_off, q_off, begin, size = spec(chunk, number)
        make(chunk, number, source_of(chunk, number), place(chunk, p_off, q_off, begin, size), axis, delta).wait_send()

    own = []
    for chunk in chunks:
        for number in (0, 1, 4, 5):
            send(chunk, number)
    for which in range(3):
        keep = pltpu.make_async_copy(
            sources[which], weights.at[which, pl.ds(pl.multiple_of(dp * SHARD, 16), SHARD), :], own_sem.at[which]
        )
        keep.start()
        own.append(keep)

    def sibling_copy(number, src, dst):
        return pltpu.make_async_remote_copy(
            src_ref=src, dst_ref=dst, send_sem=ms_sem.at[number], recv_sem=mr_sem.at[number],
            device_id={"mp": sibling}, device_id_type=MESH,
        )

    here = pl.ds(pl.multiple_of(core * HALF, 128), HALF)
    there = pl.ds(pl.multiple_of(sibling * HALF, 128), HALF)
    def slot_of(j, features):
        return first.at[j // 2, pl.ds(32 * (j % 2), ROWS), features]

    for j in range(MICRO):
        src = x_ref.at[pl.ds(pl.multiple_of(64 * j + 32 * sibling, 16), ROWS), :]
        sibling_copy(j, src, slot_of(j, here)).start()
        kept = pltpu.make_async_copy(
            x_ref.at[pl.ds(pl.multiple_of(64 * j + 32 * core, 16), ROWS), :], slot_of(j, here), own_sem.at[3 + j]
        )
        kept.start()
        own.append(kept)
    here_rows = wcond_ref.at[pl.ds(pl.multiple_of(core * HALF, 16), HALF), :]
    there_rows = wcond_ref.at[pl.ds(pl.multiple_of(sibling * HALF, 16), HALF), :]
    sibling_copy(4, wc_ref, here_rows).start()
    kept = pltpu.make_async_copy(wc_ref, here_rows, own_sem.at[7])
    kept.start()
    own.append(kept)
    cond_ref[...] = jnp.zeros_like(cond_ref)

    for chunk in chunks:
        for number in (0, 1):
            receive(chunk, number)
            send(chunk, 2 + number)
            slot = 1 + number
            send(chunk, 4 + 4 * slot)
            send(chunk, 5 + 4 * slot)
        for kind in (0, 1):
            receive(chunk, 4 + kind)
            send(chunk, 6 + kind)
    for chunk in chunks:
        for number in (2, 3):
            receive(chunk, number)
        send(chunk, 16)
        send(chunk, 17)
        for slot in (1, 2):
            for kind in (0, 1):
                receive(chunk, 4 + 4 * slot + kind)
                send(chunk, 6 + 4 * slot + kind)
    for chunk in chunks:
        for kind in (0, 1):
            receive(chunk, 16 + kind)
            send(chunk, 18 + kind)
    for j in range(MICRO):
        sibling_copy(j, slot_of(j, there), slot_of(j, there)).wait_recv()
    for keep in own[3:7]:
        keep.wait()

    def finish_gather():
        for chunk in chunks:
            for slot in range(4):
                for kind in (2, 3):
                    receive(chunk, 4 + 4 * slot + kind)
        for keep in own[:3] + own[7:]:
            keep.wait()

    def z_copy(b, g):
        return pltpu.make_async_remote_copy(
            src_ref=leaving.at[b, g], dst_ref=arrived.at[b, g], send_sem=zs_sem.at[b, g], recv_sem=zr_sem.at[b, g],
            device_id={"segment": (seg + 1) % 4}, device_id_type=MESH,
        )

    def share_copy(b, g):
        return pltpu.make_async_remote_copy(
            src_ref=share.at[b, g], dst_ref=other.at[b, g], send_sem=ps_sem.at[b, g], recv_sem=pr_sem.at[b, g],
            device_id={"mp": sibling}, device_id_type=MESH,
        )

    def normed_copy(b):
        return sibling_copy(5 + b, normed.at[b, pl.ds(0, OWN)], normed.at[b, pl.ds(OWN, OWN)])

    def cond_copy(j, target):
        return pltpu.make_async_remote_copy(
            src_ref=cond_ref.at[j], dst_ref=cond_ref.at[j], send_sem=cs_sem.at[j, target], recv_sem=cr_sem.at[j],
            device_id={"segment": target}, device_id_type=MESH,
        )

    def columns_of(g):
        return slice(PART * g, PART * (g + 1))

    def normalize(b):
        states = [arrived[b, g].astype(jnp.float32) for g in range(PARTS)]
        total = sum(jnp.sum(state * state, axis=1, keepdims=True) for state in states)
        factor = lax.rsqrt(total * (1.0 / D) + 1e-05)
        for g in range(PARTS):
            gain = gain_ref[:, columns_of(g)].astype(jnp.float32)
            normed[b, 0:OWN, columns_of(g)] = (states[g] * factor * gain).astype(jnp.bfloat16)
        normed_copy(b).start()

    def batch(b, carry):
        @pl.when(seg > 0)
        def _():
            for g in range(PARTS):
                z_copy(b, g).wait_recv()
            normalize(b)

        normed_copy(b).wait_recv()
        for n in range(FH // TILE):
            cols = slice(n * TILE, (n + 1) * TILE)
            rows = normed[b]
            gate = jnp.dot(rows, weights[0, :, cols], preferred_element_type=jnp.float32)
            lift = jnp.dot(rows, weights[1, :, cols], preferred_element_type=jnp.float32)
            hidden[:, cols] = (gate / (1.0 + jnp.exp(-gate)) * lift).astype(jnp.bfloat16)

        def finish(g):
            share_copy(b, g).wait_recv()
            whole = partial[g] + other[b, g].astype(jnp.float32)
            leaving[b, g] = (arrived[b, g].astype(jnp.float32) + whole).astype(jnp.bfloat16)

            @pl.when(seg < 3)
            def _():
                z_copy(b, g).start()

        for g in range(PARTS):
            for half in range(2):
                part = slice(TILE * half, TILE * (half + 1))
                out = lax.dot_general(
                    hidden[...], weights[2, PART * g + TILE * half : PART * g + TILE * (half + 1), :],
                    (((1,), (1,)), ((), ())), preferred_element_type=jnp.float32,
                )
                partial[g, :, part] = out[0:OWN]
                share[b, g, :, part] = out[OWN:].astype(jnp.bfloat16)
            share_copy(b, g).start()
            if g > 0:
                finish(g - 1)
        finish(PARTS - 1)

        @pl.when(seg == 3)
        def _():
            for half in range(2):
                for g in range(PARTS):
                    rows = leaving[b, g, ROWS * half : ROWS * (half + 1)].astype(jnp.float32)
                    mean = jnp.mean(rows.reshape(2, 16, PART), axis=1)
                    cond_ref[2 * b + half, 0:2, columns_of(g)] = mean.astype(jnp.bfloat16).astype(jnp.float32)
                for target in range(3):
                    cond_copy(2 * b + half, target).start()

        return carry

    @pl.when(seg == 0)
    def _():
        for b in range(BATCHES):
            for g in range(PARTS):
                arrived[b, g] = first[b, :, columns_of(g)]
            normalize(b)

    finish_gather()
    lax.fori_loop(0, BATCHES, batch, 0)

    for chunk in chunks:
        for number in range(20):
            sent(chunk, number)
    for b in range(BATCHES):
        normed_copy(b).wait_send()
        for g in range(PARTS):
            share_copy(b, g).wait_send()

    @pl.when(seg < 3)
    def _():
        for b in range(BATCHES):
            for g in range(PARTS):
                z_copy(b, g).wait_send()

    for j in range(MICRO):
        sibling_copy(j, x_ref.at[pl.ds(0, ROWS), :], slot_of(j, there)).wait_send()

        @pl.when(seg < 3)
        def _(j=j):
            cond_copy(j, 0).wait_recv()

        @pl.when(seg == 3)
        def _(j=j):
            for target in range(3):
                cond_copy(j, target).wait_send()

    last = sibling_copy(4, wc_ref, there_rows)
    last.wait_recv()
    last.wait_send()


def trunk(trunk_in, norm_gain, w_gate, w_up, w_down_t, w_cond):
    anywhere = pl.BlockSpec(memory_space=pl.ANY)
    vmem = pl.BlockSpec(memory_space=pltpu.VMEM)
    dma = pltpu.SemaphoreType.DMA
    bf16 = jnp.bfloat16
    return pl.pallas_call(
        trunk_kernel,
        out_shape=(
            jax.ShapeDtypeStruct((MICRO, 8, D), jnp.float32),
            jax.ShapeDtypeStruct((D, w_cond.shape[1]), bf16),
        ),
        in_specs=[anywhere, vmem, anywhere, anywhere, anywhere, anywhere],
        out_specs=(vmem, anywhere),
        scratch_shapes=[
            pltpu.VMEM((3, D, FH), bf16),
            pltpu.VMEM((BATCHES, OWN, D), bf16),
            pltpu.VMEM((BATCHES, PARTS, OWN, PART), bf16),
            pltpu.VMEM((BATCHES, PARTS, OWN, PART), bf16),
            pltpu.VMEM((BATCHES, 2 * OWN, D), bf16),
            pltpu.VMEM((2 * OWN, FH), bf16),
            pltpu.VMEM((PARTS, OWN, PART), jnp.float32),
            pltpu.VMEM((BATCHES, PARTS, OWN, PART), bf16),
            pltpu.VMEM((BATCHES, PARTS, OWN, PART), bf16),
            dma((8,)),
            dma((6, 20)),
            dma((6, 20)),
            dma((7,)),
            dma((7,)),
            dma((BATCHES, PARTS)),
            dma((BATCHES, PARTS)),
            dma((BATCHES, PARTS)),
            dma((BATCHES, PARTS)),
            dma((MICRO, 3)),
            dma((MICRO,)),
        ],
        compiler_params=pltpu.CompilerParams(
            collective_id=0, has_side_effects=True, vmem_limit_bytes=52 * 2**20
        ),
    )(trunk_in, norm_gain, w_gate, w_up, w_down_t, w_cond)


def mish_parts(values):
    small = jnp.exp(-jnp.abs(values))
    right = values > 0
    top = jnp.where(right, 1.0 + 2.0 * small, small * (small + 2.0))
    rest = jnp.where(right, 2.0 * small * small, 2.0)
    return small, right, top, rest


def mish_value(values):
    _, _, top, rest = mish_parts(values)
    return values * (top / (top + rest))


def mish_slope(values):
    small, right, top, rest = mish_parts(values)
    inverse = 1.0 / (top + rest)
    logistic = jnp.where(right, 1.0, small) / (1.0 + small)
    return top * inverse + values * logistic * (rest * (2.0 * top + rest)) * (inverse * inverse)


def collect_kernel(
    cond_ref, film_ref, grads_ref, wc_ref,
    total_ref, gwc_ref, gcond_ref,
    cond_sib, act_all, film_sib, film_out, film_z, film_all,
    mp_in, z_out, z_in, x_out, x_in, y_out, y_in, full,
    ms_sem, mr_sem, zs_sem, zr_sem, xs_sem, xr_sem, ys_sem, yr_sem,
):
    dp, seg, core = lax.axis_index("dp"), lax.axis_index("segment"), lax.axis_index("mp")
    y, x = dp // SIDE, dp % SIDE
    sibling = 1 - core

    def x_peer(step):
        return {"dp": y * SIDE + (x + step) % SIDE}

    def y_peer(step):
        return {"dp": ((y + step) % SIDE) * SIDE + x}

    def z_peer(step):
        return {"segment": (seg + step) % SIDE}

    barrier = pltpu.get_barrier_semaphore()
    pl.semaphore_signal(barrier, inc=1, device_id={"mp": sibling}, device_id_type=MESH)
    for step in range(1, SIDE):
        for peer in (x_peer, y_peer, z_peer):
            pl.semaphore_signal(barrier, inc=1, device_id=peer(step), device_id_type=MESH)
    pl.semaphore_wait(barrier, 10)

    def copy(src, dst, out_sem, in_sem, peer):
        return pltpu.make_async_remote_copy(
            src_ref=src, dst_ref=dst, send_sem=out_sem, recv_sem=in_sem, device_id=peer, device_id_type=MESH
        )

    started = []

    def launch(src, dst, out_sem, in_sem, peer):
        one = copy(src, dst, out_sem, in_sem, peer)
        one.start()
        started.append(one)

    def arrive(dst, in_sem):
        copy(dst, dst, ms_sem.at[0], in_sem, {"mp": sibling}).wait_recv()

    def to_sibling(number, src, dst):
        launch(src, dst, ms_sem.at[number], mr_sem.at[number], {"mp": sibling})

    def scatter(out_sem, in_sem, number, src, dst, me, peer):
        for step in range(1, SIDE):
            launch(
                src.at[(me + step) % SIDE], dst.at[me], out_sem.at[number, step - 1], in_sem.at[number, step - 1], peer(step)
            )

    def spread(out_sem, in_sem, number, slots, me, peer):
        for step in range(1, SIDE):
            launch(slots.at[me], slots.at[me], out_sem.at[number, step - 1], in_sem.at[number, step - 1], peer(step))

    def gathered(in_sem, number, slots, me):
        for step in range(1, SIDE):
            arrive(slots.at[(me - step + SIDE) % SIDE], in_sem.at[number, step - 1])

    def added(slots):
        pieces = [slots[k].astype(jnp.float32) for k in range(SIDE)]
        return (pieces[0] + pieces[1]) + (pieces[2] + pieces[3])

    here = pl.ds(pl.multiple_of(core * HALF, 128), HALF)
    there = pl.ds(pl.multiple_of(sibling * HALF, 128), HALF)
    mine = pl.ds(pl.multiple_of(core * 512, 128), 512)
    others = pl.ds(pl.multiple_of(sibling * 512, 128), 512)

    to_sibling(0, film_ref, film_sib)
    to_sibling(1, grads_ref.at[:, others, :], mp_in)
    to_sibling(2, cond_ref.at[:, :, there], cond_sib)

    arrive(film_sib, mr_sem.at[0])
    film_out[...] = jnp.zeros_like(film_out)
    for s in range(SIDE):
        film_out[s, 0:2] = film_ref[0:2, 128 * s : 128 * (s + 1)]
        film_out[s, 2:4] = film_sib[0:2, 128 * s : 128 * (s + 1)]
    scatter(zs_sem, zr_sem, 0, film_out, film_z, seg, z_peer)
    film_z[seg] = film_out[seg]

    arrive(mp_in, mr_sem.at[1])
    z_out[...] = (grads_ref[:, mine, :].astype(jnp.float32) + mp_in[...].astype(jnp.float32)).astype(jnp.bfloat16)
    scatter(zs_sem, zr_sem, 1, z_out, z_in, seg, z_peer)
    z_in[seg] = z_out[seg]

    arrive(cond_sib, mr_sem.at[2])
    rows = [cond_ref[j, 0:2, here] for j in range(MICRO)] + [cond_sib[j, 0:2] for j in range(MICRO)]
    act_all[y, x] = mish_value(jnp.concatenate(rows, axis=0)).astype(jnp.bfloat16)
    spread(xs_sem, xr_sem, 0, act_all.at[y], x, x_peer)

    gathered(zr_sem, 0, film_z, seg)
    rows = [film_z[j, 0:2] for j in range(MICRO)] + [film_z[j, 2:4] for j in range(MICRO)]
    film_all[y, x] = jnp.concatenate(rows, axis=0).astype(jnp.bfloat16)
    spread(xs_sem, xr_sem, 1, film_all.at[y], x, x_peer)

    low = jnp.where(core == 0, film_ref[0:2], film_sib[0:2])
    high = jnp.where(core == 0, film_sib[0:2], film_ref[0:2])
    film_rows = jnp.concatenate([low, high, jnp.zeros((12, 512), jnp.float32)], axis=0).astype(jnp.bfloat16)
    own_cond, sib_cond = cond_ref[seg, 0:2, here], cond_sib[seg, 0:2]
    cond_rows = jnp.concatenate(
        [jnp.where(core == 0, own_cond, sib_cond), jnp.where(core == 0, sib_cond, own_cond)], axis=0
    )
    back = lax.dot_general(film_rows, wc_ref[...], (((1,), (1,)), ((), ())), preferred_element_type=jnp.float32)
    gcond_ref[...] = back[0:4] * mish_slope(cond_rows)

    gathered(zr_sem, 1, z_in, seg)
    x_out[...] = added(z_in).astype(jnp.bfloat16).reshape(x_out.shape)
    scatter(xs_sem, xr_sem, 2, x_out, x_in, x, x_peer)
    x_in[x] = x_out[x]

    gathered(xr_sem, 0, act_all.at[y], x)
    spread(ys_sem, yr_sem, 0, act_all, y, y_peer)
    gathered(xr_sem, 1, film_all.at[y], x)
    spread(ys_sem, yr_sem, 1, film_all, y, y_peer)

    gathered(xr_sem, 2, x_in, x)
    y_out[...] = added(x_in).astype(jnp.bfloat16).reshape(y_out.shape)
    scatter(ys_sem, yr_sem, 2, y_out, y_in, y, y_peer)
    y_in[y] = y_out[y]
    gathered(yr_sem, 2, y_in, y)
    full[core, x, y] = added(y_in).astype(jnp.bfloat16)
    spread(ys_sem, yr_sem, 3, full.at[core, x], y, y_peer)
    gathered(yr_sem, 3, full.at[core, x], y)
    spread(xs_sem, xr_sem, 3, full.at[core], x, x_peer)

    gathered(yr_sem, 0, act_all, y)
    gathered(yr_sem, 1, film_all, y)

    gathered(xr_sem, 3, full.at[core], x)
    to_sibling(3, full.at[core], full.at[core])
    gwc_ref[...] = lax.dot_general(
        act_all[...].reshape(256, HALF), film_all[...].reshape(256, 128), (((0,), (0,)), ((), ())),
        preferred_element_type=jnp.float32,
    )
    arrive(full.at[sibling], mr_sem.at[3])
    total_ref[...] = full[...].astype(jnp.float32).reshape(total_ref.shape)
    for one in started:
        one.wait_send()


def collect(cond, film, grads, w_cond):
    vmem = pl.BlockSpec(memory_space=pltpu.VMEM)
    dma = pltpu.SemaphoreType.DMA
    bf16, f32 = jnp.bfloat16, jnp.float32
    return pl.pallas_call(
        collect_kernel,
        out_shape=(
            jax.ShapeDtypeStruct((1024, 128), f32),
            jax.ShapeDtypeStruct((HALF, 128), f32),
            jax.ShapeDtypeStruct((4, HALF), f32),
        ),
        in_specs=[vmem] * 4,
        out_specs=(vmem, vmem, vmem),
        scratch_shapes=[
            pltpu.VMEM((MICRO, 8, HALF), f32),
            pltpu.VMEM((SIDE, SIDE, 16, HALF), bf16),
            pltpu.VMEM((8, 512), f32),
            pltpu.VMEM((SIDE, 8, 128), f32),
            pltpu.VMEM((SIDE, 8, 128), f32),
            pltpu.VMEM((SIDE, SIDE, 16, 128), bf16),
            pltpu.VMEM((SIDE, 512, 128), bf16),
            pltpu.VMEM((SIDE, 512, 128), bf16),
            pltpu.VMEM((SIDE, 512, 128), bf16),
            pltpu.VMEM((SIDE, 128, 128), bf16),
            pltpu.VMEM((SIDE, 128, 128), bf16),
            pltpu.VMEM((SIDE, 32, 128), bf16),
            pltpu.VMEM((SIDE, 32, 128), bf16),
            pltpu.VMEM((2, SIDE, SIDE, 32, 128), bf16),
            dma((4,)), dma((4,)),
            dma((2, 3)), dma((2, 3)),
            dma((4, 3)), dma((4, 3)),
            dma((4, 3)), dma((4, 3)),
        ],
        compiler_params=pltpu.CompilerParams(
            collective_id=1, has_side_effects=True, vmem_limit_bytes=32 * 2**20
        ),
    )(cond, film, grads, w_cond)


FLATS = 16
STEPS = 64
C = 256
BLOCK = 256


def denoise_kernel(
    film_cond_ref, noise_ref, actions_ref, keep_ref, blend_ref, adv_ref, time_ref,
    win_ref, wres_ref, wmid_ref, wmid_t_ref, wout_ref, wout_t_ref, wtime_ref,
    packed_ref, film_ref,
    npad, cols, pad, mid, back, pre, res, unit1, act1, slope1, unit2, slope2, block, d_block, d_pred,
    d_second, d_first, film, d_film, sum1, sum2, inv1, inv2, mean1, mean2,
):
    bf16, f32 = jnp.bfloat16, jnp.float32

    def rows_of(f, size=STEPS):
        return pl.ds(pl.multiple_of(f * size, size), size)

    def one(f):
        return pl.ds(f, 1)

    def each(body, count=FLATS):
        def step(f, carry):
            body(f)
            return carry

        lax.fori_loop(0, count, step, 0)

    lanes = lax.broadcasted_iota(jnp.int32, (C, C), 1)
    row_ids = lax.broadcasted_iota(jnp.int32, (C, C), 0)
    same = jnp.where(lanes // 32 == row_ids // 32, 1.0 / 2048.0, 0.0).astype(f32)

    def group_mean(values):
        return jnp.dot(values, same, preferred_element_type=f32, precision=lax.Precision.HIGHEST)

    def dot(left, right):
        return jnp.dot(left, right, preferred_element_type=f32)

    npad[...] = jnp.zeros_like(npad)
    pad[...] = jnp.zeros_like(pad)

    def make_cols(f):
        sample = rows_of(f // 8)
        noisy = keep_ref[one(f)] * actions_ref[sample].astype(f32) + blend_ref[one(f)] * noise_ref[rows_of(f)].astype(f32)
        noisy = noisy.astype(bf16).astype(f32)
        npad[f, 8:72] = noisy
        total = pltpu.roll(noisy, 114, 1)
        for tap in range(5):
            total = total + pltpu.roll(npad[f, 6 + tap : 70 + tap], 44 + 14 * tap, 1)
        cols[rows_of(f)] = total.astype(bf16)

    each(make_cols)

    time_film = dot(time_ref[...], wtime_ref[...])
    top = jnp.broadcast_to(film_cond_ref[0:1], (8, 2 * C))
    low = jnp.broadcast_to(film_cond_ref[1:2], (8, 2 * C))
    film[...] = jnp.concatenate([top, low], axis=0) + time_film

    def first_conv(b):
        rows = rows_of(b, BLOCK)
        out = dot(cols[rows], win_ref[...])
        pre[rows] = out
        res[rows] = dot(cols[rows], wres_ref[...])

    each(first_conv, 4)

    def centre(inverse):
        def total(f):
            sum1[one(f)] = jnp.sum(pre[rows_of(f)], axis=0, keepdims=True)

        each(total)
        mean1[...] = group_mean(sum1[...])

        def moved(f):
            left = pre[rows_of(f)] - mean1[one(f)]
            pre[rows_of(f)] = left
            sum1[one(f)] = jnp.sum(left * left, axis=0, keepdims=True)

        each(moved)
        inverse[...] = lax.rsqrt(group_mean(sum1[...]) + 1e-05)

    def mish_both(values):
        small, right, above, rest = mish_parts(values)
        inverse = 1.0 / (above + rest)
        logistic = jnp.where(right, 1.0, small) / (1.0 + small)
        ratio = above * inverse
        value = values * ratio
        return value, ratio + values * logistic * (rest * (2.0 * above + rest)) * (inverse * inverse)

    centre(inv1)

    def first_act(f):
        unit = pre[rows_of(f)] * inv1[one(f)]
        value, slope = mish_both(unit)
        unit1[rows_of(f)] = unit
        act1[rows_of(f)] = value
        slope1[rows_of(f)] = slope
        changed = film[one(f), 0:C] * value + film[one(f), C:]
        pad[f, 8:72] = changed.astype(bf16).astype(f32)
        for tap in range(5):
            mid[rows_of(f), C * tap : C * (tap + 1)] = pad[f, 6 + tap : 70 + tap].astype(bf16)

    each(first_act)

    def second_conv(b):
        rows = rows_of(b, BLOCK)
        pre[rows] = dot(mid[rows], wmid_ref[...])

    each(second_conv, 4)
    centre(inv2)

    def second_act(f):
        unit = pre[rows_of(f)] * inv2[one(f)]
        value, slope = mish_both(unit)
        unit2[rows_of(f)] = unit
        slope2[rows_of(f)] = slope
        block[rows_of(f)] = (value + res[rows_of(f)]).astype(bf16)

    each(second_act)

    def errors(f, total):
        rows = rows_of(f)
        error = dot(block[rows], wout_ref[...]) - noise_ref[rows].astype(f32)
        d_pred[rows] = (adv_ref[one(f)] * error * (2.0 / 896.0)).astype(bf16)
        return total + error * error

    err = lax.fori_loop(0, FLATS, errors, jnp.zeros((STEPS, 128), f32))
    err_sum = jnp.sum(err) * (1.0 / 896.0)

    def from_pred(b):
        rows = rows_of(b, BLOCK)
        out = dot(d_pred[rows], wout_t_ref[...])
        pre[rows] = out
        d_block[rows] = out.astype(bf16)

    each(from_pred, 4)

    def act_back(scale, unit, slope):
        def totals(f):
            grad = scale(f) * slope[rows_of(f)]
            pre[rows_of(f)] = grad
            sum1[one(f)] = jnp.sum(grad, axis=0, keepdims=True)
            sum2[one(f)] = jnp.sum(grad * unit[rows_of(f)], axis=0, keepdims=True)

        each(totals)
        mean1[...] = group_mean(sum1[...])
        mean2[...] = group_mean(sum2[...])

    act_back(lambda f: pre[rows_of(f)], unit2, slope2)

    def second_back(f):
        grad = inv2[one(f)] * (pre[rows_of(f)] - mean1[one(f)] - unit2[rows_of(f)] * mean2[one(f)])
        rounded = grad.astype(bf16)
        d_second[rows_of(f)] = rounded
        pad[f, 8:72] = rounded.astype(f32)
        for tap in range(5):
            back[rows_of(f), C * tap : C * (tap + 1)] = pad[f, 10 - tap : 74 - tap].astype(bf16)

    each(second_back)

    def mid_back(b):
        rows = rows_of(b, BLOCK)
        pre[rows] = dot(back[rows], wmid_t_ref[...])

    each(mid_back, 4)

    def film_back(f):
        grad = pre[rows_of(f)]
        d_film[one(f), 0:C] = jnp.sum(grad * act1[rows_of(f)], axis=0, keepdims=True)
        d_film[one(f), C:] = jnp.sum(grad, axis=0, keepdims=True)

    each(film_back)
    film_ref[...] = jnp.zeros_like(film_ref)
    film_ref[0:1] = jnp.sum(d_film[0:8], axis=0, keepdims=True)
    film_ref[1:2] = jnp.sum(d_film[8:16], axis=0, keepdims=True)

    act_back(lambda f: pre[rows_of(f)] * film[one(f), 0:C], unit1, slope1)

    def first_back(f):
        grad = inv1[one(f)] * (pre[rows_of(f)] - mean1[one(f)] - unit1[rows_of(f)] * mean2[one(f)])
        d_first[rows_of(f)] = grad.astype(bf16)

    each(first_back)

    def over_rows(left, right):
        return lax.dot_general(left, right, (((0,), (0,)), ((), ())), preferred_element_type=f32)

    for tap in range(5):
        grad = over_rows(d_second[...], mid[:, C * tap : C * (tap + 1)]).astype(bf16)
        for s in range(4):
            for half in range(2):
                begin = 64 * (2 * tap + half)
                packed_ref[s, begin : begin + 64] = grad[64 * s : 64 * (s + 1), 128 * half : 128 * (half + 1)]
    lane = lax.broadcasted_iota(jnp.int32, (C, 128), 1)
    inner = over_rows(d_first[...], cols[...])
    skip = over_rows(d_block[...], cols[...])
    out = over_rows(block[...], d_pred[...])
    joined = jnp.where(lane < 70, inner, jnp.where(lane < 84, skip, jnp.where(lane < 98, out, err_sum))).astype(bf16)
    timed = over_rows(time_ref[...], d_film[...].astype(bf16)).astype(bf16)
    for s in range(4):
        packed_ref[s, 640:704] = joined[64 * s : 64 * (s + 1)]
        packed_ref[s, 704:960] = timed[:, 128 * s : 128 * (s + 1)]
        packed_ref[s, 960:1024] = jnp.zeros((64, 128), bf16)


def denoise(film_cond, tsteps, advantage, actions, noise, w_time, w_in, w_mid, w_res, w_out):
    bf16, f32 = jnp.bfloat16, jnp.float32
    flat = tsteps.reshape(FLATS, 1)
    table = schedule()
    picked = (flat == jnp.arange(TSTEPS, dtype=jnp.int32)[None]).astype(f32)
    keep = jnp.sum(picked * jnp.asarray(np.sqrt(table), f32)[None], axis=1, keepdims=True)
    blend = jnp.sum(picked * jnp.asarray(np.sqrt(1.0 - table), f32)[None], axis=1, keepdims=True)

    def wide(values):
        return jnp.broadcast_to(values, (FLATS, 128))

    half_dim = w_time.shape[0] // 2
    frequencies = jnp.exp(-math.log(10000.0) * jnp.arange(half_dim, dtype=f32) / (half_dim - 1))
    angles = flat.astype(f32) * frequencies[None]
    time_act = mish_value(jnp.concatenate([jnp.sin(angles), jnp.cos(angles)], axis=1)).astype(bf16)
    noise_lanes = jnp.pad(noise.reshape(FLATS * STEPS, 14), ((0, 0), (84, 30)))
    action_lanes = jnp.pad(actions.reshape(2 * STEPS, 14), ((0, 0), (84, 30)))
    w_mid_t = w_mid.reshape(5, C, C).transpose(0, 2, 1).reshape(5 * C, C)
    vmem = pl.BlockSpec(memory_space=pltpu.VMEM)
    flat_rows = FLATS * STEPS
    big, small = pltpu.VMEM((flat_rows, C), f32), pltpu.VMEM((FLATS, C), f32)
    big16 = pltpu.VMEM((flat_rows, C), bf16)
    return pl.pallas_call(
        denoise_kernel,
        out_shape=(jax.ShapeDtypeStruct((4, 1024, 128), bf16), jax.ShapeDtypeStruct((8, 2 * C), f32)),
        in_specs=[vmem] * 14,
        out_specs=(vmem, vmem),
        scratch_shapes=[
            pltpu.VMEM((FLATS, 80, 128), f32),
            pltpu.VMEM((flat_rows, 128), bf16),
            pltpu.VMEM((FLATS, 80, C), f32),
            pltpu.VMEM((flat_rows, 5 * C), bf16),
            pltpu.VMEM((flat_rows, 5 * C), bf16),
            big, big, big, big, big, big, big,
            big16, big16,
            pltpu.VMEM((flat_rows, 128), bf16),
            big16, big16,
            pltpu.VMEM((FLATS, 2 * C), f32),
            pltpu.VMEM((FLATS, 2 * C), f32),
            small, small, small, small, small, small,
        ],
        compiler_params=pltpu.CompilerParams(vmem_limit_bytes=48 * 2**20),
    )(
        film_cond, noise_lanes, action_lanes, wide(keep), wide(blend), wide(advantage.reshape(FLATS, 1)), time_act,
        jnp.pad(w_in, ((0, 58), (0, 0))), jnp.pad(w_res, ((70, 44), (0, 0))), w_mid, w_mid_t,
        jnp.pad(w_out, ((0, 0), (84, 30))), jnp.pad(w_out.T, ((84, 30), (0, 0))), w_time,
    )


def body(
    trunk_in, norm_gain, w_gate, w_up, w_down, w_cond, w_time, w_in, w_mid, w_res, w_out,
    tsteps, advantage, actions, noise,
):
    seg, core = lax.axis_index("segment"), lax.axis_index("mp")
    cond_all, w_cond_full = trunk(trunk_in, norm_gain, w_gate[0], w_up[0], w_down[0].T, w_cond)
    cond = lax.dynamic_index_in_dim(cond_all, seg, 0, keepdims=False)[0:2]
    cond_act = mish_value(cond).astype(jnp.bfloat16)
    film_cond = jnp.dot(cond_act, w_cond_full, preferred_element_type=jnp.float32)
    begin = 4 * seg + 2 * core

    def own(values):
        return lax.dynamic_slice_in_dim(values, begin, 2, 0)

    packed, d_film_cond = denoise(
        film_cond, own(tsteps), own(advantage), own(actions), own(noise), w_time, w_in, w_mid, w_res, w_out
    )
    total, grad_w_cond, grad_cond = collect(cond_all, d_film_cond, packed, w_cond)
    joined = total[640:704]
    return (
        joined[:, 0:70].T,
        total[0:640].reshape(10, 64, 128).transpose(0, 2, 1).reshape(1280, 64),
        joined[:, 70:84].T,
        joined[:, 84:98],
        total[704:960],
        grad_w_cond,
        grad_cond,
        joined[0, 98:99] / 2048.0,
    )


def solution(mesh):
    in_specs = (
        P("dp", "mp"),
        P("segment", None),
        P("segment", "dp", "mp"),
        P("segment", "dp", "mp"),
        P("segment", "mp", "dp"),
        P("mp", None),
        P(),
        P(),
        P(),
        P(),
        P(),
        P("dp", None),
        P("dp", None),
        P("dp", None, None),
        P("dp", None, None, None),
    )
    out_specs = (
        P(None, "segment"),
        P(None, "segment"),
        P(None, "segment"),
        P("segment", None),
        P(None, "segment"),
        P("mp", "segment"),
        P(("dp", "segment"), "mp"),
        P(),
    )
    return jax.shard_map(body, mesh=mesh, in_specs=in_specs, out_specs=out_specs, check_vma=False)
```

```python
import functools
import math

import jax
import jax.numpy as jnp
import numpy as np
from jax import lax
from jax.experimental import pallas as pl
from jax.experimental.pallas import tpu as pltpu
from jax.sharding import PartitionSpec as P

MESH = pl.DeviceIdType.MESH
TSTEPS = 100
SIDE = 4
MICRO = 4
ROWS = 32
BATCHES = 2
OWN = 64
PART = 512
PARTS = 5
D = 2560
HALF = 1280
FH = 1792
SHARD = 160
CUT = 80
TILE = 256


def schedule():
    grid = np.arange(TSTEPS + 1, dtype=np.float64) / TSTEPS
    curve = np.cos((grid + 0.008) / 1.008 * math.pi / 2.0) ** 2
    betas = np.minimum(1.0 - curve[1:] / curve[:-1], 0.999)
    return np.cumprod(1.0 - betas)


def trunk_kernel(
    x_ref, gain_ref, wg_ref, wu_ref, wd_ref, wc_ref,
    cond_ref, wcond_ref,
    weights, first, arrived, leaving, normed, hidden, partial, share, other,
    own_sem, gs_sem, gr_sem, ms_sem, mr_sem, ps_sem, pr_sem, zs_sem, zr_sem, cs_sem, cr_sem,
):
    dp, seg, core = lax.axis_index("dp"), lax.axis_index("segment"), lax.axis_index("mp")
    y, x = dp // SIDE, dp % SIDE
    sibling = 1 - core

    def at(axis, delta):
        if axis == "x":
            return y * SIDE + (x + delta + SIDE) % SIDE
        return ((y + delta + SIDE) % SIDE) * SIDE + x

    barrier = pltpu.get_barrier_semaphore()
    for axis in ("x", "y"):
        for delta in (1, -1):
            pl.semaphore_signal(barrier, inc=1, device_id={"dp": at(axis, delta)}, device_id_type=MESH)
    pl.semaphore_signal(barrier, inc=1, device_id={"mp": sibling}, device_id_type=MESH)
    for step in range(1, 4):
        pl.semaphore_signal(barrier, inc=1, device_id={"segment": (seg + step) % 4}, device_id_type=MESH)
    pl.semaphore_wait(barrier, 8)

    sources = (wg_ref, wu_ref, wd_ref)
    chunks = [(which, part) for which in range(3) for part in range(2)]

    def spot(which, part, px, py, begin=0, size=CUT):
        row = (py * SIDE + px) * SHARD + part * CUT + begin
        return weights.at[which, pl.ds(pl.multiple_of(row, 16), size), :]

    def place(chunk, p_off, q_off, begin=0, size=CUT):
        which, part = chunk
        dx, dy = (p_off, q_off) if part == 0 else (q_off, p_off)
        return spot(which, part, (x + dx + SIDE) % SIDE, (y + dy + SIDE) % SIDE, begin, size)

    def axes(chunk):
        return ("x", "y") if chunk[1] == 0 else ("y", "x")

    def piece(chunk, kind):
        return (0, 48) if kind == 0 else (48, 32)

    def make(chunk, number, src, dst, axis, delta):
        q = chunks.index(chunk)
        return pltpu.make_async_remote_copy(
            src_ref=src, dst_ref=dst, send_sem=gs_sem.at[q, number], recv_sem=gr_sem.at[q, number],
            device_id={"dp": at(axis, delta)}, device_id_type=MESH,
        )

    OFF = (0, -1, 1, 2)

    def spec(chunk, number):
        p_axis, q_axis = axes(chunk)
        if number < 4:
            delta = 1 if number % 2 == 0 else -1
            if number < 2:
                return p_axis, delta, 0, 0, 0, CUT
            begin, size = piece(chunk, number - 2)
            return p_axis, delta, -delta, 0, begin, size
        slot, kind = divmod(number - 4, 4)
        delta = 1 if kind % 2 == 0 else -1
        if kind < 2:
            return q_axis, delta, OFF[slot], 0, 0, CUT
        begin, size = piece(chunk, kind - 2)
        return q_axis, delta, OFF[slot], -delta, begin, size

    def source_of(chunk, number):
        _, _, p_off, q_off, begin, size = spec(chunk, number)
        if p_off == 0 and q_off == 0:
            return sources[chunk[0]].at[pl.ds(chunk[1] * CUT + begin, size), :]
        return place(chunk, p_off, q_off, begin, size)

    def send(chunk, number):
        axis, delta, p_off, q_off, begin, size = spec(chunk, number)
        make(chunk, number, source_of(chunk, number), place(chunk, p_off, q_off, begin, size), axis, delta).start()

    def receive(chunk, number):
        axis, delta, p_off, q_off, begin, size = spec(chunk, number)
        if number < 4:
            p_off = p_off - delta
        else:
            q_off = q_off - delta
        spot_here = place(chunk, p_off, q_off, begin, size)
        make(chunk, number, spot_here, spot_here, axis, delta).wait_recv()

    def sent(chunk, number):
        axis, delta, p_off, q_off, begin, size = spec(chunk, number)
        make(chunk, number, source_of(chunk, number), place(chunk, p_off, q_off, begin, size), axis, delta).wait_send()

    own = []
    for chunk in chunks:
        for number in (0, 1, 4, 5):
            send(chunk, number)
    for which in range(3):
        keep = pltpu.make_async_copy(
            sources[which], weights.at[which, pl.ds(pl.multiple_of(dp * SHARD, 16), SHARD), :], own_sem.at[which]
        )
        keep.start()
        own.append(keep)

    def sibling_copy(number, src, dst):
        return pltpu.make_async_remote_copy(
            src_ref=src, dst_ref=dst, send_sem=ms_sem.at[number], recv_sem=mr_sem.at[number],
            device_id={"mp": sibling}, device_id_type=MESH,
        )

    here = pl.ds(pl.multiple_of(core * HALF, 128), HALF)
    there = pl.ds(pl.multiple_of(sibling * HALF, 128), HALF)
    def slot_of(j, features):
        return first.at[j // 2, pl.ds(32 * (j % 2), ROWS), features]

    for j in range(MICRO):
        src = x_ref.at[pl.ds(pl.multiple_of(64 * j + 32 * sibling, 16), ROWS), :]
        sibling_copy(j, src, slot_of(j, here)).start()
        kept = pltpu.make_async_copy(
            x_ref.at[pl.ds(pl.multiple_of(64 * j + 32 * core, 16), ROWS), :], slot_of(j, here), own_sem.at[3 + j]
        )
        kept.start()
        own.append(kept)
    here_rows = wcond_ref.at[pl.ds(pl.multiple_of(core * HALF, 16), HALF), :]
    there_rows = wcond_ref.at[pl.ds(pl.multiple_of(sibling * HALF, 16), HALF), :]
    sibling_copy(4, wc_ref, here_rows).start()
    kept = pltpu.make_async_copy(wc_ref, here_rows, own_sem.at[7])
    kept.start()
    own.append(kept)
    cond_ref[...] = jnp.zeros_like(cond_ref)

    for chunk in chunks:
        for number in (0, 1):
            receive(chunk, number)
            send(chunk, 2 + number)
            slot = 1 + number
            send(chunk, 4 + 4 * slot)
            send(chunk, 5 + 4 * slot)
        for kind in (0, 1):
            receive(chunk, 4 + kind)
            send(chunk, 6 + kind)
    for chunk in chunks:
        for number in (2, 3):
            receive(chunk, number)
        send(chunk, 16)
        send(chunk, 17)
        for slot in (1, 2):
            for kind in (0, 1):
                receive(chunk, 4 + 4 * slot + kind)
                send(chunk, 6 + 4 * slot + kind)
    for chunk in chunks:
        for kind in (0, 1):
            receive(chunk, 16 + kind)
            send(chunk, 18 + kind)
    for j in range(MICRO):
        sibling_copy(j, slot_of(j, there), slot_of(j, there)).wait_recv()
    for keep in own[3:7]:
        keep.wait()

    def finish_gather():
        for chunk in chunks:
            for slot in range(4):
                for kind in (2, 3):
                    receive(chunk, 4 + 4 * slot + kind)
        for keep in own[:3] + own[7:]:
            keep.wait()

    def z_copy(b, g):
        return pltpu.make_async_remote_copy(
            src_ref=leaving.at[b, g], dst_ref=arrived.at[b, g], send_sem=zs_sem.at[b, g], recv_sem=zr_sem.at[b, g],
            device_id={"segment": (seg + 1) % 4}, device_id_type=MESH,
        )

    def share_copy(b, g):
        return pltpu.make_async_remote_copy(
            src_ref=share.at[b, g], dst_ref=other.at[b, g], send_sem=ps_sem.at[b, g], recv_sem=pr_sem.at[b, g],
            device_id={"mp": sibling}, device_id_type=MESH,
        )

    def normed_copy(b):
        return sibling_copy(5 + b, normed.at[b, pl.ds(0, OWN)], normed.at[b, pl.ds(OWN, OWN)])

    def cond_copy(j, target):
        return pltpu.make_async_remote_copy(
            src_ref=cond_ref.at[j], dst_ref=cond_ref.at[j], send_sem=cs_sem.at[j, target], recv_sem=cr_sem.at[j],
            device_id={"segment": target}, device_id_type=MESH,
        )

    def columns_of(g):
        return slice(PART * g, PART * (g + 1))

    def normalize(b):
        states = [arrived[b, g].astype(jnp.float32) for g in range(PARTS)]
        total = sum(jnp.sum(state * state, axis=1, keepdims=True) for state in states)
        factor = lax.rsqrt(total * (1.0 / D) + 1e-05)
        for g in range(PARTS):
            gain = gain_ref[:, columns_of(g)].astype(jnp.float32)
            normed[b, 0:OWN, columns_of(g)] = (states[g] * factor * gain).astype(jnp.bfloat16)
        normed_copy(b).start()

    def batch(b, carry):
        @pl.when(seg > 0)
        def _():
            for g in range(PARTS):
                z_copy(b, g).wait_recv()
            normalize(b)

        normed_copy(b).wait_recv()
        for n in range(FH // TILE):
            cols = slice(n * TILE, (n + 1) * TILE)
            rows = normed[b]
            gate = jnp.dot(rows, weights[0, :, cols], preferred_element_type=jnp.float32)
            lift = jnp.dot(rows, weights[1, :, cols], preferred_element_type=jnp.float32)
            hidden[:, cols] = (gate / (1.0 + jnp.exp(-gate)) * lift).astype(jnp.bfloat16)

        def finish(g):
            share_copy(b, g).wait_recv()
            whole = partial[g] + other[b, g].astype(jnp.float32)
            leaving[b, g] = (arrived[b, g].astype(jnp.float32) + whole).astype(jnp.bfloat16)

            @pl.when(seg < 3)
            def _():
                z_copy(b, g).start()

        for g in range(PARTS):
            for half in range(2):
                part = slice(TILE * half, TILE * (half + 1))
                out = lax.dot_general(
                    hidden[...], weights[2, PART * g + TILE * half : PART * g + TILE * (half + 1), :],
                    (((1,), (1,)), ((), ())), preferred_element_type=jnp.float32,
                )
                partial[g, :, part] = out[0:OWN]
                share[b, g, :, part] = out[OWN:].astype(jnp.bfloat16)
            share_copy(b, g).start()
            if g > 0:
                finish(g - 1)
        finish(PARTS - 1)

        @pl.when(seg == 3)
        def _():
            for half in range(2):
                for g in range(PARTS):
                    rows = leaving[b, g, ROWS * half : ROWS * (half + 1)].astype(jnp.float32)
                    mean = jnp.mean(rows.reshape(2, 16, PART), axis=1)
                    cond_ref[2 * b + half, 0:2, columns_of(g)] = mean.astype(jnp.bfloat16).astype(jnp.float32)
                for target in range(3):
                    cond_copy(2 * b + half, target).start()

        return carry

    @pl.when(seg == 0)
    def _():
        for b in range(BATCHES):
            for g in range(PARTS):
                arrived[b, g] = first[b, :, columns_of(g)]
            normalize(b)

    finish_gather()
    lax.fori_loop(0, BATCHES, batch, 0)

    for chunk in chunks:
        for number in range(20):
            sent(chunk, number)
    for b in range(BATCHES):
        normed_copy(b).wait_send()
        for g in range(PARTS):
            share_copy(b, g).wait_send()

    @pl.when(seg < 3)
    def _():
        for b in range(BATCHES):
            for g in range(PARTS):
                z_copy(b, g).wait_send()

    for j in range(MICRO):
        sibling_copy(j, x_ref.at[pl.ds(0, ROWS), :], slot_of(j, there)).wait_send()

        @pl.when(seg < 3)
        def _(j=j):
            cond_copy(j, 0).wait_recv()

        @pl.when(seg == 3)
        def _(j=j):
            for target in range(3):
                cond_copy(j, target).wait_send()

    last = sibling_copy(4, wc_ref, there_rows)
    last.wait_recv()
    last.wait_send()


def trunk(trunk_in, norm_gain, w_gate, w_up, w_down_t, w_cond):
    anywhere = pl.BlockSpec(memory_space=pl.ANY)
    vmem = pl.BlockSpec(memory_space=pltpu.VMEM)
    dma = pltpu.SemaphoreType.DMA
    bf16 = jnp.bfloat16
    return pl.pallas_call(
        trunk_kernel,
        out_shape=(
            jax.ShapeDtypeStruct((MICRO, 8, D), jnp.float32),
            jax.ShapeDtypeStruct((D, w_cond.shape[1]), bf16),
        ),
        in_specs=[anywhere, vmem, anywhere, anywhere, anywhere, anywhere],
        out_specs=(vmem, anywhere),
        scratch_shapes=[
            pltpu.VMEM((3, D, FH), bf16),
            pltpu.VMEM((BATCHES, OWN, D), bf16),
            pltpu.VMEM((BATCHES, PARTS, OWN, PART), bf16),
            pltpu.VMEM((BATCHES, PARTS, OWN, PART), bf16),
            pltpu.VMEM((BATCHES, 2 * OWN, D), bf16),
            pltpu.VMEM((2 * OWN, FH), bf16),
            pltpu.VMEM((PARTS, OWN, PART), jnp.float32),
            pltpu.VMEM((BATCHES, PARTS, OWN, PART), bf16),
            pltpu.VMEM((BATCHES, PARTS, OWN, PART), bf16),
            dma((8,)),
            dma((6, 20)),
            dma((6, 20)),
            dma((7,)),
            dma((7,)),
            dma((BATCHES, PARTS)),
            dma((BATCHES, PARTS)),
            dma((BATCHES, PARTS)),
            dma((BATCHES, PARTS)),
            dma((MICRO, 3)),
            dma((MICRO,)),
        ],
        compiler_params=pltpu.CompilerParams(
            collective_id=0, has_side_effects=True, vmem_limit_bytes=52 * 2**20
        ),
    )(trunk_in, norm_gain, w_gate, w_up, w_down_t, w_cond)


def mish_parts(values):
    small = jnp.exp(-jnp.abs(values))
    right = values > 0
    top = jnp.where(right, 1.0 + 2.0 * small, small * (small + 2.0))
    rest = jnp.where(right, 2.0 * small * small, 2.0)
    return small, right, top, rest


def mish_value(values):
    _, _, top, rest = mish_parts(values)
    return values * (top / (top + rest))


def mish_slope(values):
    small, right, top, rest = mish_parts(values)
    inverse = 1.0 / (top + rest)
    logistic = jnp.where(right, 1.0, small) / (1.0 + small)
    return top * inverse + values * logistic * (rest * (2.0 * top + rest)) * (inverse * inverse)


FLATS = 16
STEPS = 64
C = 256
BLOCK = 256
ROWS_A = 320
ROWS_B = 192


def finish_kernel(
    cond_ref, wcond_ref, wc_ref, noise_in, actions_in, tsteps_ref, advantage_ref, roots_ref, table_ref,
    win_in, wres_in, wmid_ref, wout_in, wtime_ref,
    full_a, full_b, act_all, film_all, gcond_ref,
    noise_ref, actions_ref, keep_ref, blend_ref, adv_ref, time_ref, wide_in, wide_res, wide_out, win_ref, wres_ref,
    wout_ref, wout_t_ref, npad, cols, pad, mid, back, pre, res, unit1, act1, slope1, unit2, slope2, block, d_block, d_pred,
    d_second, d_first, film, d_film, sum1, sum2, inv1, inv2, mean1, mean2,
    cond_sib, film_ref, film_sib, film_out, film_z,
    grads_a, grads_b, mp_a, mp_b, zo_a, zo_b, zi_a, zi_b, xo_a, xo_b, xi_a, xi_b, yi_a, yi_b,
    ms_sem, mr_sem, zs_sem, zr_sem, xs_sem, xr_sem, ys_sem, yr_sem,
):
    dp, seg, core = lax.axis_index("dp"), lax.axis_index("segment"), lax.axis_index("mp")
    y, x = dp // SIDE, dp % SIDE
    sibling = 1 - core

    def x_peer(step):
        return {"dp": y * SIDE + (x + step) % SIDE}

    def y_peer(step):
        return {"dp": ((y + step) % SIDE) * SIDE + x}

    def z_peer(step):
        return {"segment": (seg + step) % SIDE}

    barrier = pltpu.get_barrier_semaphore()
    pl.semaphore_signal(barrier, inc=1, device_id={"mp": sibling}, device_id_type=MESH)
    for step in range(1, SIDE):
        for peer in (x_peer, y_peer, z_peer):
            pl.semaphore_signal(barrier, inc=1, device_id=peer(step), device_id_type=MESH)

    def copy(src, dst, out_sem, in_sem, peer):
        return pltpu.make_async_remote_copy(
            src_ref=src, dst_ref=dst, send_sem=out_sem, recv_sem=in_sem, device_id=peer, device_id_type=MESH
        )

    started = []

    def launch(src, dst, out_sem, in_sem, peer):
        one = copy(src, dst, out_sem, in_sem, peer)
        one.start()
        started.append(one)

    def arrive(dst, in_sem):
        copy(dst, dst, ms_sem.at[0], in_sem, {"mp": sibling}).wait_recv()

    def to_sibling(number, src, dst):
        launch(src, dst, ms_sem.at[number], mr_sem.at[number], {"mp": sibling})

    def scatter(out_sem, in_sem, number, src, dst, me, peer):
        for step in range(1, SIDE):
            launch(
                src.at[(me + step) % SIDE], dst.at[me], out_sem.at[number, step - 1], in_sem.at[number, step - 1], peer(step)
            )

    def spread(out_sem, in_sem, number, slots, me, peer):
        for step in range(1, SIDE):
            launch(slots.at[me], slots.at[me], out_sem.at[number, step - 1], in_sem.at[number, step - 1], peer(step))

    def gathered(in_sem, number, slots, me):
        for step in range(1, SIDE):
            arrive(slots.at[(me - step + SIDE) % SIDE], in_sem.at[number, step - 1])

    def added(slots):
        pieces = [slots[k].astype(jnp.float32) for k in range(SIDE)]
        return (pieces[0] + pieces[1]) + (pieces[2] + pieces[3])

    here = pl.ds(pl.multiple_of(core * HALF, 128), HALF)
    there = pl.ds(pl.multiple_of(sibling * HALF, 128), HALF)
    bf16, f32 = jnp.bfloat16, jnp.float32

    def rows_of(f, size=STEPS):
        return pl.ds(pl.multiple_of(f * size, size), size)

    def one(f):
        return pl.ds(f, 1)

    def each(body, count=FLATS):
        def step(f, carry):
            body(f)
            return carry

        lax.fori_loop(0, count, step, 0)

    lanes = lax.broadcasted_iota(jnp.int32, (C, C), 1)
    row_ids = lax.broadcasted_iota(jnp.int32, (C, C), 0)
    same = jnp.where(lanes // 32 == row_ids // 32, 1.0 / 2048.0, 0.0).astype(f32)

    def group_mean(values):
        return jnp.dot(values, same, preferred_element_type=f32, precision=lax.Precision.HIGHEST)

    def dot(left, right):
        return jnp.dot(left, right, preferred_element_type=f32)

    begin = 4 * seg + 2 * core
    sample_at = lax.broadcasted_iota(jnp.int32, (8, 16), 1)

    def column(ref):
        pieces = []
        for sample in range(2):
            chosen = jnp.where(sample_at == begin + sample, ref[...].astype(f32), 0.0)
            pieces.append(jnp.sum(chosen, axis=1, keepdims=True))
        return jnp.broadcast_to(jnp.concatenate(pieces, axis=0), (FLATS, 128))

    steps_at = column(tsteps_ref)
    lane_at = lax.broadcasted_iota(jnp.int32, (FLATS, 128), 1).astype(f32)
    picked = jnp.where(steps_at == lane_at, 1.0, 0.0)
    keep_ref[...] = jnp.broadcast_to(jnp.sum(picked * roots_ref[0:1], axis=1, keepdims=True), (FLATS, 128))
    blend_ref[...] = jnp.broadcast_to(jnp.sum(picked * roots_ref[1:2], axis=1, keepdims=True), (FLATS, 128))
    adv_ref[...] = column(advantage_ref)
    time_ref[...] = dot(picked.astype(bf16), table_ref[...]).astype(bf16)
    for sample in range(2):
        actions_ref[sample] = jnp.zeros((STEPS, 128), f32)
        actions_ref[sample, :, 0:14] = actions_in[sample].astype(f32)

    def widen(f):
        noise_ref[rows_of(f)] = jnp.zeros((STEPS, 128), f32)
        noise_ref[rows_of(f), 0:14] = noise_in[rows_of(f)].astype(f32)

    each(widen)
    wide_in[...] = jnp.zeros_like(wide_in)
    wide_in[0:70] = win_in[...].astype(f32)
    win_ref[...] = wide_in[...].astype(bf16)
    wide_res[...] = jnp.zeros_like(wide_res)
    wide_res[70:84] = wres_in[...].astype(f32)
    wres_ref[...] = wide_res[...].astype(bf16)
    wide_out[...] = jnp.zeros_like(wide_out)
    wide_out[0:14] = wout_in[...].astype(f32)
    wout_t_ref[...] = wide_out[...].astype(bf16)
    wout_ref[...] = wide_out[...].T.astype(bf16)

    npad[...] = jnp.zeros_like(npad)
    pad[...] = jnp.zeros_like(pad)

    def make_cols(f):
        noisy = keep_ref[one(f)] * actions_ref[f // 8] + blend_ref[one(f)] * noise_ref[rows_of(f)]
        noisy = noisy.astype(bf16).astype(f32)
        npad[f, 8:72] = noisy
        total = pltpu.roll(noisy, 70, 1)
        for tap in range(5):
            total = total + pltpu.roll(npad[f, 6 + tap : 70 + tap], 14 * tap, 1)
        cols[rows_of(f)] = total.astype(bf16)

    each(make_cols)

    pl.semaphore_wait(barrier, 10)
    to_sibling(3, cond_ref.at[:, :, there], cond_sib)

    time_film = dot(time_ref[...], wtime_ref[...])
    film_cond = dot(mish_value(cond_ref[seg]).astype(bf16), wcond_ref[...])
    top = jnp.broadcast_to(film_cond[0:1], (8, 2 * C))
    low = jnp.broadcast_to(film_cond[1:2], (8, 2 * C))
    film[...] = jnp.concatenate([top, low], axis=0) + time_film

    def first_conv(b):
        rows = rows_of(b, BLOCK)
        out = dot(cols[rows], win_ref[...])
        pre[rows] = out
        res[rows] = dot(cols[rows], wres_ref[...])

    each(first_conv, 4)

    arrive(cond_sib, mr_sem.at[3])
    pairs = [cond_ref[j, 0:2, here] for j in range(MICRO)] + [cond_sib[j, 0:2] for j in range(MICRO)]
    act_all[y, x] = mish_value(jnp.concatenate(pairs, axis=0)).astype(bf16)
    spread(xs_sem, xr_sem, 0, act_all.at[y], x, x_peer)

    def centre(inverse):
        def total(f):
            sum1[one(f)] = jnp.sum(pre[rows_of(f)], axis=0, keepdims=True)

        each(total)
        mean1[...] = group_mean(sum1[...])

        def moved(f):
            left = pre[rows_of(f)] - mean1[one(f)]
            pre[rows_of(f)] = left
            sum1[one(f)] = jnp.sum(left * left, axis=0, keepdims=True)

        each(moved)
        inverse[...] = lax.rsqrt(group_mean(sum1[...]) + 1e-05)

    def mish_both(values):
        small, right, above, rest = mish_parts(values)
        inverse = 1.0 / (above + rest)
        logistic = jnp.where(right, 1.0, small) / (1.0 + small)
        ratio = above * inverse
        value = values * ratio
        return value, ratio + values * logistic * (rest * (2.0 * above + rest)) * (inverse * inverse)

    centre(inv1)

    def first_act(f):
        unit = pre[rows_of(f)] * inv1[one(f)]
        value, slope = mish_both(unit)
        unit1[rows_of(f)] = unit
        act1[rows_of(f)] = value
        slope1[rows_of(f)] = slope
        changed = film[one(f), 0:C] * value + film[one(f), C:]
        pad[f, 8:72] = changed.astype(bf16).astype(f32)
        for tap in range(5):
            mid[rows_of(f), C * tap : C * (tap + 1)] = pad[f, 6 + tap : 70 + tap].astype(bf16)

    each(first_act)

    gathered(xr_sem, 0, act_all.at[y], x)
    spread(ys_sem, yr_sem, 0, act_all, y, y_peer)

    def second_conv(b):
        rows = rows_of(b, BLOCK)
        pre[rows] = dot(mid[rows], wmid_ref[...])

    each(second_conv, 4)
    centre(inv2)

    def second_act(f):
        unit = pre[rows_of(f)] * inv2[one(f)]
        value, slope = mish_both(unit)
        unit2[rows_of(f)] = unit
        slope2[rows_of(f)] = slope
        block[rows_of(f)] = (value + res[rows_of(f)]).astype(bf16)

    each(second_act)

    def errors(f, total):
        rows = rows_of(f)
        error = dot(block[rows], wout_ref[...]) - noise_ref[rows]
        d_pred[rows] = (adv_ref[one(f)] * error * (2.0 / 896.0)).astype(bf16)
        return total + error * error

    err = lax.fori_loop(0, FLATS, errors, jnp.zeros((STEPS, 128), f32))
    err_sum = jnp.sum(err) * (1.0 / 896.0)

    def from_pred(b):
        rows = rows_of(b, BLOCK)
        out = dot(d_pred[rows], wout_t_ref[...])
        pre[rows] = out
        d_block[rows] = out.astype(bf16)

    each(from_pred, 4)

    def act_back(scale, unit, slope):
        def totals(f):
            grad = scale(f) * slope[rows_of(f)]
            pre[rows_of(f)] = grad
            sum1[one(f)] = jnp.sum(grad, axis=0, keepdims=True)
            sum2[one(f)] = jnp.sum(grad * unit[rows_of(f)], axis=0, keepdims=True)

        each(totals)
        mean1[...] = group_mean(sum1[...])
        mean2[...] = group_mean(sum2[...])

    act_back(lambda f: pre[rows_of(f)], unit2, slope2)

    def second_back(f):
        grad = inv2[one(f)] * (pre[rows_of(f)] - mean1[one(f)] - unit2[rows_of(f)] * mean2[one(f)])
        rounded = grad.astype(bf16)
        d_second[rows_of(f)] = rounded
        pad[f, 8:72] = rounded.astype(f32)
        for tap in range(5):
            back[rows_of(f), C * tap : C * (tap + 1)] = pad[f, 10 - tap : 74 - tap].astype(bf16)

    each(second_back)

    def over_rows(left, right):
        return lax.dot_general(left, right, (((0,), (0,)), ((), ())), preferred_element_type=f32)

    for tap in range(5):
        grad = over_rows(d_second[...], mid[:, C * tap : C * (tap + 1)]).astype(bf16)
        for s in range(4):
            for half in range(2):
                begin = 64 * (2 * tap + half)
                grads_a[s, begin : begin + 64] = grad[64 * s : 64 * (s + 1), 128 * half : 128 * (half + 1)]

    def ours(rows):
        return pl.ds(pl.multiple_of(core * rows, 16), rows)

    def theirs(rows):
        return pl.ds(pl.multiple_of(sibling * rows, 16), rows)

    def to_segments(number, grads, landed, out, slots, rows):
        out[...] = (grads[:, ours(rows), :].astype(f32) + landed[...].astype(f32)).astype(bf16)
        scatter(zs_sem, zr_sem, number, out, slots, seg, z_peer)
        slots[seg] = out[seg]

    def to_row(number, got, out, slots):
        out[...] = added(got).astype(bf16).reshape(out.shape)
        scatter(xs_sem, xr_sem, number, out, slots, x, x_peer)
        slots[x] = out[x]

    def to_column(number, got, slots):
        slots[y] = added(got).astype(bf16)
        spread(ys_sem, yr_sem, number, slots, y, y_peer)

    to_sibling(1, grads_a.at[:, theirs(ROWS_A), :], mp_a)

    def mid_back(b):
        rows = rows_of(b, BLOCK)
        pre[rows] = sum(
            lax.dot_general(
                back[rows, C * tap : C * (tap + 1)], wmid_ref[C * tap : C * (tap + 1)], (((1,), (1,)), ((), ())),
                preferred_element_type=f32,
            )
            for tap in range(5)
        )

    each(mid_back, 4)

    arrive(mp_a, mr_sem.at[1])
    to_segments(1, grads_a, mp_a, zo_a, zi_a, ROWS_A)

    def film_back(f):
        grad = pre[rows_of(f)]
        d_film[one(f), 0:C] = jnp.sum(grad * act1[rows_of(f)], axis=0, keepdims=True)
        d_film[one(f), C:] = jnp.sum(grad, axis=0, keepdims=True)

    each(film_back)
    film_ref[...] = jnp.zeros_like(film_ref)
    film_ref[0:1] = jnp.sum(d_film[0:8], axis=0, keepdims=True)
    film_ref[1:2] = jnp.sum(d_film[8:16], axis=0, keepdims=True)

    to_sibling(0, film_ref, film_sib)

    act_back(lambda f: pre[rows_of(f)] * film[one(f), 0:C], unit1, slope1)

    arrive(film_sib, mr_sem.at[0])
    film_out[...] = jnp.zeros_like(film_out)
    for s in range(SIDE):
        film_out[s, 0:2] = film_ref[0:2, 128 * s : 128 * (s + 1)]
        film_out[s, 2:4] = film_sib[0:2, 128 * s : 128 * (s + 1)]
    scatter(zs_sem, zr_sem, 0, film_out, film_z, seg, z_peer)
    film_z[seg] = film_out[seg]

    def first_back(f):
        grad = inv1[one(f)] * (pre[rows_of(f)] - mean1[one(f)] - unit1[rows_of(f)] * mean2[one(f)])
        d_first[rows_of(f)] = grad.astype(bf16)

    each(first_back)

    lane = lax.broadcasted_iota(jnp.int32, (C, 128), 1)
    inner = over_rows(d_first[...], cols[...])
    skip = over_rows(d_block[...], cols[...])
    out = pltpu.roll(over_rows(block[...], d_pred[...]), 84, 1)
    joined = jnp.where(lane < 70, inner, jnp.where(lane < 84, skip, jnp.where(lane < 98, out, err_sum))).astype(bf16)
    timed = over_rows(time_ref[...], d_film[...].astype(bf16)).astype(bf16)
    for s in range(4):
        grads_b[s, 0:64] = joined[64 * s : 64 * (s + 1)]
        grads_b[s, 64:320] = timed[:, 128 * s : 128 * (s + 1)]
        grads_b[s, 320:384] = jnp.zeros((64, 128), bf16)
    to_sibling(2, grads_b.at[:, theirs(ROWS_B), :], mp_b)

    gathered(zr_sem, 1, zi_a, seg)
    to_row(2, zi_a, xo_a, xi_a)
    arrive(mp_b, mr_sem.at[2])
    to_segments(2, grads_b, mp_b, zo_b, zi_b, ROWS_B)

    gathered(zr_sem, 0, film_z, seg)
    pairs = [film_z[j, 0:2] for j in range(MICRO)] + [film_z[j, 2:4] for j in range(MICRO)]
    film_all[y, x] = jnp.concatenate(pairs, axis=0).astype(bf16)
    spread(xs_sem, xr_sem, 1, film_all.at[y], x, x_peer)

    gathered(xr_sem, 2, xi_a, x)
    to_column(2, xi_a, yi_a)
    gathered(zr_sem, 2, zi_b, seg)
    to_row(3, zi_b, xo_b, xi_b)
    gathered(xr_sem, 1, film_all.at[y], x)
    spread(ys_sem, yr_sem, 1, film_all, y, y_peer)
    gathered(yr_sem, 2, yi_a, y)
    full_a[core, x] = added(yi_a).astype(bf16)
    spread(xs_sem, xr_sem, 4, full_a.at[core], x, x_peer)
    gathered(xr_sem, 3, xi_b, x)
    to_column(3, xi_b, yi_b)

    low = jnp.where(core == 0, film_ref[0:2], film_sib[0:2])
    high = jnp.where(core == 0, film_sib[0:2], film_ref[0:2])
    film_rows = jnp.concatenate([low, high, jnp.zeros((12, 512), jnp.float32)], axis=0).astype(jnp.bfloat16)
    own_cond, sib_cond = cond_ref[seg, 0:2, here], cond_sib[seg, 0:2]
    cond_rows = jnp.concatenate(
        [jnp.where(core == 0, own_cond, sib_cond), jnp.where(core == 0, sib_cond, own_cond)], axis=0
    )
    back = lax.dot_general(film_rows, wc_ref[...], (((1,), (1,)), ((), ())), preferred_element_type=jnp.float32)
    gcond_ref[...] = back[0:4] * mish_slope(cond_rows)

    gathered(xr_sem, 4, full_a.at[core], x)
    to_sibling(4, full_a.at[core], full_a.at[core])
    gathered(yr_sem, 3, yi_b, y)
    full_b[core, x] = added(yi_b).astype(bf16)
    spread(xs_sem, xr_sem, 5, full_b.at[core], x, x_peer)
    gathered(yr_sem, 0, act_all, y)
    gathered(yr_sem, 1, film_all, y)
    gathered(xr_sem, 5, full_b.at[core], x)
    to_sibling(5, full_b.at[core], full_b.at[core])
    arrive(full_a.at[sibling], mr_sem.at[4])
    arrive(full_b.at[sibling], mr_sem.at[5])
    for sent_copy in started:
        sent_copy.wait_send()


def unpack_kernel(full_a, full_b, act_all, film_all, back_ref, gin, gmid, gres, gout, gtime, gwc, gcond, loss):
    f32 = jnp.float32
    flat_a = full_a[...].astype(f32).reshape(640, 128)
    for q in range(10):
        gmid[:, 128 * q : 128 * (q + 1)] = flat_a[64 * q : 64 * (q + 1)]
    flat_b = full_b[...].astype(f32).reshape(384, 128)
    joined = flat_b[0:64]
    turned = joined.T
    gin[...] = joined[:, 0:70]
    gres[...] = turned[70:84]
    gout[...] = turned[84:98]
    loss[...] = joined[0:1, 98:99] * (1.0 / 2048.0)
    gtime[...] = flat_b[64:320]
    gcond[...] = back_ref[...]
    gwc[...] = lax.dot_general(
        act_all[...].reshape(256, HALF), film_all[...].reshape(256, 128), (((0,), (0,)), ((), ())),
        preferred_element_type=f32,
    )


def step_tables():
    table = schedule()
    roots = np.zeros((8, 128))
    roots[0, :TSTEPS], roots[1, :TSTEPS] = np.sqrt(table), np.sqrt(1.0 - table)
    half = C // 2
    angles = np.arange(TSTEPS)[:, None] * np.exp(-math.log(10000.0) * np.arange(half) / (half - 1))[None]
    embedded = np.concatenate([np.sin(angles), np.cos(angles)], axis=1)
    times = np.zeros((128, C))
    times[:TSTEPS] = embedded * np.tanh(np.log1p(np.exp(embedded)))
    return jnp.asarray(roots, jnp.float32), jnp.asarray(times, jnp.float32).astype(jnp.bfloat16)


def finish(cond, w_cond_full, w_cond, noise, actions, tsteps, advantage, w_in, w_res, w_mid, w_out, w_time):
    bf16, f32 = jnp.bfloat16, jnp.float32
    roots, times = step_tables()
    vmem = pl.BlockSpec(memory_space=pltpu.VMEM)
    flat_rows = FLATS * STEPS
    big, small = pltpu.VMEM((flat_rows, C), f32), pltpu.VMEM((FLATS, C), f32)
    big16 = pltpu.VMEM((flat_rows, C), bf16)
    rows_a, rows_b = pltpu.VMEM((SIDE, ROWS_A, 128), bf16), pltpu.VMEM((SIDE, ROWS_B, 128), bf16)
    part_a, part_b = pltpu.VMEM((SIDE, ROWS_A // SIDE, 128), bf16), pltpu.VMEM((SIDE, ROWS_B // SIDE, 128), bf16)
    dma = pltpu.SemaphoreType.DMA
    return pl.pallas_call(
        finish_kernel,
        out_shape=(
            jax.ShapeDtypeStruct((2, SIDE, ROWS_A // SIDE, 128), bf16),
            jax.ShapeDtypeStruct((2, SIDE, ROWS_B // SIDE, 128), bf16),
            jax.ShapeDtypeStruct((SIDE, SIDE, 16, HALF), bf16),
            jax.ShapeDtypeStruct((SIDE, SIDE, 16, 128), bf16),
            jax.ShapeDtypeStruct((4, HALF), f32),
        ),
        in_specs=[vmem] * 14,
        out_specs=(vmem,) * 5,
        scratch_shapes=[
            pltpu.VMEM((flat_rows, 128), f32),
            pltpu.VMEM((2, STEPS, 128), f32),
            pltpu.VMEM((FLATS, 128), f32),
            pltpu.VMEM((FLATS, 128), f32),
            pltpu.VMEM((FLATS, 128), f32),
            pltpu.VMEM((FLATS, C), bf16),
            pltpu.VMEM((128, C), f32),
            pltpu.VMEM((128, C), f32),
            pltpu.VMEM((128, C), f32),
            pltpu.VMEM((128, C), bf16),
            pltpu.VMEM((128, C), bf16),
            pltpu.VMEM((C, 128), bf16),
            pltpu.VMEM((128, C), bf16),
            pltpu.VMEM((FLATS, 80, 128), f32),
            pltpu.VMEM((flat_rows, 128), bf16),
            pltpu.VMEM((FLATS, 80, C), f32),
            pltpu.VMEM((flat_rows, 5 * C), bf16),
            pltpu.VMEM((flat_rows, 5 * C), bf16),
            big, big, big, big, big, big, big,
            big16, big16,
            pltpu.VMEM((flat_rows, 128), bf16),
            big16, big16,
            pltpu.VMEM((FLATS, 2 * C), f32),
            pltpu.VMEM((FLATS, 2 * C), f32),
            small, small, small, small, small, small,
            pltpu.VMEM((MICRO, 8, HALF), f32),
            pltpu.VMEM((8, 512), f32),
            pltpu.VMEM((8, 512), f32),
            pltpu.VMEM((SIDE, 8, 128), f32),
            pltpu.VMEM((SIDE, 8, 128), f32),
            pltpu.VMEM((SIDE, 2 * ROWS_A, 128), bf16),
            pltpu.VMEM((SIDE, 2 * ROWS_B, 128), bf16),
            rows_a, rows_b, rows_a, rows_b, rows_a, rows_b,
            part_a, part_b, part_a, part_b, part_a, part_b,
            dma((6,)), dma((6,)),
            dma((3, 3)), dma((3, 3)),
            dma((6, 3)), dma((6, 3)),
            dma((4, 3)), dma((4, 3)),
        ],
        compiler_params=pltpu.CompilerParams(
            collective_id=1, has_side_effects=True, vmem_limit_bytes=48 * 2**20
        ),
    )(
        cond, w_cond_full, w_cond, noise, actions, tsteps, advantage, roots, times, w_in, w_res, w_mid, w_out, w_time
    )


def unpack(*arrays):
    f32 = jnp.float32
    vmem = pl.BlockSpec(memory_space=pltpu.VMEM)
    shapes = ((64, 70), (64, 1280), (14, 64), (14, 64), (256, 128), (HALF, 128), (4, HALF), (1, 1))
    return pl.pallas_call(
        unpack_kernel,
        out_shape=tuple(jax.ShapeDtypeStruct(shape, f32) for shape in shapes),
        in_specs=[vmem] * 5,
        out_specs=(vmem,) * 8,
        compiler_params=pltpu.CompilerParams(vmem_limit_bytes=32 * 2**20),
    )(*arrays)


def body(
    trunk_in, norm_gain, w_gate, w_up, w_down, w_cond, w_time, w_in, w_mid, w_res, w_out,
    tsteps, advantage, actions, noise,
):
    cond_all, w_cond_full = trunk(trunk_in, norm_gain, w_gate[0], w_up[0], w_down[0].T, w_cond)
    begin = 4 * lax.axis_index("segment") + 2 * lax.axis_index("mp")

    def own(values):
        return lax.dynamic_slice_in_dim(values, begin, 2, 0)

    parts = finish(
        cond_all, w_cond_full, w_cond, own(noise).reshape(FLATS * STEPS, 14), own(actions), tsteps.T, advantage.T,
        w_in, w_res, w_mid, w_out.T, w_time,
    )
    gin, gmid, gres, gout, gtime, gwc, gcond, loss = unpack(*parts)
    return gin.T, gmid.T, gres, gout.T, gtime, gwc, gcond, loss.reshape(1)


def solution(mesh):
    in_specs = (
        P("dp", "mp"),
        P("segment", None),
        P("segment", "dp", "mp"),
        P("segment", "dp", "mp"),
        P("segment", "mp", "dp"),
        P("mp", None),
        P(),
        P(),
        P(),
        P(),
        P(),
        P("dp", None),
        P("dp", None),
        P("dp", None, None),
        P("dp", None, None, None),
    )
    out_specs = (
        P(None, "segment"),
        P(None, "segment"),
        P(None, "segment"),
        P("segment", None),
        P(None, "segment"),
        P("mp", "segment"),
        P(("dp", "segment"), "mp"),
        P(),
    )
    return jax.shard_map(body, mesh=mesh, in_specs=in_specs, out_specs=out_specs, check_vma=False)
```

```python
import functools
import math

import jax
import jax.numpy as jnp
import numpy as np
from jax import lax
from jax.experimental import pallas as pl
from jax.experimental.pallas import tpu as pltpu
from jax.sharding import PartitionSpec as P

MESH = pl.DeviceIdType.MESH
TSTEPS = 100
SIDE = 4
MICRO = 4
ROWS = 32
BATCHES = 2
OWN = 64
PART = 512
PARTS = 5
D = 2560
HALF = 1280
FH = 1792
SHARD = 160
CUT = 80
TILE = 256


def schedule():
    grid = np.arange(TSTEPS + 1, dtype=np.float64) / TSTEPS
    curve = np.cos((grid + 0.008) / 1.008 * math.pi / 2.0) ** 2
    betas = np.minimum(1.0 - curve[1:] / curve[:-1], 0.999)
    return np.cumprod(1.0 - betas)


def trunk_kernel(
    x_ref, gain_ref, wg_ref, wu_ref, wd_ref, wc_ref,
    cond_ref, wcond_ref,
    weights, first, arrived, leaving, normed, hidden, partial, share, other,
    own_sem, gs_sem, gr_sem, ms_sem, mr_sem, ps_sem, pr_sem, zs_sem, zr_sem, cs_sem, cr_sem,
):
    dp, seg, core = lax.axis_index("dp"), lax.axis_index("segment"), lax.axis_index("mp")
    y, x = dp // SIDE, dp % SIDE
    sibling = 1 - core

    def at(axis, delta):
        if axis == "x":
            return y * SIDE + (x + delta + SIDE) % SIDE
        return ((y + delta + SIDE) % SIDE) * SIDE + x

    barrier = pltpu.get_barrier_semaphore()
    for axis in ("x", "y"):
        for delta in (1, -1):
            pl.semaphore_signal(barrier, inc=1, device_id={"dp": at(axis, delta)}, device_id_type=MESH)
    pl.semaphore_signal(barrier, inc=1, device_id={"mp": sibling}, device_id_type=MESH)
    for step in range(1, 4):
        pl.semaphore_signal(barrier, inc=1, device_id={"segment": (seg + step) % 4}, device_id_type=MESH)
    pl.semaphore_wait(barrier, 8)

    sources = (wg_ref, wu_ref, wd_ref)
    chunks = [(which, part) for which in range(3) for part in range(2)]

    def spot(which, part, px, py, begin=0, size=CUT):
        row = (py * SIDE + px) * SHARD + part * CUT + begin
        return weights.at[which, pl.ds(pl.multiple_of(row, 16), size), :]

    def place(chunk, p_off, q_off, begin=0, size=CUT):
        which, part = chunk
        dx, dy = (p_off, q_off) if part == 0 else (q_off, p_off)
        return spot(which, part, (x + dx + SIDE) % SIDE, (y + dy + SIDE) % SIDE, begin, size)

    def axes(chunk):
        return ("x", "y") if chunk[1] == 0 else ("y", "x")

    def piece(chunk, kind):
        return (0, 48) if kind == 0 else (48, 32)

    def make(chunk, number, src, dst, axis, delta):
        q = chunks.index(chunk)
        return pltpu.make_async_remote_copy(
            src_ref=src, dst_ref=dst, send_sem=gs_sem.at[q, number], recv_sem=gr_sem.at[q, number],
            device_id={"dp": at(axis, delta)}, device_id_type=MESH,
        )

    OFF = (0, -1, 1, 2)

    def spec(chunk, number):
        p_axis, q_axis = axes(chunk)
        if number < 4:
            delta = 1 if number % 2 == 0 else -1
            if number < 2:
                return p_axis, delta, 0, 0, 0, CUT
            begin, size = piece(chunk, number - 2)
            return p_axis, delta, -delta, 0, begin, size
        slot, kind = divmod(number - 4, 4)
        delta = 1 if kind % 2 == 0 else -1
        if kind < 2:
            return q_axis, delta, OFF[slot], 0, 0, CUT
        begin, size = piece(chunk, kind - 2)
        return q_axis, delta, OFF[slot], -delta, begin, size

    def source_of(chunk, number):
        _, _, p_off, q_off, begin, size = spec(chunk, number)
        if p_off == 0 and q_off == 0:
            return sources[chunk[0]].at[pl.ds(chunk[1] * CUT + begin, size), :]
        return place(chunk, p_off, q_off, begin, size)

    def send(chunk, number):
        axis, delta, p_off, q_off, begin, size = spec(chunk, number)
        make(chunk, number, source_of(chunk, number), place(chunk, p_off, q_off, begin, size), axis, delta).start()

    def receive(chunk, number):
        axis, delta, p_off, q_off, begin, size = spec(chunk, number)
        if number < 4:
            p_off = p_off - delta
        else:
            q_off = q_off - delta
        spot_here = place(chunk, p_off, q_off, begin, size)
        make(chunk, number, spot_here, spot_here, axis, delta).wait_recv()

    def sent(chunk, number):
        axis, delta, p_off, q_off, begin, size = spec(chunk, number)
        make(chunk, number, source_of(chunk, number), place(chunk, p_off, q_off, begin, size), axis, delta).wait_send()

    own = []
    for chunk in chunks:
        for number in (0, 1, 4, 5):
            send(chunk, number)
    for which in range(3):
        keep = pltpu.make_async_copy(
            sources[which], weights.at[which, pl.ds(pl.multiple_of(dp * SHARD, 16), SHARD), :], own_sem.at[which]
        )
        keep.start()
        own.append(keep)

    def sibling_copy(number, src, dst):
        return pltpu.make_async_remote_copy(
            src_ref=src, dst_ref=dst, send_sem=ms_sem.at[number], recv_sem=mr_sem.at[number],
            device_id={"mp": sibling}, device_id_type=MESH,
        )

    here = pl.ds(pl.multiple_of(core * HALF, 128), HALF)
    there = pl.ds(pl.multiple_of(sibling * HALF, 128), HALF)
    def slot_of(j, features):
        return first.at[j // 2, pl.ds(32 * (j % 2), ROWS), features]

    for j in range(MICRO):
        src = x_ref.at[pl.ds(pl.multiple_of(64 * j + 32 * sibling, 16), ROWS), :]
        sibling_copy(j, src, slot_of(j, here)).start()
        kept = pltpu.make_async_copy(
            x_ref.at[pl.ds(pl.multiple_of(64 * j + 32 * core, 16), ROWS), :], slot_of(j, here), own_sem.at[3 + j]
        )
        kept.start()
        own.append(kept)
    here_rows = wcond_ref.at[pl.ds(pl.multiple_of(core * HALF, 16), HALF), :]
    there_rows = wcond_ref.at[pl.ds(pl.multiple_of(sibling * HALF, 16), HALF), :]
    sibling_copy(4, wc_ref, here_rows).start()
    kept = pltpu.make_async_copy(wc_ref, here_rows, own_sem.at[7])
    kept.start()
    own.append(kept)
    cond_ref[...] = jnp.zeros_like(cond_ref)

    for chunk in chunks:
        for number in (0, 1):
            receive(chunk, number)
            send(chunk, 2 + number)
            slot = 1 + number
            send(chunk, 4 + 4 * slot)
            send(chunk, 5 + 4 * slot)
        for kind in (0, 1):
            receive(chunk, 4 + kind)
            send(chunk, 6 + kind)
    for chunk in chunks:
        for number in (2, 3):
            receive(chunk, number)
        send(chunk, 16)
        send(chunk, 17)
        for slot in (1, 2):
            for kind in (0, 1):
                receive(chunk, 4 + 4 * slot + kind)
                send(chunk, 6 + 4 * slot + kind)
    for chunk in chunks:
        for kind in (0, 1):
            receive(chunk, 16 + kind)
            send(chunk, 18 + kind)
    for j in range(MICRO):
        sibling_copy(j, slot_of(j, there), slot_of(j, there)).wait_recv()
    for keep in own[3:7]:
        keep.wait()

    def finish_gather():
        for chunk in chunks:
            for slot in range(4):
                for kind in (2, 3):
                    receive(chunk, 4 + 4 * slot + kind)
        for keep in own[:3] + own[7:]:
            keep.wait()

    def z_copy(b, g):
        return pltpu.make_async_remote_copy(
            src_ref=leaving.at[b, g], dst_ref=arrived.at[b, g], send_sem=zs_sem.at[b, g], recv_sem=zr_sem.at[b, g],
            device_id={"segment": (seg + 1) % 4}, device_id_type=MESH,
        )

    def share_copy(b, g):
        return pltpu.make_async_remote_copy(
            src_ref=share.at[b, g], dst_ref=other.at[b, g], send_sem=ps_sem.at[b, g], recv_sem=pr_sem.at[b, g],
            device_id={"mp": sibling}, device_id_type=MESH,
        )

    def normed_copy(b):
        return sibling_copy(5 + b, normed.at[b, pl.ds(0, OWN)], normed.at[b, pl.ds(OWN, OWN)])

    def cond_copy(j, target):
        return pltpu.make_async_remote_copy(
            src_ref=cond_ref.at[j], dst_ref=cond_ref.at[j], send_sem=cs_sem.at[j, target], recv_sem=cr_sem.at[j],
            device_id={"segment": target}, device_id_type=MESH,
        )

    def columns_of(g):
        return slice(PART * g, PART * (g + 1))

    def normalize(b):
        states = [arrived[b, g].astype(jnp.float32) for g in range(PARTS)]
        total = sum(jnp.sum(state * state, axis=1, keepdims=True) for state in states)
        factor = lax.rsqrt(total * (1.0 / D) + 1e-05)
        for g in range(PARTS):
            gain = gain_ref[:, columns_of(g)].astype(jnp.float32)
            normed[b, 0:OWN, columns_of(g)] = (states[g] * factor * gain).astype(jnp.bfloat16)
        normed_copy(b).start()

    def batch(b, carry):
        @pl.when(seg > 0)
        def _():
            for g in range(PARTS):
                z_copy(b, g).wait_recv()
            normalize(b)

        normed_copy(b).wait_recv()
        for n in range(FH // TILE):
            cols = slice(n * TILE, (n + 1) * TILE)
            rows = normed[b]
            gate = jnp.dot(rows, weights[0, :, cols], preferred_element_type=jnp.float32)
            lift = jnp.dot(rows, weights[1, :, cols], preferred_element_type=jnp.float32)
            hidden[:, cols] = (gate / (1.0 + jnp.exp(-gate)) * lift).astype(jnp.bfloat16)

        def finish(g):
            share_copy(b, g).wait_recv()
            whole = partial[g] + other[b, g].astype(jnp.float32)
            leaving[b, g] = (arrived[b, g].astype(jnp.float32) + whole).astype(jnp.bfloat16)

            @pl.when(seg < 3)
            def _():
                z_copy(b, g).start()

        for g in range(PARTS):
            for half in range(2):
                part = slice(TILE * half, TILE * (half + 1))
                out = lax.dot_general(
                    hidden[...], weights[2, PART * g + TILE * half : PART * g + TILE * (half + 1), :],
                    (((1,), (1,)), ((), ())), preferred_element_type=jnp.float32,
                )
                partial[g, :, part] = out[0:OWN]
                share[b, g, :, part] = out[OWN:].astype(jnp.bfloat16)
            share_copy(b, g).start()
            if g > 0:
                finish(g - 1)
        finish(PARTS - 1)

        @pl.when(seg == 3)
        def _():
            for half in range(2):
                for g in range(PARTS):
                    rows = leaving[b, g, ROWS * half : ROWS * (half + 1)].astype(jnp.float32)
                    mean = jnp.mean(rows.reshape(2, 16, PART), axis=1)
                    cond_ref[2 * b + half, 0:2, columns_of(g)] = mean.astype(jnp.bfloat16).astype(jnp.float32)
                for target in range(3):
                    cond_copy(2 * b + half, target).start()

        return carry

    @pl.when(seg == 0)
    def _():
        for b in range(BATCHES):
            for g in range(PARTS):
                arrived[b, g] = first[b, :, columns_of(g)]
            normalize(b)

    finish_gather()
    lax.fori_loop(0, BATCHES, batch, 0)

    for chunk in chunks:
        for number in range(20):
            sent(chunk, number)
    for b in range(BATCHES):
        normed_copy(b).wait_send()
        for g in range(PARTS):
            share_copy(b, g).wait_send()

    @pl.when(seg < 3)
    def _():
        for b in range(BATCHES):
            for g in range(PARTS):
                z_copy(b, g).wait_send()

    for j in range(MICRO):
        sibling_copy(j, x_ref.at[pl.ds(0, ROWS), :], slot_of(j, there)).wait_send()

        @pl.when(seg < 3)
        def _(j=j):
            cond_copy(j, 0).wait_recv()

        @pl.when(seg == 3)
        def _(j=j):
            for target in range(3):
                cond_copy(j, target).wait_send()

    last = sibling_copy(4, wc_ref, there_rows)
    last.wait_recv()
    last.wait_send()


def trunk(trunk_in, norm_gain, w_gate, w_up, w_down_t, w_cond):
    anywhere = pl.BlockSpec(memory_space=pl.ANY)
    vmem = pl.BlockSpec(memory_space=pltpu.VMEM)
    dma = pltpu.SemaphoreType.DMA
    bf16 = jnp.bfloat16
    return pl.pallas_call(
        trunk_kernel,
        out_shape=(
            jax.ShapeDtypeStruct((MICRO, 8, D), jnp.float32),
            jax.ShapeDtypeStruct((D, w_cond.shape[1]), bf16),
        ),
        in_specs=[anywhere, vmem, anywhere, anywhere, anywhere, anywhere],
        out_specs=(vmem, anywhere),
        scratch_shapes=[
            pltpu.VMEM((3, D, FH), bf16),
            pltpu.VMEM((BATCHES, OWN, D), bf16),
            pltpu.VMEM((BATCHES, PARTS, OWN, PART), bf16),
            pltpu.VMEM((BATCHES, PARTS, OWN, PART), bf16),
            pltpu.VMEM((BATCHES, 2 * OWN, D), bf16),
            pltpu.VMEM((2 * OWN, FH), bf16),
            pltpu.VMEM((PARTS, OWN, PART), jnp.float32),
            pltpu.VMEM((BATCHES, PARTS, OWN, PART), bf16),
            pltpu.VMEM((BATCHES, PARTS, OWN, PART), bf16),
            dma((8,)),
            dma((6, 20)),
            dma((6, 20)),
            dma((7,)),
            dma((7,)),
            dma((BATCHES, PARTS)),
            dma((BATCHES, PARTS)),
            dma((BATCHES, PARTS)),
            dma((BATCHES, PARTS)),
            dma((MICRO, 3)),
            dma((MICRO,)),
        ],
        compiler_params=pltpu.CompilerParams(
            collective_id=0, has_side_effects=True, vmem_limit_bytes=52 * 2**20
        ),
    )(trunk_in, norm_gain, w_gate, w_up, w_down_t, w_cond)


def mish_parts(values):
    small = jnp.exp(-jnp.abs(values))
    right = values > 0
    top = jnp.where(right, 1.0 + 2.0 * small, small * (small + 2.0))
    rest = jnp.where(right, 2.0 * small * small, 2.0)
    return small, right, top, rest


def mish_value(values):
    _, _, top, rest = mish_parts(values)
    return values * (top / (top + rest))


def mish_slope(values):
    small, right, top, rest = mish_parts(values)
    inverse = 1.0 / (top + rest)
    logistic = jnp.where(right, 1.0, small) / (1.0 + small)
    return top * inverse + values * logistic * (rest * (2.0 * top + rest)) * (inverse * inverse)


FLATS = 16
STEPS = 64
C = 256
BLOCK = 256
ROWS_A = 320
ROWS_B = 192


def finish_kernel(
    cond_ref, wcond_ref, wc_ref, noise_in, actions_in, tsteps_ref, advantage_ref, roots_ref, table_ref,
    win_in, wres_in, wmid_ref, wout_in, wtime_ref,
    full_a, full_b, act_all, film_all, gcond_ref,
    noise_ref, actions_ref, keep_ref, blend_ref, adv_ref, time_ref, wide_in, wide_res, wide_out, win_ref, wres_ref,
    wout_ref, wout_t_ref, npad, cols, pad, mid, back, pre, res, unit1, act1, slope1, unit2, slope2, block, d_block, d_pred,
    d_second, d_first, film, d_film, sum1, sum2, inv1, inv2, mean1, mean2,
    cond_sib, film_ref, film_sib, film_out, film_z,
    grads_a, grads_b, mp_a, mp_b, zo_a, zo_b, zi_a, zi_b, xo_a, xi_a, yi_a, xi_b, yi_b,
    ms_sem, mr_sem, zs_sem, zr_sem, xs_sem, xr_sem, ys_sem, yr_sem,
):
    dp, seg, core = lax.axis_index("dp"), lax.axis_index("segment"), lax.axis_index("mp")
    y, x = dp // SIDE, dp % SIDE
    sibling = 1 - core

    def x_peer(step):
        return {"dp": y * SIDE + (x + step) % SIDE}

    def y_peer(step):
        return {"dp": ((y + step) % SIDE) * SIDE + x}

    def z_peer(step):
        return {"segment": (seg + step) % SIDE}

    barrier = pltpu.get_barrier_semaphore()
    pl.semaphore_signal(barrier, inc=1, device_id={"mp": sibling}, device_id_type=MESH)
    for step in range(1, SIDE):
        for peer in (x_peer, y_peer, z_peer):
            pl.semaphore_signal(barrier, inc=1, device_id=peer(step), device_id_type=MESH)

    def copy(src, dst, out_sem, in_sem, peer):
        return pltpu.make_async_remote_copy(
            src_ref=src, dst_ref=dst, send_sem=out_sem, recv_sem=in_sem, device_id=peer, device_id_type=MESH
        )

    started = []

    def launch(src, dst, out_sem, in_sem, peer):
        one = copy(src, dst, out_sem, in_sem, peer)
        one.start()
        started.append(one)

    def arrive(dst, in_sem):
        copy(dst, dst, ms_sem.at[0], in_sem, {"mp": sibling}).wait_recv()

    def to_sibling(number, src, dst):
        launch(src, dst, ms_sem.at[number], mr_sem.at[number], {"mp": sibling})

    def scatter(out_sem, in_sem, number, src, dst, me, peer):
        for step in range(1, SIDE):
            launch(
                src.at[(me + step) % SIDE], dst.at[me], out_sem.at[number, step - 1], in_sem.at[number, step - 1], peer(step)
            )

    def spread(out_sem, in_sem, number, slots, me, peer):
        for step in range(1, SIDE):
            launch(slots.at[me], slots.at[me], out_sem.at[number, step - 1], in_sem.at[number, step - 1], peer(step))

    def gathered(in_sem, number, slots, me):
        for step in range(1, SIDE):
            arrive(slots.at[(me - step + SIDE) % SIDE], in_sem.at[number, step - 1])

    def added(slots):
        pieces = [slots[k].astype(jnp.float32) for k in range(SIDE)]
        return (pieces[0] + pieces[1]) + (pieces[2] + pieces[3])

    here = pl.ds(pl.multiple_of(core * HALF, 128), HALF)
    there = pl.ds(pl.multiple_of(sibling * HALF, 128), HALF)
    bf16, f32 = jnp.bfloat16, jnp.float32

    def rows_of(f, size=STEPS):
        return pl.ds(pl.multiple_of(f * size, size), size)

    def one(f):
        return pl.ds(f, 1)

    def each(body, count=FLATS):
        def step(f, carry):
            body(f)
            return carry

        lax.fori_loop(0, count, step, 0, unroll=4 if count == FLATS else 2)

    lanes = lax.broadcasted_iota(jnp.int32, (C, C), 1)
    row_ids = lax.broadcasted_iota(jnp.int32, (C, C), 0)
    same = jnp.where(lanes // 32 == row_ids // 32, 1.0 / 2048.0, 0.0).astype(bf16)

    def group_mean(values):
        high = values.astype(bf16)
        rest = values - high.astype(f32)
        middle = rest.astype(bf16)
        low = (rest - middle.astype(f32)).astype(bf16)
        count = values.shape[0]
        sums = jnp.dot(jnp.concatenate([high, middle, low], axis=0), same, preferred_element_type=f32)
        return sums[0:count] + (sums[count : 2 * count] + sums[2 * count : 3 * count])

    def dot(left, right):
        return jnp.dot(left, right, preferred_element_type=f32)

    begin = 4 * seg + 2 * core
    sample_at = lax.broadcasted_iota(jnp.int32, (8, 16), 1)

    def column(ref):
        pieces = []
        for sample in range(2):
            chosen = jnp.where(sample_at == begin + sample, ref[...].astype(f32), 0.0)
            pieces.append(jnp.sum(chosen, axis=1, keepdims=True))
        return jnp.broadcast_to(jnp.concatenate(pieces, axis=0), (FLATS, 128))

    steps_at = column(tsteps_ref)
    lane_at = lax.broadcasted_iota(jnp.int32, (FLATS, 128), 1).astype(f32)
    picked = jnp.where(steps_at == lane_at, 1.0, 0.0)
    keep_ref[...] = jnp.broadcast_to(jnp.sum(picked * roots_ref[0:1], axis=1, keepdims=True), (FLATS, 128))
    blend_ref[...] = jnp.broadcast_to(jnp.sum(picked * roots_ref[1:2], axis=1, keepdims=True), (FLATS, 128))
    adv_ref[...] = column(advantage_ref)
    time_ref[...] = dot(picked.astype(bf16), table_ref[...]).astype(bf16)
    for sample in range(2):
        actions_ref[sample] = jnp.zeros((STEPS, 128), f32)
        actions_ref[sample, :, 0:14] = actions_in[sample].astype(f32)

    def widen(f):
        noise_ref[rows_of(f)] = jnp.zeros((STEPS, 128), f32)
        noise_ref[rows_of(f), 0:14] = noise_in[rows_of(f)].astype(f32)

    each(widen)
    wide_in[...] = jnp.zeros_like(wide_in)
    wide_in[0:70] = win_in[...].astype(f32)
    win_ref[...] = wide_in[...].astype(bf16)
    wide_res[...] = jnp.zeros_like(wide_res)
    wide_res[70:84] = wres_in[...].astype(f32)
    wres_ref[...] = wide_res[...].astype(bf16)
    wide_out[...] = jnp.zeros_like(wide_out)
    wide_out[0:14] = wout_in[...].astype(f32)
    wout_t_ref[...] = wide_out[...].astype(bf16)
    wout_ref[...] = wide_out[...].T.astype(bf16)

    npad[...] = jnp.zeros_like(npad)
    pad[...] = jnp.zeros_like(pad)

    def make_cols(f):
        noisy = keep_ref[one(f)] * actions_ref[f // 8] + blend_ref[one(f)] * noise_ref[rows_of(f)]
        noisy = noisy.astype(bf16).astype(f32)
        npad[f, 8:72] = noisy
        total = pltpu.roll(noisy, 70, 1)
        for tap in range(5):
            total = total + pltpu.roll(npad[f, 6 + tap : 70 + tap], 14 * tap, 1)
        cols[rows_of(f)] = total.astype(bf16)

    each(make_cols)

    pl.semaphore_wait(barrier, 10)
    to_sibling(3, cond_ref.at[:, :, there], cond_sib)

    time_film = dot(time_ref[...], wtime_ref[...])
    film_cond = dot(mish_value(cond_ref[seg]).astype(bf16), wcond_ref[...])
    top = jnp.broadcast_to(film_cond[0:1], (8, 2 * C))
    low = jnp.broadcast_to(film_cond[1:2], (8, 2 * C))
    film[...] = jnp.concatenate([top, low], axis=0) + time_film

    def first_conv(b):
        rows = rows_of(b, BLOCK)
        out = dot(cols[rows], win_ref[...])
        pre[rows] = out
        res[rows] = dot(cols[rows], wres_ref[...])

    each(first_conv, 4)

    arrive(cond_sib, mr_sem.at[3])
    pairs = [cond_ref[j, 0:2, here] for j in range(MICRO)] + [cond_sib[j, 0:2] for j in range(MICRO)]
    act_all[y, x] = mish_value(jnp.concatenate(pairs, axis=0)).astype(bf16)
    spread(xs_sem, xr_sem, 0, act_all.at[y], x, x_peer)

    def centre(inverse):
        def total(f):
            sum1[one(f)] = jnp.sum(pre[rows_of(f)], axis=0, keepdims=True)

        each(total)
        mean1[...] = group_mean(sum1[...])

        def moved(f):
            left = pre[rows_of(f)] - mean1[one(f)]
            pre[rows_of(f)] = left
            sum1[one(f)] = jnp.sum(left * left, axis=0, keepdims=True)

        each(moved)
        inverse[...] = lax.rsqrt(group_mean(sum1[...]) + 1e-05)

    def mish_both(values):
        small, right, above, rest = mish_parts(values)
        inverse = 1.0 / (above + rest)
        logistic = jnp.where(right, 1.0, small) / (1.0 + small)
        ratio = above * inverse
        value = values * ratio
        return value, ratio + values * logistic * (rest * (2.0 * above + rest)) * (inverse * inverse)

    centre(inv1)

    def first_act(f):
        unit = pre[rows_of(f)] * inv1[one(f)]
        value, slope = mish_both(unit)
        unit1[rows_of(f)] = unit
        act1[rows_of(f)] = value
        slope1[rows_of(f)] = slope
        changed = film[one(f), 0:C] * value + film[one(f), C:]
        pad[f, 8:72] = changed.astype(bf16).astype(f32)
        for tap in range(5):
            mid[rows_of(f), C * tap : C * (tap + 1)] = pad[f, 6 + tap : 70 + tap].astype(bf16)

    each(first_act)

    gathered(xr_sem, 0, act_all.at[y], x)
    spread(ys_sem, yr_sem, 0, act_all, y, y_peer)

    def second_conv(b):
        rows = rows_of(b, BLOCK)
        pre[rows] = dot(mid[rows], wmid_ref[...])

    each(second_conv, 4)
    centre(inv2)

    def second_act(f):
        unit = pre[rows_of(f)] * inv2[one(f)]
        value, slope = mish_both(unit)
        unit2[rows_of(f)] = unit
        slope2[rows_of(f)] = slope
        block[rows_of(f)] = (value + res[rows_of(f)]).astype(bf16)

    each(second_act)

    def errors(f, total):
        rows = rows_of(f)
        error = dot(block[rows], wout_ref[...]) - noise_ref[rows]
        d_pred[rows] = (adv_ref[one(f)] * error * (2.0 / 896.0)).astype(bf16)
        return total + error * error

    err = lax.fori_loop(0, FLATS, errors, jnp.zeros((STEPS, 128), f32), unroll=4)
    err_sum = jnp.sum(err) * (1.0 / 896.0)

    def from_pred(b):
        rows = rows_of(b, BLOCK)
        out = dot(d_pred[rows], wout_t_ref[...])
        pre[rows] = out
        d_block[rows] = out.astype(bf16)

    each(from_pred, 4)

    def act_back(scale, unit, slope):
        def totals(f):
            grad = scale(f) * slope[rows_of(f)]
            pre[rows_of(f)] = grad
            sum1[one(f)] = jnp.sum(grad, axis=0, keepdims=True)
            sum2[one(f)] = jnp.sum(grad * unit[rows_of(f)], axis=0, keepdims=True)

        each(totals)
        means = group_mean(jnp.concatenate([sum1[...], sum2[...]], axis=0))
        mean1[...] = means[0:FLATS]
        mean2[...] = means[FLATS:]

    act_back(lambda f: pre[rows_of(f)], unit2, slope2)

    def second_back(f):
        grad = inv2[one(f)] * (pre[rows_of(f)] - mean1[one(f)] - unit2[rows_of(f)] * mean2[one(f)])
        rounded = grad.astype(bf16)
        d_second[rows_of(f)] = rounded
        pad[f, 8:72] = rounded.astype(f32)
        for tap in range(5):
            back[rows_of(f), C * tap : C * (tap + 1)] = pad[f, 10 - tap : 74 - tap].astype(bf16)

    each(second_back)

    def over_rows(left, right):
        return lax.dot_general(left, right, (((0,), (0,)), ((), ())), preferred_element_type=f32)

    for tap in range(5):
        grad = over_rows(d_second[...], mid[:, C * tap : C * (tap + 1)]).astype(bf16)
        for s in range(4):
            for half in range(2):
                begin = 64 * (2 * tap + half)
                grads_a[s, begin : begin + 64] = grad[64 * s : 64 * (s + 1), 128 * half : 128 * (half + 1)]

    def ours(rows):
        return pl.ds(pl.multiple_of(core * rows, 16), rows)

    def theirs(rows):
        return pl.ds(pl.multiple_of(sibling * rows, 16), rows)

    def to_segments(number, grads, landed, out, slots, rows):
        out[...] = (grads[:, ours(rows), :].astype(f32) + landed[...].astype(f32)).astype(bf16)
        scatter(zs_sem, zr_sem, number, out, slots, seg, z_peer)
        slots[seg] = out[seg]

    def to_row(number, got, out, slots):
        out[...] = added(got).astype(bf16).reshape(out.shape)
        scatter(xs_sem, xr_sem, number, out, slots, x, x_peer)
        slots[x] = out[x]

    def to_column(number, got, slots):
        slots[y] = added(got).astype(bf16)
        spread(ys_sem, yr_sem, number, slots, y, y_peer)

    to_sibling(1, grads_a.at[:, theirs(ROWS_A), :], mp_a)

    def mid_back(b):
        rows = rows_of(b, BLOCK)
        pre[rows] = sum(
            lax.dot_general(
                back[rows, C * tap : C * (tap + 1)], wmid_ref[C * tap : C * (tap + 1)], (((1,), (1,)), ((), ())),
                preferred_element_type=f32,
            )
            for tap in range(5)
        )

    each(mid_back, 4)

    arrive(mp_a, mr_sem.at[1])
    to_segments(1, grads_a, mp_a, zo_a, zi_a, ROWS_A)

    def film_back(f):
        grad = pre[rows_of(f)]
        d_film[one(f), 0:C] = jnp.sum(grad * act1[rows_of(f)], axis=0, keepdims=True)
        d_film[one(f), C:] = jnp.sum(grad, axis=0, keepdims=True)

    each(film_back)
    film_ref[...] = jnp.zeros_like(film_ref)
    film_ref[0:1] = jnp.sum(d_film[0:8], axis=0, keepdims=True)
    film_ref[1:2] = jnp.sum(d_film[8:16], axis=0, keepdims=True)

    to_sibling(0, film_ref, film_sib)

    act_back(lambda f: pre[rows_of(f)] * film[one(f), 0:C], unit1, slope1)

    arrive(film_sib, mr_sem.at[0])
    film_out[...] = jnp.zeros_like(film_out)
    for s in range(SIDE):
        film_out[s, 0:2] = film_ref[0:2, 128 * s : 128 * (s + 1)]
        film_out[s, 2:4] = film_sib[0:2, 128 * s : 128 * (s + 1)]
    scatter(zs_sem, zr_sem, 0, film_out, film_z, seg, z_peer)
    film_z[seg] = film_out[seg]

    def first_back(f):
        grad = inv1[one(f)] * (pre[rows_of(f)] - mean1[one(f)] - unit1[rows_of(f)] * mean2[one(f)])
        d_first[rows_of(f)] = grad.astype(bf16)

    each(first_back)

    lane = lax.broadcasted_iota(jnp.int32, (C, 128), 1)
    inner = over_rows(d_first[...], cols[...])
    skip = over_rows(d_block[...], cols[...])
    out = pltpu.roll(over_rows(block[...], d_pred[...]), 84, 1)
    joined = jnp.where(lane < 70, inner, jnp.where(lane < 84, skip, jnp.where(lane < 98, out, err_sum))).astype(bf16)
    timed = over_rows(time_ref[...], d_film[...].astype(bf16)).astype(bf16)
    for s in range(4):
        grads_b[s, 0:64] = joined[64 * s : 64 * (s + 1)]
        grads_b[s, 64:320] = timed[:, 128 * s : 128 * (s + 1)]
        grads_b[s, 320:384] = jnp.zeros((64, 128), bf16)
    to_sibling(2, grads_b.at[:, theirs(ROWS_B), :], mp_b)

    gathered(zr_sem, 1, zi_a, seg)
    to_row(2, zi_a, xo_a, xi_a)
    arrive(mp_b, mr_sem.at[2])
    to_segments(2, grads_b, mp_b, zo_b, zi_b, ROWS_B)

    gathered(zr_sem, 0, film_z, seg)
    pairs = [film_z[j, 0:2] for j in range(MICRO)] + [film_z[j, 2:4] for j in range(MICRO)]
    film_all[y, x] = jnp.concatenate(pairs, axis=0).astype(bf16)
    spread(xs_sem, xr_sem, 1, film_all.at[y], x, x_peer)

    gathered(xr_sem, 2, xi_a, x)
    to_column(2, xi_a, yi_a)
    gathered(zr_sem, 2, zi_b, seg)
    xi_b[x] = added(zi_b).astype(bf16)
    spread(xs_sem, xr_sem, 3, xi_b, x, x_peer)
    gathered(xr_sem, 1, film_all.at[y], x)
    spread(ys_sem, yr_sem, 1, film_all, y, y_peer)
    gathered(yr_sem, 2, yi_a, y)
    full_a[core, x] = added(yi_a).astype(bf16)
    spread(xs_sem, xr_sem, 4, full_a.at[core], x, x_peer)
    gathered(xr_sem, 3, xi_b, x)
    to_column(3, xi_b, yi_b)

    low = jnp.where(core == 0, film_ref[0:2], film_sib[0:2])
    high = jnp.where(core == 0, film_sib[0:2], film_ref[0:2])
    film_rows = jnp.concatenate([low, high, jnp.zeros((12, 512), jnp.float32)], axis=0).astype(jnp.bfloat16)
    own_cond, sib_cond = cond_ref[seg, 0:2, here], cond_sib[seg, 0:2]
    cond_rows = jnp.concatenate(
        [jnp.where(core == 0, own_cond, sib_cond), jnp.where(core == 0, sib_cond, own_cond)], axis=0
    )
    back = lax.dot_general(film_rows, wc_ref[...], (((1,), (1,)), ((), ())), preferred_element_type=jnp.float32)
    gcond_ref[...] = back[0:4] * mish_slope(cond_rows)

    gathered(xr_sem, 4, full_a.at[core], x)
    to_sibling(4, full_a.at[core], full_a.at[core])
    gathered(yr_sem, 3, yi_b, y)
    full_b[core] = added(yi_b).astype(bf16)
    to_sibling(5, full_b.at[core], full_b.at[core])
    gathered(yr_sem, 0, act_all, y)
    gathered(yr_sem, 1, film_all, y)
    arrive(full_a.at[sibling], mr_sem.at[4])
    arrive(full_b.at[sibling], mr_sem.at[5])
    for sent_copy in started:
        sent_copy.wait_send()


def unpack_kernel(full_a, full_b, act_all, film_all, back_ref, gin, gmid, gres, gout, gtime, gwc, gcond, loss):
    f32 = jnp.float32
    flat_a = full_a[...].astype(f32).reshape(640, 128)
    for q in range(10):
        gmid[:, 128 * q : 128 * (q + 1)] = flat_a[64 * q : 64 * (q + 1)]
    flat_b = full_b[...].astype(f32).reshape(384, 128)
    joined = flat_b[0:64]
    turned = joined.T
    gin[...] = joined[:, 0:70]
    gres[...] = turned[70:84]
    gout[...] = turned[84:98]
    loss[...] = joined[0:1, 98:99] * (1.0 / 2048.0)
    gtime[...] = flat_b[64:320]
    gcond[...] = back_ref[...]
    gwc[...] = lax.dot_general(
        act_all[...].reshape(256, HALF), film_all[...].reshape(256, 128), (((0,), (0,)), ((), ())),
        preferred_element_type=f32,
    )


def step_tables():
    table = schedule()
    roots = np.zeros((8, 128))
    roots[0, :TSTEPS], roots[1, :TSTEPS] = np.sqrt(table), np.sqrt(1.0 - table)
    half = C // 2
    angles = np.arange(TSTEPS)[:, None] * np.exp(-math.log(10000.0) * np.arange(half) / (half - 1))[None]
    embedded = np.concatenate([np.sin(angles), np.cos(angles)], axis=1)
    times = np.zeros((128, C))
    times[:TSTEPS] = embedded * np.tanh(np.log1p(np.exp(embedded)))
    return jnp.asarray(roots, jnp.float32), jnp.asarray(times, jnp.float32).astype(jnp.bfloat16)


def finish(cond, w_cond_full, w_cond, noise, actions, tsteps, advantage, w_in, w_res, w_mid, w_out, w_time):
    bf16, f32 = jnp.bfloat16, jnp.float32
    roots, times = step_tables()
    vmem = pl.BlockSpec(memory_space=pltpu.VMEM)
    flat_rows = FLATS * STEPS
    big, small = pltpu.VMEM((flat_rows, C), f32), pltpu.VMEM((FLATS, C), f32)
    big16 = pltpu.VMEM((flat_rows, C), bf16)
    rows_a, rows_b = pltpu.VMEM((SIDE, ROWS_A, 128), bf16), pltpu.VMEM((SIDE, ROWS_B, 128), bf16)
    part_a = pltpu.VMEM((SIDE, ROWS_A // SIDE, 128), bf16)
    dma = pltpu.SemaphoreType.DMA
    return pl.pallas_call(
        finish_kernel,
        out_shape=(
            jax.ShapeDtypeStruct((2, SIDE, ROWS_A // SIDE, 128), bf16),
            jax.ShapeDtypeStruct((2, ROWS_B, 128), bf16),
            jax.ShapeDtypeStruct((SIDE, SIDE, 16, HALF), bf16),
            jax.ShapeDtypeStruct((SIDE, SIDE, 16, 128), bf16),
            jax.ShapeDtypeStruct((4, HALF), f32),
        ),
        in_specs=[vmem] * 14,
        out_specs=(vmem,) * 5,
        scratch_shapes=[
            pltpu.VMEM((flat_rows, 128), f32),
            pltpu.VMEM((2, STEPS, 128), f32),
            pltpu.VMEM((FLATS, 128), f32),
            pltpu.VMEM((FLATS, 128), f32),
            pltpu.VMEM((FLATS, 128), f32),
            pltpu.VMEM((FLATS, C), bf16),
            pltpu.VMEM((128, C), f32),
            pltpu.VMEM((128, C), f32),
            pltpu.VMEM((128, C), f32),
            pltpu.VMEM((128, C), bf16),
            pltpu.VMEM((128, C), bf16),
            pltpu.VMEM((C, 128), bf16),
            pltpu.VMEM((128, C), bf16),
            pltpu.VMEM((FLATS, 80, 128), f32),
            pltpu.VMEM((flat_rows, 128), bf16),
            pltpu.VMEM((FLATS, 80, C), f32),
            pltpu.VMEM((flat_rows, 5 * C), bf16),
            pltpu.VMEM((flat_rows, 5 * C), bf16),
            big, big, big, big, big, big, big,
            big16, big16,
            pltpu.VMEM((flat_rows, 128), bf16),
            big16, big16,
            pltpu.VMEM((FLATS, 2 * C), f32),
            pltpu.VMEM((FLATS, 2 * C), f32),
            small, small, small, small, small, small,
            pltpu.VMEM((MICRO, 8, HALF), f32),
            pltpu.VMEM((8, 512), f32),
            pltpu.VMEM((8, 512), f32),
            pltpu.VMEM((SIDE, 8, 128), f32),
            pltpu.VMEM((SIDE, 8, 128), f32),
            pltpu.VMEM((SIDE, 2 * ROWS_A, 128), bf16),
            pltpu.VMEM((SIDE, 2 * ROWS_B, 128), bf16),
            rows_a, rows_b, rows_a, rows_b, rows_a, rows_b,
            part_a, part_a, part_a, rows_b, rows_b,
            dma((6,)), dma((6,)),
            dma((3, 3)), dma((3, 3)),
            dma((5, 3)), dma((5, 3)),
            dma((4, 3)), dma((4, 3)),
        ],
        compiler_params=pltpu.CompilerParams(
            collective_id=1, has_side_effects=True, vmem_limit_bytes=48 * 2**20
        ),
    )(
        cond, w_cond_full, w_cond, noise, actions, tsteps, advantage, roots, times, w_in, w_res, w_mid, w_out, w_time
    )


def unpack(*arrays):
    f32 = jnp.float32
    vmem = pl.BlockSpec(memory_space=pltpu.VMEM)
    shapes = ((64, 70), (64, 1280), (14, 64), (14, 64), (256, 128), (HALF, 128), (4, HALF), (1, 1))
    return pl.pallas_call(
        unpack_kernel,
        out_shape=tuple(jax.ShapeDtypeStruct(shape, f32) for shape in shapes),
        in_specs=[vmem] * 5,
        out_specs=(vmem,) * 8,
        compiler_params=pltpu.CompilerParams(vmem_limit_bytes=32 * 2**20),
    )(*arrays)


def body(
    trunk_in, norm_gain, w_gate, w_up, w_down, w_cond, w_time, w_in, w_mid, w_res, w_out,
    tsteps, advantage, actions, noise,
):
    cond_all, w_cond_full = trunk(trunk_in, norm_gain, w_gate[0], w_up[0], w_down[0].T, w_cond)
    begin = 4 * lax.axis_index("segment") + 2 * lax.axis_index("mp")

    def own(values):
        return lax.dynamic_slice_in_dim(values, begin, 2, 0)

    parts = finish(
        cond_all, w_cond_full, w_cond, own(noise).reshape(FLATS * STEPS, 14), own(actions), tsteps.T, advantage.T,
        w_in, w_res, w_mid, w_out.T, w_time,
    )
    gin, gmid, gres, gout, gtime, gwc, gcond, loss = unpack(*parts)
    return gin.T, gmid.T, gres, gout.T, gtime, gwc, gcond, loss.reshape(1)


def solution(mesh):
    in_specs = (
        P("dp", "mp"),
        P("segment", None),
        P("segment", "dp", "mp"),
        P("segment", "dp", "mp"),
        P("segment", "mp", "dp"),
        P("mp", None),
        P(),
        P(),
        P(),
        P(),
        P(),
        P("dp", None),
        P("dp", None),
        P("dp", None, None),
        P("dp", None, None, None),
    )
    out_specs = (
        P(None, "segment"),
        P(None, "segment"),
        P(None, "segment"),
        P("segment", None),
        P(None, "segment"),
        P("mp", "segment"),
        P(("dp", "segment"), "mp"),
        P(),
    )
    return jax.shard_map(body, mesh=mesh, in_specs=in_specs, out_specs=out_specs, check_vma=False)
```

```python
import functools
import math

import jax
import jax.numpy as jnp
import numpy as np
from jax import lax
from jax.experimental import pallas as pl
from jax.experimental.pallas import tpu as pltpu
from jax.sharding import PartitionSpec as P

MESH = pl.DeviceIdType.MESH
TSTEPS = 100
SIDE = 4
MICRO = 4
ROWS = 32
BATCHES = 2
OWN = 64
PART = 512
PARTS = 5
D = 2560
HALF = 1280
FH = 1792
SHARD = 160
CUT = 80
TILE = 256


def schedule():
    grid = np.arange(TSTEPS + 1, dtype=np.float64) / TSTEPS
    curve = np.cos((grid + 0.008) / 1.008 * math.pi / 2.0) ** 2
    betas = np.minimum(1.0 - curve[1:] / curve[:-1], 0.999)
    return np.cumprod(1.0 - betas)


def trunk_kernel(
    x_ref, gain_ref, wg_ref, wu_ref, wd_ref, wc_ref,
    cond_ref, wcond_ref,
    weights, first, arrived, leaving, normed, hidden, partial, share, other,
    own_sem, gs_sem, gr_sem, ms_sem, mr_sem, ps_sem, pr_sem, zs_sem, zr_sem, cs_sem, cr_sem,
):
    dp, seg, core = lax.axis_index("dp"), lax.axis_index("segment"), lax.axis_index("mp")
    y, x = dp // SIDE, dp % SIDE
    sibling = 1 - core

    def at(axis, delta):
        if axis == "x":
            return y * SIDE + (x + delta + SIDE) % SIDE
        return ((y + delta + SIDE) % SIDE) * SIDE + x

    barrier = pltpu.get_barrier_semaphore()
    for axis in ("x", "y"):
        for delta in (1, -1):
            pl.semaphore_signal(barrier, inc=1, device_id={"dp": at(axis, delta)}, device_id_type=MESH)
    pl.semaphore_signal(barrier, inc=1, device_id={"mp": sibling}, device_id_type=MESH)
    for step in range(1, 4):
        pl.semaphore_signal(barrier, inc=1, device_id={"segment": (seg + step) % 4}, device_id_type=MESH)
    pl.semaphore_wait(barrier, 8)

    sources = (wg_ref, wu_ref, wd_ref)
    chunks = [(which, part) for which in range(3) for part in range(2)]

    def spot(which, part, px, py, begin=0, size=CUT):
        row = (py * SIDE + px) * SHARD + part * CUT + begin
        return weights.at[which, pl.ds(pl.multiple_of(row, 16), size), :]

    def place(chunk, p_off, q_off, begin=0, size=CUT):
        which, part = chunk
        dx, dy = (p_off, q_off) if part == 0 else (q_off, p_off)
        return spot(which, part, (x + dx + SIDE) % SIDE, (y + dy + SIDE) % SIDE, begin, size)

    def axes(chunk):
        return ("x", "y") if chunk[1] == 0 else ("y", "x")

    def piece(chunk, kind):
        return (0, 48) if kind == 0 else (48, 32)

    def make(chunk, number, src, dst, axis, delta):
        q = chunks.index(chunk)
        return pltpu.make_async_remote_copy(
            src_ref=src, dst_ref=dst, send_sem=gs_sem.at[q, number], recv_sem=gr_sem.at[q, number],
            device_id={"dp": at(axis, delta)}, device_id_type=MESH,
        )

    OFF = (0, -1, 1, 2)

    def spec(chunk, number):
        p_axis, q_axis = axes(chunk)
        if number < 4:
            delta = 1 if number % 2 == 0 else -1
            if number < 2:
                return p_axis, delta, 0, 0, 0, CUT
            begin, size = piece(chunk, number - 2)
            return p_axis, delta, -delta, 0, begin, size
        slot, kind = divmod(number - 4, 4)
        delta = 1 if kind % 2 == 0 else -1
        if kind < 2:
            return q_axis, delta, OFF[slot], 0, 0, CUT
        begin, size = piece(chunk, kind - 2)
        return q_axis, delta, OFF[slot], -delta, begin, size

    def source_of(chunk, number):
        _, _, p_off, q_off, begin, size = spec(chunk, number)
        if p_off == 0 and q_off == 0:
            return sources[chunk[0]].at[pl.ds(chunk[1] * CUT + begin, size), :]
        return place(chunk, p_off, q_off, begin, size)

    def send(chunk, number):
        axis, delta, p_off, q_off, begin, size = spec(chunk, number)
        make(chunk, number, source_of(chunk, number), place(chunk, p_off, q_off, begin, size), axis, delta).start()

    def receive(chunk, number):
        axis, delta, p_off, q_off, begin, size = spec(chunk, number)
        if number < 4:
            p_off = p_off - delta
        else:
            q_off = q_off - delta
        spot_here = place(chunk, p_off, q_off, begin, size)
        make(chunk, number, spot_here, spot_here, axis, delta).wait_recv()

    def sent(chunk, number):
        axis, delta, p_off, q_off, begin, size = spec(chunk, number)
        make(chunk, number, source_of(chunk, number), place(chunk, p_off, q_off, begin, size), axis, delta).wait_send()

    own = []
    for chunk in chunks:
        for number in (0, 1, 4, 5):
            send(chunk, number)
    for which in range(3):
        keep = pltpu.make_async_copy(
            sources[which], weights.at[which, pl.ds(pl.multiple_of(dp * SHARD, 16), SHARD), :], own_sem.at[which]
        )
        keep.start()
        own.append(keep)

    def sibling_copy(number, src, dst):
        return pltpu.make_async_remote_copy(
            src_ref=src, dst_ref=dst, send_sem=ms_sem.at[number], recv_sem=mr_sem.at[number],
            device_id={"mp": sibling}, device_id_type=MESH,
        )

    here = pl.ds(pl.multiple_of(core * HALF, 128), HALF)
    there = pl.ds(pl.multiple_of(sibling * HALF, 128), HALF)
    def slot_of(j, features):
        return first.at[j // 2, pl.ds(32 * (j % 2), ROWS), features]

    for j in range(MICRO):
        src = x_ref.at[pl.ds(pl.multiple_of(64 * j + 32 * sibling, 16), ROWS), :]
        sibling_copy(j, src, slot_of(j, here)).start()
        kept = pltpu.make_async_copy(
            x_ref.at[pl.ds(pl.multiple_of(64 * j + 32 * core, 16), ROWS), :], slot_of(j, here), own_sem.at[3 + j]
        )
        kept.start()
        own.append(kept)
    here_rows = wcond_ref.at[pl.ds(pl.multiple_of(core * HALF, 16), HALF), :]
    there_rows = wcond_ref.at[pl.ds(pl.multiple_of(sibling * HALF, 16), HALF), :]
    sibling_copy(4, wc_ref, here_rows).start()
    kept = pltpu.make_async_copy(wc_ref, here_rows, own_sem.at[7])
    kept.start()
    own.append(kept)

    for chunk in chunks:
        for number in (0, 1):
            receive(chunk, number)
            send(chunk, 2 + number)
            slot = 1 + number
            send(chunk, 4 + 4 * slot)
            send(chunk, 5 + 4 * slot)
        for kind in (0, 1):
            receive(chunk, 4 + kind)
            send(chunk, 6 + kind)
    for chunk in chunks:
        for number in (2, 3):
            receive(chunk, number)
        send(chunk, 16)
        send(chunk, 17)
        for slot in (1, 2):
            for kind in (0, 1):
                receive(chunk, 4 + 4 * slot + kind)
                send(chunk, 6 + 4 * slot + kind)
    for chunk in chunks:
        for kind in (0, 1):
            receive(chunk, 16 + kind)
            send(chunk, 18 + kind)
    for j in range(MICRO):
        sibling_copy(j, slot_of(j, there), slot_of(j, there)).wait_recv()
    for keep in own[3:7]:
        keep.wait()

    def finish_gather():
        for chunk in chunks:
            for slot in range(4):
                for kind in (2, 3):
                    receive(chunk, 4 + 4 * slot + kind)
        for keep in own[:3] + own[7:]:
            keep.wait()

    def z_copy(b, g):
        return pltpu.make_async_remote_copy(
            src_ref=leaving.at[b, g], dst_ref=arrived.at[b, g], send_sem=zs_sem.at[b, g], recv_sem=zr_sem.at[b, g],
            device_id={"segment": (seg + 1) % 4}, device_id_type=MESH,
        )

    def share_copy(b, g):
        return pltpu.make_async_remote_copy(
            src_ref=share.at[b, g], dst_ref=other.at[b, g], send_sem=ps_sem.at[b, g], recv_sem=pr_sem.at[b, g],
            device_id={"mp": sibling}, device_id_type=MESH,
        )

    def normed_copy(b):
        return sibling_copy(5 + b, normed.at[b, pl.ds(0, OWN)], normed.at[b, pl.ds(OWN, OWN)])

    def cond_copy(j, target):
        return pltpu.make_async_remote_copy(
            src_ref=cond_ref.at[j], dst_ref=cond_ref.at[j], send_sem=cs_sem.at[j, target], recv_sem=cr_sem.at[j],
            device_id={"segment": target}, device_id_type=MESH,
        )

    def columns_of(g):
        return slice(PART * g, PART * (g + 1))

    def normalize(b):
        states = [arrived[b, g].astype(jnp.float32) for g in range(PARTS)]
        total = sum(jnp.sum(state * state, axis=1, keepdims=True) for state in states)
        factor = lax.rsqrt(total * (1.0 / D) + 1e-05)
        for g in range(PARTS):
            gain = gain_ref[:, columns_of(g)].astype(jnp.float32)
            normed[b, 0:OWN, columns_of(g)] = (states[g] * factor * gain).astype(jnp.bfloat16)
        normed_copy(b).start()

    def batch(b, carry):
        @pl.when(seg > 0)
        def _():
            for g in range(PARTS):
                z_copy(b, g).wait_recv()
            normalize(b)

        normed_copy(b).wait_recv()
        for n in range(FH // TILE):
            cols = slice(n * TILE, (n + 1) * TILE)
            rows = normed[b]
            gate = jnp.dot(rows, weights[0, :, cols], preferred_element_type=jnp.float32)
            lift = jnp.dot(rows, weights[1, :, cols], preferred_element_type=jnp.float32)
            hidden[:, cols] = (gate / (1.0 + jnp.exp(-gate)) * lift).astype(jnp.bfloat16)

        def finish(g):
            share_copy(b, g).wait_recv()
            whole = partial[g] + other[b, g].astype(jnp.float32)
            leaving[b, g] = (arrived[b, g].astype(jnp.float32) + whole).astype(jnp.bfloat16)

            @pl.when(seg < 3)
            def _():
                z_copy(b, g).start()

        for g in range(PARTS):
            for half in range(2):
                part = slice(TILE * half, TILE * (half + 1))
                out = lax.dot_general(
                    hidden[...], weights[2, PART * g + TILE * half : PART * g + TILE * (half + 1), :],
                    (((1,), (1,)), ((), ())), preferred_element_type=jnp.float32,
                )
                partial[g, :, part] = out[0:OWN]
                share[b, g, :, part] = out[OWN:].astype(jnp.bfloat16)
            share_copy(b, g).start()
            if g > 0:
                finish(g - 1)
        finish(PARTS - 1)

        @pl.when(seg == 3)
        def _():
            for half in range(2):
                for g in range(PARTS):
                    rows = leaving[b, g, ROWS * half : ROWS * (half + 1)].astype(jnp.float32)
                    mean = jnp.mean(rows.reshape(2, 16, PART), axis=1)
                    cond_ref[2 * b + half, 0:2, columns_of(g)] = mean.astype(jnp.bfloat16).astype(jnp.float32)
                for target in range(3):
                    cond_copy(2 * b + half, target).start()

        return carry

    @pl.when(seg == 0)
    def _():
        for b in range(BATCHES):
            for g in range(PARTS):
                arrived[b, g] = first[b, :, columns_of(g)]
            normalize(b)

    finish_gather()
    lax.fori_loop(0, BATCHES, batch, 0)

    for chunk in chunks:
        for number in range(20):
            sent(chunk, number)
    for b in range(BATCHES):
        normed_copy(b).wait_send()
        for g in range(PARTS):
            share_copy(b, g).wait_send()

    @pl.when(seg < 3)
    def _():
        for b in range(BATCHES):
            for g in range(PARTS):
                z_copy(b, g).wait_send()

    for j in range(MICRO):
        sibling_copy(j, x_ref.at[pl.ds(0, ROWS), :], slot_of(j, there)).wait_send()

        @pl.when(seg < 3)
        def _(j=j):
            cond_copy(j, 0).wait_recv()

        @pl.when(seg == 3)
        def _(j=j):
            for target in range(3):
                cond_copy(j, target).wait_send()

    last = sibling_copy(4, wc_ref, there_rows)
    last.wait_recv()
    last.wait_send()


def trunk(trunk_in, norm_gain, w_gate, w_up, w_down_t, w_cond):
    anywhere = pl.BlockSpec(memory_space=pl.ANY)
    vmem = pl.BlockSpec(memory_space=pltpu.VMEM)
    dma = pltpu.SemaphoreType.DMA
    bf16 = jnp.bfloat16
    return pl.pallas_call(
        trunk_kernel,
        out_shape=(
            jax.ShapeDtypeStruct((MICRO, 2, D), jnp.float32),
            jax.ShapeDtypeStruct((D, w_cond.shape[1]), bf16),
        ),
        in_specs=[anywhere, vmem, anywhere, anywhere, anywhere, anywhere],
        out_specs=(vmem, anywhere),
        scratch_shapes=[
            pltpu.VMEM((3, D, FH), bf16),
            pltpu.VMEM((BATCHES, OWN, D), bf16),
            pltpu.VMEM((BATCHES, PARTS, OWN, PART), bf16),
            pltpu.VMEM((BATCHES, PARTS, OWN, PART), bf16),
            pltpu.VMEM((BATCHES, 2 * OWN, D), bf16),
            pltpu.VMEM((2 * OWN, FH), bf16),
            pltpu.VMEM((PARTS, OWN, PART), jnp.float32),
            pltpu.VMEM((BATCHES, PARTS, OWN, PART), bf16),
            pltpu.VMEM((BATCHES, PARTS, OWN, PART), bf16),
            dma((8,)),
            dma((6, 20)),
            dma((6, 20)),
            dma((7,)),
            dma((7,)),
            dma((BATCHES, PARTS)),
            dma((BATCHES, PARTS)),
            dma((BATCHES, PARTS)),
            dma((BATCHES, PARTS)),
            dma((MICRO, 3)),
            dma((MICRO,)),
        ],
        compiler_params=pltpu.CompilerParams(
            collective_id=0, has_side_effects=True, vmem_limit_bytes=52 * 2**20
        ),
    )(trunk_in, norm_gain, w_gate, w_up, w_down_t, w_cond)


def mish_parts(values):
    small = jnp.exp(-jnp.abs(values))
    right = values > 0
    top = jnp.where(right, 1.0 + 2.0 * small, small * (small + 2.0))
    rest = jnp.where(right, 2.0 * small * small, 2.0)
    return small, right, top, rest


def mish_value(values):
    _, _, top, rest = mish_parts(values)
    return values * (top / (top + rest))


def mish_slope(values):
    small, right, top, rest = mish_parts(values)
    inverse = 1.0 / (top + rest)
    logistic = jnp.where(right, 1.0, small) / (1.0 + small)
    return top * inverse + values * logistic * (rest * (2.0 * top + rest)) * (inverse * inverse)


FLATS = 16
STEPS = 64
C = 256
BLOCK = 256
ROWS_A = 320
ROWS_B = 192


def finish_kernel(
    cond_ref, wcond_ref, wc_ref, noise_in, actions_in, tsteps_ref, advantage_ref, roots_ref, table_ref,
    win_in, wres_in, wmid_ref, wout_in, wtime_ref,
    full_a, full_b, act_all, film_all, gcond_ref,
    noise_ref, actions_ref, keep_ref, blend_ref, adv_ref, time_ref, wide_in, wide_res, wide_out, win_ref, wres_ref,
    wout_ref, wout_t_ref, npad, cols, pad, mid, back, pre, res, unit1, act1, slope1, unit2, slope2, block, d_block, d_pred,
    d_second, d_first, film, d_film, sum1, sum2, inv1, inv2, mean1, mean2,
    cond_sib, film_ref, film_sib, film_out, film_z,
    grads_a, grads_b, mp_a, mp_b, zo_a, zo_b, zi_a, zi_b, xo_a, xi_a, yi_a, xi_b, yi_b,
    ms_sem, mr_sem, zs_sem, zr_sem, xs_sem, xr_sem, ys_sem, yr_sem,
):
    dp, seg, core = lax.axis_index("dp"), lax.axis_index("segment"), lax.axis_index("mp")
    y, x = dp // SIDE, dp % SIDE
    sibling = 1 - core

    def x_peer(step):
        return {"dp": y * SIDE + (x + step) % SIDE}

    def y_peer(step):
        return {"dp": ((y + step) % SIDE) * SIDE + x}

    def z_peer(step):
        return {"segment": (seg + step) % SIDE}

    barrier = pltpu.get_barrier_semaphore()
    pl.semaphore_signal(barrier, inc=1, device_id={"mp": sibling}, device_id_type=MESH)
    for step in range(1, SIDE):
        for peer in (x_peer, y_peer, z_peer):
            pl.semaphore_signal(barrier, inc=1, device_id=peer(step), device_id_type=MESH)

    def copy(src, dst, out_sem, in_sem, peer):
        return pltpu.make_async_remote_copy(
            src_ref=src, dst_ref=dst, send_sem=out_sem, recv_sem=in_sem, device_id=peer, device_id_type=MESH
        )

    started = []

    def launch(src, dst, out_sem, in_sem, peer):
        one = copy(src, dst, out_sem, in_sem, peer)
        one.start()
        started.append(one)

    def arrive(dst, in_sem):
        copy(dst, dst, ms_sem.at[0], in_sem, {"mp": sibling}).wait_recv()

    def to_sibling(number, src, dst):
        launch(src, dst, ms_sem.at[number], mr_sem.at[number], {"mp": sibling})

    def scatter(out_sem, in_sem, number, src, dst, me, peer):
        for step in range(1, SIDE):
            launch(
                src.at[(me + step) % SIDE], dst.at[me], out_sem.at[number, step - 1], in_sem.at[number, step - 1], peer(step)
            )

    def spread(out_sem, in_sem, number, slots, me, peer):
        for step in range(1, SIDE):
            launch(slots.at[me], slots.at[me], out_sem.at[number, step - 1], in_sem.at[number, step - 1], peer(step))

    def gathered(in_sem, number, slots, me):
        for step in range(1, SIDE):
            arrive(slots.at[(me - step + SIDE) % SIDE], in_sem.at[number, step - 1])

    def added(slots):
        pieces = [slots[k].astype(jnp.float32) for k in range(SIDE)]
        return (pieces[0] + pieces[1]) + (pieces[2] + pieces[3])

    here = pl.ds(pl.multiple_of(core * HALF, 128), HALF)
    there = pl.ds(pl.multiple_of(sibling * HALF, 128), HALF)
    bf16, f32 = jnp.bfloat16, jnp.float32

    def rows_of(f, size=STEPS):
        return pl.ds(pl.multiple_of(f * size, size), size)

    def one(f):
        return pl.ds(f, 1)

    def each(body, count=FLATS):
        def step(f, carry):
            body(f)
            return carry

        lax.fori_loop(0, count, step, 0, unroll=4 if count == FLATS else 2)

    lanes = lax.broadcasted_iota(jnp.int32, (C, C), 1)
    row_ids = lax.broadcasted_iota(jnp.int32, (C, C), 0)
    same = jnp.where(lanes // 32 == row_ids // 32, 1.0 / 2048.0, 0.0).astype(bf16)

    def group_mean(values):
        high = values.astype(bf16)
        rest = values - high.astype(f32)
        middle = rest.astype(bf16)
        low = (rest - middle.astype(f32)).astype(bf16)
        count = values.shape[0]
        sums = jnp.dot(jnp.concatenate([high, middle, low], axis=0), same, preferred_element_type=f32)
        return sums[0:count] + (sums[count : 2 * count] + sums[2 * count : 3 * count])

    def dot(left, right):
        return jnp.dot(left, right, preferred_element_type=f32)

    begin = 4 * seg + 2 * core
    sample_at = lax.broadcasted_iota(jnp.int32, (8, 16), 1)

    def column(ref):
        pieces = []
        for sample in range(2):
            chosen = jnp.where(sample_at == begin + sample, ref[...].astype(f32), 0.0)
            pieces.append(jnp.sum(chosen, axis=1, keepdims=True))
        return jnp.broadcast_to(jnp.concatenate(pieces, axis=0), (FLATS, 128))

    steps_at = column(tsteps_ref)
    lane_at = lax.broadcasted_iota(jnp.int32, (FLATS, 128), 1).astype(f32)
    picked = jnp.where(steps_at == lane_at, 1.0, 0.0)
    keep_ref[...] = jnp.broadcast_to(jnp.sum(picked * roots_ref[0:1], axis=1, keepdims=True), (FLATS, 128))
    blend_ref[...] = jnp.broadcast_to(jnp.sum(picked * roots_ref[1:2], axis=1, keepdims=True), (FLATS, 128))
    adv_ref[...] = column(advantage_ref)
    time_ref[...] = dot(picked.astype(bf16), table_ref[...]).astype(bf16)
    for sample in range(2):
        actions_ref[sample] = jnp.zeros((STEPS, 128), f32)
        actions_ref[sample, :, 0:14] = actions_in[sample].astype(f32)

    def widen(f):
        noise_ref[rows_of(f)] = jnp.zeros((STEPS, 128), f32)
        noise_ref[rows_of(f), 0:14] = noise_in[rows_of(f)].astype(f32)

    each(widen)
    wide_in[...] = jnp.zeros_like(wide_in)
    wide_in[0:70] = win_in[...].astype(f32)
    win_ref[...] = wide_in[...].astype(bf16)
    wide_res[...] = jnp.zeros_like(wide_res)
    wide_res[70:84] = wres_in[...].astype(f32)
    wres_ref[...] = wide_res[...].astype(bf16)
    wide_out[...] = jnp.zeros_like(wide_out)
    wide_out[0:14] = wout_in[...].astype(f32)
    wout_t_ref[...] = wide_out[...].astype(bf16)
    wout_ref[...] = wide_out[...].T.astype(bf16)

    npad[...] = jnp.zeros_like(npad)
    pad[...] = jnp.zeros_like(pad)

    def make_cols(f):
        noisy = keep_ref[one(f)] * actions_ref[f // 8] + blend_ref[one(f)] * noise_ref[rows_of(f)]
        noisy = noisy.astype(bf16).astype(f32)
        npad[f, 8:72] = noisy
        total = pltpu.roll(noisy, 70, 1)
        for tap in range(5):
            total = total + pltpu.roll(npad[f, 6 + tap : 70 + tap], 14 * tap, 1)
        cols[rows_of(f)] = total.astype(bf16)

    each(make_cols)

    pl.semaphore_wait(barrier, 10)
    to_sibling(3, cond_ref.at[:, :, there], cond_sib)

    time_film = dot(time_ref[...], wtime_ref[...])
    own_pair = jnp.concatenate([mish_value(cond_ref[seg]), jnp.zeros((6, D), f32)], axis=0)
    film_cond = dot(own_pair.astype(bf16), wcond_ref[...])
    top = jnp.broadcast_to(film_cond[0:1], (8, 2 * C))
    low = jnp.broadcast_to(film_cond[1:2], (8, 2 * C))
    film[...] = jnp.concatenate([top, low], axis=0) + time_film

    def first_conv(b):
        rows = rows_of(b, BLOCK)
        out = dot(cols[rows], win_ref[...])
        pre[rows] = out
        res[rows] = dot(cols[rows], wres_ref[...])

    each(first_conv, 4)

    arrive(cond_sib, mr_sem.at[3])
    pairs = [cond_ref[j, 0:2, here] for j in range(MICRO)] + [cond_sib[j, 0:2] for j in range(MICRO)]
    act_all[y, x] = mish_value(jnp.concatenate(pairs, axis=0)).astype(bf16)
    spread(xs_sem, xr_sem, 0, act_all.at[y], x, x_peer)

    def centre(inverse):
        def total(f):
            sum1[one(f)] = jnp.sum(pre[rows_of(f)], axis=0, keepdims=True)

        each(total)
        mean1[...] = group_mean(sum1[...])

        def moved(f):
            left = pre[rows_of(f)] - mean1[one(f)]
            pre[rows_of(f)] = left
            sum1[one(f)] = jnp.sum(left * left, axis=0, keepdims=True)

        each(moved)
        inverse[...] = lax.rsqrt(group_mean(sum1[...]) + 1e-05)

    def mish_both(values):
        small, right, above, rest = mish_parts(values)
        inverse = 1.0 / (above + rest)
        logistic = jnp.where(right, 1.0, small) / (1.0 + small)
        ratio = above * inverse
        value = values * ratio
        return value, ratio + values * logistic * (rest * (2.0 * above + rest)) * (inverse * inverse)

    centre(inv1)

    def first_act(f):
        unit = pre[rows_of(f)] * inv1[one(f)]
        value, slope = mish_both(unit)
        unit1[rows_of(f)] = unit
        act1[rows_of(f)] = value
        slope1[rows_of(f)] = slope
        changed = film[one(f), 0:C] * value + film[one(f), C:]
        pad[f, 8:72] = changed.astype(bf16).astype(f32)
        for tap in range(5):
            mid[rows_of(f), C * tap : C * (tap + 1)] = pad[f, 6 + tap : 70 + tap].astype(bf16)

    each(first_act)

    gathered(xr_sem, 0, act_all.at[y], x)
    spread(ys_sem, yr_sem, 0, act_all, y, y_peer)

    def second_conv(b):
        rows = rows_of(b, BLOCK)
        pre[rows] = dot(mid[rows], wmid_ref[...])

    each(second_conv, 4)
    centre(inv2)

    def second_act(f):
        unit = pre[rows_of(f)] * inv2[one(f)]
        value, slope = mish_both(unit)
        unit2[rows_of(f)] = unit
        slope2[rows_of(f)] = slope
        block[rows_of(f)] = (value + res[rows_of(f)]).astype(bf16)

    each(second_act)

    def errors(f, total):
        rows = rows_of(f)
        error = dot(block[rows], wout_ref[...]) - noise_ref[rows]
        d_pred[rows] = (adv_ref[one(f)] * error * (2.0 / 896.0)).astype(bf16)
        return total + error * error

    err = lax.fori_loop(0, FLATS, errors, jnp.zeros((STEPS, 128), f32), unroll=4)
    err_sum = jnp.sum(err) * (1.0 / 896.0)

    def from_pred(b):
        rows = rows_of(b, BLOCK)
        out = dot(d_pred[rows], wout_t_ref[...])
        pre[rows] = out
        d_block[rows] = out.astype(bf16)

    each(from_pred, 4)

    def act_back(scale, unit, slope):
        def totals(f):
            grad = scale(f) * slope[rows_of(f)]
            pre[rows_of(f)] = grad
            sum1[one(f)] = jnp.sum(grad, axis=0, keepdims=True)
            sum2[one(f)] = jnp.sum(grad * unit[rows_of(f)], axis=0, keepdims=True)

        each(totals)
        means = group_mean(jnp.concatenate([sum1[...], sum2[...]], axis=0))
        mean1[...] = means[0:FLATS]
        mean2[...] = means[FLATS:]

    act_back(lambda f: pre[rows_of(f)], unit2, slope2)

    def second_back(f):
        grad = inv2[one(f)] * (pre[rows_of(f)] - mean1[one(f)] - unit2[rows_of(f)] * mean2[one(f)])
        rounded = grad.astype(bf16)
        d_second[rows_of(f)] = rounded
        pad[f, 8:72] = rounded.astype(f32)
        for tap in range(5):
            back[rows_of(f), C * tap : C * (tap + 1)] = pad[f, 10 - tap : 74 - tap].astype(bf16)

    each(second_back)

    def over_rows(left, right):
        return lax.dot_general(left, right, (((0,), (0,)), ((), ())), preferred_element_type=f32)

    for tap in range(5):
        grad = over_rows(d_second[...], mid[:, C * tap : C * (tap + 1)]).astype(bf16)
        for s in range(4):
            for half in range(2):
                begin = 64 * (2 * tap + half)
                grads_a[s, begin : begin + 64] = grad[64 * s : 64 * (s + 1), 128 * half : 128 * (half + 1)]

    def ours(rows):
        return pl.ds(pl.multiple_of(core * rows, 16), rows)

    def theirs(rows):
        return pl.ds(pl.multiple_of(sibling * rows, 16), rows)

    def to_segments(number, grads, landed, out, slots, rows):
        out[...] = (grads[:, ours(rows), :].astype(f32) + landed[...].astype(f32)).astype(bf16)
        scatter(zs_sem, zr_sem, number, out, slots, seg, z_peer)
        slots[seg] = out[seg]

    def to_row(number, got, out, slots):
        out[...] = added(got).astype(bf16).reshape(out.shape)
        scatter(xs_sem, xr_sem, number, out, slots, x, x_peer)
        slots[x] = out[x]

    def to_column(number, got, slots):
        slots[y] = added(got).astype(bf16)
        spread(ys_sem, yr_sem, number, slots, y, y_peer)

    to_sibling(1, grads_a.at[:, theirs(ROWS_A), :], mp_a)

    def mid_back(b):
        rows = rows_of(b, BLOCK)
        pre[rows] = sum(
            lax.dot_general(
                back[rows, C * tap : C * (tap + 1)], wmid_ref[C * tap : C * (tap + 1)], (((1,), (1,)), ((), ())),
                preferred_element_type=f32,
            )
            for tap in range(5)
        )

    each(mid_back, 4)

    arrive(mp_a, mr_sem.at[1])
    to_segments(1, grads_a, mp_a, zo_a, zi_a, ROWS_A)

    def film_back(f):
        grad = pre[rows_of(f)]
        d_film[one(f), 0:C] = jnp.sum(grad * act1[rows_of(f)], axis=0, keepdims=True)
        d_film[one(f), C:] = jnp.sum(grad, axis=0, keepdims=True)

    each(film_back)
    film_ref[...] = jnp.zeros_like(film_ref)
    film_ref[0:1] = jnp.sum(d_film[0:8], axis=0, keepdims=True)
    film_ref[1:2] = jnp.sum(d_film[8:16], axis=0, keepdims=True)

    to_sibling(0, film_ref, film_sib)

    act_back(lambda f: pre[rows_of(f)] * film[one(f), 0:C], unit1, slope1)

    arrive(film_sib, mr_sem.at[0])
    film_out[...] = jnp.zeros_like(film_out)
    for s in range(SIDE):
        film_out[s, 0:2] = film_ref[0:2, 128 * s : 128 * (s + 1)]
        film_out[s, 2:4] = film_sib[0:2, 128 * s : 128 * (s + 1)]
    scatter(zs_sem, zr_sem, 0, film_out, film_z, seg, z_peer)
    film_z[seg] = film_out[seg]

    def first_back(f):
        grad = inv1[one(f)] * (pre[rows_of(f)] - mean1[one(f)] - unit1[rows_of(f)] * mean2[one(f)])
        d_first[rows_of(f)] = grad.astype(bf16)

    each(first_back)

    lane = lax.broadcasted_iota(jnp.int32, (C, 128), 1)
    inner = over_rows(d_first[...], cols[...])
    skip = over_rows(d_block[...], cols[...])
    out = pltpu.roll(over_rows(block[...], d_pred[...]), 84, 1)
    joined = jnp.where(lane < 70, inner, jnp.where(lane < 84, skip, jnp.where(lane < 98, out, err_sum))).astype(bf16)
    timed = over_rows(time_ref[...], d_film[...].astype(bf16)).astype(bf16)
    for s in range(4):
        grads_b[s, 0:64] = joined[64 * s : 64 * (s + 1)]
        grads_b[s, 64:320] = timed[:, 128 * s : 128 * (s + 1)]
        grads_b[s, 320:384] = jnp.zeros((64, 128), bf16)
    to_sibling(2, grads_b.at[:, theirs(ROWS_B), :], mp_b)

    gathered(zr_sem, 1, zi_a, seg)
    to_row(2, zi_a, xo_a, xi_a)
    arrive(mp_b, mr_sem.at[2])
    to_segments(2, grads_b, mp_b, zo_b, zi_b, ROWS_B)

    gathered(zr_sem, 0, film_z, seg)
    pairs = [film_z[j, 0:2] for j in range(MICRO)] + [film_z[j, 2:4] for j in range(MICRO)]
    film_all[y, x] = jnp.concatenate(pairs, axis=0).astype(bf16)
    spread(xs_sem, xr_sem, 1, film_all.at[y], x, x_peer)

    gathered(xr_sem, 2, xi_a, x)
    to_column(2, xi_a, yi_a)
    gathered(zr_sem, 2, zi_b, seg)
    xi_b[x] = added(zi_b).astype(bf16)
    spread(xs_sem, xr_sem, 3, xi_b, x, x_peer)
    gathered(xr_sem, 1, film_all.at[y], x)
    spread(ys_sem, yr_sem, 1, film_all, y, y_peer)
    gathered(yr_sem, 2, yi_a, y)
    full_a[core, x] = added(yi_a).astype(bf16)
    spread(xs_sem, xr_sem, 4, full_a.at[core], x, x_peer)
    gathered(xr_sem, 3, xi_b, x)
    to_column(3, xi_b, yi_b)

    low = jnp.where(core == 0, film_ref[0:2], film_sib[0:2])
    high = jnp.where(core == 0, film_sib[0:2], film_ref[0:2])
    film_rows = jnp.concatenate([low, high, jnp.zeros((12, 512), jnp.float32)], axis=0).astype(jnp.bfloat16)
    own_cond, sib_cond = cond_ref[seg, 0:2, here], cond_sib[seg, 0:2]
    cond_rows = jnp.concatenate(
        [jnp.where(core == 0, own_cond, sib_cond), jnp.where(core == 0, sib_cond, own_cond)], axis=0
    )
    back = lax.dot_general(film_rows, wc_ref[...], (((1,), (1,)), ((), ())), preferred_element_type=jnp.float32)
    gcond_ref[...] = back[0:4] * mish_slope(cond_rows)

    gathered(xr_sem, 4, full_a.at[core], x)
    to_sibling(4, full_a.at[core], full_a.at[core])
    gathered(yr_sem, 3, yi_b, y)
    full_b[core] = added(yi_b).astype(bf16)
    to_sibling(5, full_b.at[core], full_b.at[core])
    gathered(yr_sem, 0, act_all, y)
    gathered(yr_sem, 1, film_all, y)
    arrive(full_a.at[sibling], mr_sem.at[4])
    arrive(full_b.at[sibling], mr_sem.at[5])
    for sent_copy in started:
        sent_copy.wait_send()


def unpack_kernel(full_a, full_b, act_all, film_all, back_ref, gin, gmid, gres, gout, gtime, gwc, gcond, loss):
    f32 = jnp.float32
    flat_a = full_a[...].astype(f32).reshape(640, 128)
    for q in range(10):
        gmid[:, 128 * q : 128 * (q + 1)] = flat_a[64 * q : 64 * (q + 1)]
    flat_b = full_b[...].astype(f32).reshape(384, 128)
    joined = flat_b[0:64]
    turned = joined.T
    gin[...] = joined[:, 0:70]
    gres[...] = turned[70:84]
    gout[...] = turned[84:98]
    loss[...] = joined[0:1, 98:99] * (1.0 / 2048.0)
    gtime[...] = flat_b[64:320]
    gcond[...] = back_ref[...]
    gwc[...] = lax.dot_general(
        act_all[...].reshape(256, HALF), film_all[...].reshape(256, 128), (((0,), (0,)), ((), ())),
        preferred_element_type=f32,
    )


def step_tables():
    table = schedule()
    roots = np.zeros((8, 128))
    roots[0, :TSTEPS], roots[1, :TSTEPS] = np.sqrt(table), np.sqrt(1.0 - table)
    half = C // 2
    angles = np.arange(TSTEPS)[:, None] * np.exp(-math.log(10000.0) * np.arange(half) / (half - 1))[None]
    embedded = np.concatenate([np.sin(angles), np.cos(angles)], axis=1)
    times = np.zeros((128, C))
    times[:TSTEPS] = embedded * np.tanh(np.log1p(np.exp(embedded)))
    return jnp.asarray(roots, jnp.float32), jnp.asarray(times, jnp.float32).astype(jnp.bfloat16)


def finish(cond, w_cond_full, w_cond, noise, actions, tsteps, advantage, w_in, w_res, w_mid, w_out, w_time):
    bf16, f32 = jnp.bfloat16, jnp.float32
    roots, times = step_tables()
    vmem = pl.BlockSpec(memory_space=pltpu.VMEM)
    flat_rows = FLATS * STEPS
    big, small = pltpu.VMEM((flat_rows, C), f32), pltpu.VMEM((FLATS, C), f32)
    big16 = pltpu.VMEM((flat_rows, C), bf16)
    rows_a, rows_b = pltpu.VMEM((SIDE, ROWS_A, 128), bf16), pltpu.VMEM((SIDE, ROWS_B, 128), bf16)
    part_a = pltpu.VMEM((SIDE, ROWS_A // SIDE, 128), bf16)
    dma = pltpu.SemaphoreType.DMA
    return pl.pallas_call(
        finish_kernel,
        out_shape=(
            jax.ShapeDtypeStruct((2, SIDE, ROWS_A // SIDE, 128), bf16),
            jax.ShapeDtypeStruct((2, ROWS_B, 128), bf16),
            jax.ShapeDtypeStruct((SIDE, SIDE, 16, HALF), bf16),
            jax.ShapeDtypeStruct((SIDE, SIDE, 16, 128), bf16),
            jax.ShapeDtypeStruct((4, HALF), f32),
        ),
        in_specs=[vmem] * 14,
        out_specs=(vmem,) * 5,
        scratch_shapes=[
            pltpu.VMEM((flat_rows, 128), f32),
            pltpu.VMEM((2, STEPS, 128), f32),
            pltpu.VMEM((FLATS, 128), f32),
            pltpu.VMEM((FLATS, 128), f32),
            pltpu.VMEM((FLATS, 128), f32),
            pltpu.VMEM((FLATS, C), bf16),
            pltpu.VMEM((128, C), f32),
            pltpu.VMEM((128, C), f32),
            pltpu.VMEM((128, C), f32),
            pltpu.VMEM((128, C), bf16),
            pltpu.VMEM((128, C), bf16),
            pltpu.VMEM((C, 128), bf16),
            pltpu.VMEM((128, C), bf16),
            pltpu.VMEM((FLATS, 80, 128), f32),
            pltpu.VMEM((flat_rows, 128), bf16),
            pltpu.VMEM((FLATS, 80, C), f32),
            pltpu.VMEM((flat_rows, 5 * C), bf16),
            pltpu.VMEM((flat_rows, 5 * C), bf16),
            big, big, big, big, big, big, big,
            big16, big16,
            pltpu.VMEM((flat_rows, 128), bf16),
            big16, big16,
            pltpu.VMEM((FLATS, 2 * C), f32),
            pltpu.VMEM((FLATS, 2 * C), f32),
            small, small, small, small, small, small,
            pltpu.VMEM((MICRO, 2, HALF), f32),
            pltpu.VMEM((8, 512), f32),
            pltpu.VMEM((8, 512), f32),
            pltpu.VMEM((SIDE, 8, 128), f32),
            pltpu.VMEM((SIDE, 8, 128), f32),
            pltpu.VMEM((SIDE, 2 * ROWS_A, 128), bf16),
            pltpu.VMEM((SIDE, 2 * ROWS_B, 128), bf16),
            rows_a, rows_b, rows_a, rows_b, rows_a, rows_b,
            part_a, part_a, part_a, rows_b, rows_b,
            dma((6,)), dma((6,)),
            dma((3, 3)), dma((3, 3)),
            dma((5, 3)), dma((5, 3)),
            dma((4, 3)), dma((4, 3)),
        ],
        compiler_params=pltpu.CompilerParams(
            collective_id=1, has_side_effects=True, vmem_limit_bytes=48 * 2**20
        ),
    )(
        cond, w_cond_full, w_cond, noise, actions, tsteps, advantage, roots, times, w_in, w_res, w_mid, w_out, w_time
    )


def unpack(*arrays):
    f32 = jnp.float32
    vmem = pl.BlockSpec(memory_space=pltpu.VMEM)
    shapes = ((64, 70), (64, 1280), (14, 64), (14, 64), (256, 128), (HALF, 128), (4, HALF), (1, 1))
    return pl.pallas_call(
        unpack_kernel,
        out_shape=tuple(jax.ShapeDtypeStruct(shape, f32) for shape in shapes),
        in_specs=[vmem] * 5,
        out_specs=(vmem,) * 8,
        compiler_params=pltpu.CompilerParams(vmem_limit_bytes=32 * 2**20),
    )(*arrays)


def body(
    trunk_in, norm_gain, w_gate, w_up, w_down, w_cond, w_time, w_in, w_mid, w_res, w_out,
    tsteps, advantage, actions, noise,
):
    cond_all, w_cond_full = trunk(trunk_in, norm_gain, w_gate[0], w_up[0], w_down[0].T, w_cond)
    begin = 4 * lax.axis_index("segment") + 2 * lax.axis_index("mp")

    def own(values):
        return lax.dynamic_slice_in_dim(values, begin, 2, 0)

    parts = finish(
        cond_all, w_cond_full, w_cond, own(noise).reshape(FLATS * STEPS, 14), own(actions), tsteps.T, advantage.T,
        w_in, w_res, w_mid, w_out.T, w_time,
    )
    gin, gmid, gres, gout, gtime, gwc, gcond, loss = unpack(*parts)
    return gin.T, gmid.T, gres, gout.T, gtime, gwc, gcond, loss.reshape(1)


def solution(mesh):
    in_specs = (
        P("dp", "mp"),
        P("segment", None),
        P("segment", "dp", "mp"),
        P("segment", "dp", "mp"),
        P("segment", "mp", "dp"),
        P("mp", None),
        P(),
        P(),
        P(),
        P(),
        P(),
        P("dp", None),
        P("dp", None),
        P("dp", None, None),
        P("dp", None, None, None),
    )
    out_specs = (
        P(None, "segment"),
        P(None, "segment"),
        P(None, "segment"),
        P("segment", None),
        P(None, "segment"),
        P("mp", "segment"),
        P(("dp", "segment"), "mp"),
        P(),
    )
    return jax.shard_map(body, mesh=mesh, in_specs=in_specs, out_specs=out_specs, check_vma=False)
```

```python
import functools
import math

import jax
import jax.numpy as jnp
import numpy as np
from jax import lax
from jax.experimental import pallas as pl
from jax.experimental.pallas import tpu as pltpu
from jax.sharding import PartitionSpec as P

MESH = pl.DeviceIdType.MESH
TSTEPS = 100
SIDE = 4
MICRO = 4
ROWS = 32
BATCHES = 2
OWN = 64
PART = 512
PARTS = 5
D = 2560
HALF = 1280
FH = 1792
SHARD = 160
CUT = 80
TILE = 256


def schedule():
    grid = np.arange(TSTEPS + 1, dtype=np.float64) / TSTEPS
    curve = np.cos((grid + 0.008) / 1.008 * math.pi / 2.0) ** 2
    betas = np.minimum(1.0 - curve[1:] / curve[:-1], 0.999)
    return np.cumprod(1.0 - betas)


def trunk_kernel(
    x_ref, gain_ref, wg_ref, wu_ref, wd_ref, wc_ref,
    cond_ref, wcond_ref,
    weights, first, arrived, leaving, normed, hidden, partial, share, other,
    own_sem, gs_sem, gr_sem, ms_sem, mr_sem, ps_sem, pr_sem, zs_sem, zr_sem, cs_sem, cr_sem,
):
    dp, seg, core = lax.axis_index("dp"), lax.axis_index("segment"), lax.axis_index("mp")
    y, x = dp // SIDE, dp % SIDE
    sibling = 1 - core

    def at(axis, delta):
        if axis == "x":
            return y * SIDE + (x + delta + SIDE) % SIDE
        return ((y + delta + SIDE) % SIDE) * SIDE + x

    barrier = pltpu.get_barrier_semaphore()
    for axis in ("x", "y"):
        for delta in (1, -1):
            pl.semaphore_signal(barrier, inc=1, device_id={"dp": at(axis, delta)}, device_id_type=MESH)
    pl.semaphore_signal(barrier, inc=1, device_id={"mp": sibling}, device_id_type=MESH)
    for step in range(1, 4):
        pl.semaphore_signal(barrier, inc=1, device_id={"segment": (seg + step) % 4}, device_id_type=MESH)
    pl.semaphore_wait(barrier, 8)

    sources = (wg_ref, wu_ref, wd_ref)
    chunks = [(which, part) for which in range(3) for part in range(2)]

    def spot(which, part, px, py, begin=0, size=CUT):
        row = (py * SIDE + px) * SHARD + part * CUT + begin
        return weights.at[which, pl.ds(pl.multiple_of(row, 16), size), :]

    def place(chunk, p_off, q_off, begin=0, size=CUT):
        which, part = chunk
        dx, dy = (p_off, q_off) if part == 0 else (q_off, p_off)
        return spot(which, part, (x + dx + SIDE) % SIDE, (y + dy + SIDE) % SIDE, begin, size)

    def axes(chunk):
        return ("x", "y") if chunk[1] == 0 else ("y", "x")

    def piece(chunk, kind):
        return (0, 48) if kind == 0 else (48, 32)

    def make(chunk, number, src, dst, axis, delta):
        q = chunks.index(chunk)
        return pltpu.make_async_remote_copy(
            src_ref=src, dst_ref=dst, send_sem=gs_sem.at[q, number], recv_sem=gr_sem.at[q, number],
            device_id={"dp": at(axis, delta)}, device_id_type=MESH,
        )

    OFF = (0, -1, 1, 2)

    def spec(chunk, number):
        p_axis, q_axis = axes(chunk)
        if number < 4:
            delta = 1 if number % 2 == 0 else -1
            if number < 2:
                return p_axis, delta, 0, 0, 0, CUT
            begin, size = piece(chunk, number - 2)
            return p_axis, delta, -delta, 0, begin, size
        slot, kind = divmod(number - 4, 4)
        delta = 1 if kind % 2 == 0 else -1
        if kind < 2:
            return q_axis, delta, OFF[slot], 0, 0, CUT
        begin, size = piece(chunk, kind - 2)
        return q_axis, delta, OFF[slot], -delta, begin, size

    def source_of(chunk, number):
        _, _, p_off, q_off, begin, size = spec(chunk, number)
        if p_off == 0 and q_off == 0:
            return sources[chunk[0]].at[pl.ds(chunk[1] * CUT + begin, size), :]
        return place(chunk, p_off, q_off, begin, size)

    def send(chunk, number):
        axis, delta, p_off, q_off, begin, size = spec(chunk, number)
        make(chunk, number, source_of(chunk, number), place(chunk, p_off, q_off, begin, size), axis, delta).start()

    def receive(chunk, number):
        axis, delta, p_off, q_off, begin, size = spec(chunk, number)
        if number < 4:
            p_off = p_off - delta
        else:
            q_off = q_off - delta
        spot_here = place(chunk, p_off, q_off, begin, size)
        make(chunk, number, spot_here, spot_here, axis, delta).wait_recv()

    def sent(chunk, number):
        axis, delta, p_off, q_off, begin, size = spec(chunk, number)
        make(chunk, number, source_of(chunk, number), place(chunk, p_off, q_off, begin, size), axis, delta).wait_send()

    own = []
    for chunk in chunks:
        for number in (0, 1, 4, 5):
            send(chunk, number)
    for which in range(3):
        keep = pltpu.make_async_copy(
            sources[which], weights.at[which, pl.ds(pl.multiple_of(dp * SHARD, 16), SHARD), :], own_sem.at[which]
        )
        keep.start()
        own.append(keep)

    def sibling_copy(number, src, dst):
        return pltpu.make_async_remote_copy(
            src_ref=src, dst_ref=dst, send_sem=ms_sem.at[number], recv_sem=mr_sem.at[number],
            device_id={"mp": sibling}, device_id_type=MESH,
        )

    here = pl.ds(pl.multiple_of(core * HALF, 128), HALF)
    there = pl.ds(pl.multiple_of(sibling * HALF, 128), HALF)
    def slot_of(j, features):
        return first.at[j // 2, pl.ds(32 * (j % 2), ROWS), features]

    for j in range(MICRO):
        src = x_ref.at[pl.ds(pl.multiple_of(64 * j + 32 * sibling, 16), ROWS), :]
        sibling_copy(j, src, slot_of(j, here)).start()
        kept = pltpu.make_async_copy(
            x_ref.at[pl.ds(pl.multiple_of(64 * j + 32 * core, 16), ROWS), :], slot_of(j, here), own_sem.at[3 + j]
        )
        kept.start()
        own.append(kept)
    here_rows = wcond_ref.at[pl.ds(pl.multiple_of(core * HALF, 16), HALF), :]
    there_rows = wcond_ref.at[pl.ds(pl.multiple_of(sibling * HALF, 16), HALF), :]
    sibling_copy(4, wc_ref, here_rows).start()
    kept = pltpu.make_async_copy(wc_ref, here_rows, own_sem.at[7])
    kept.start()
    own.append(kept)

    for chunk in chunks:
        for number in (0, 1):
            receive(chunk, number)
            send(chunk, 2 + number)
            slot = 1 + number
            send(chunk, 4 + 4 * slot)
            send(chunk, 5 + 4 * slot)
        for kind in (0, 1):
            receive(chunk, 4 + kind)
            send(chunk, 6 + kind)
    for chunk in chunks:
        for number in (2, 3):
            receive(chunk, number)
        send(chunk, 16)
        send(chunk, 17)
        for slot in (1, 2):
            for kind in (0, 1):
                receive(chunk, 4 + 4 * slot + kind)
                send(chunk, 6 + 4 * slot + kind)
    for chunk in chunks:
        for kind in (0, 1):
            receive(chunk, 16 + kind)
            send(chunk, 18 + kind)
    for j in range(MICRO):
        sibling_copy(j, slot_of(j, there), slot_of(j, there)).wait_recv()
    for keep in own[3:7]:
        keep.wait()

    def finish_gather():
        for chunk in chunks:
            for slot in range(4):
                for kind in (2, 3):
                    receive(chunk, 4 + 4 * slot + kind)
        for keep in own[:3] + own[7:]:
            keep.wait()

    def z_copy(b, g):
        return pltpu.make_async_remote_copy(
            src_ref=leaving.at[b, g], dst_ref=arrived.at[b, g], send_sem=zs_sem.at[b, g], recv_sem=zr_sem.at[b, g],
            device_id={"segment": (seg + 1) % 4}, device_id_type=MESH,
        )

    def share_copy(b, g):
        return pltpu.make_async_remote_copy(
            src_ref=share.at[b, g], dst_ref=other.at[b, g], send_sem=ps_sem.at[b, g], recv_sem=pr_sem.at[b, g],
            device_id={"mp": sibling}, device_id_type=MESH,
        )

    def normed_copy(b):
        return sibling_copy(5 + b, normed.at[b, pl.ds(0, OWN)], normed.at[b, pl.ds(OWN, OWN)])

    def cond_copy(j, target):
        return pltpu.make_async_remote_copy(
            src_ref=cond_ref.at[j], dst_ref=cond_ref.at[j], send_sem=cs_sem.at[j, target], recv_sem=cr_sem.at[j],
            device_id={"segment": target}, device_id_type=MESH,
        )

    def columns_of(g):
        return slice(PART * g, PART * (g + 1))

    def normalize(b):
        states = [arrived[b, g].astype(jnp.float32) for g in range(PARTS)]
        total = sum(jnp.sum(state * state, axis=1, keepdims=True) for state in states)
        factor = lax.rsqrt(total * (1.0 / D) + 1e-05)
        for g in range(PARTS):
            gain = gain_ref[:, columns_of(g)].astype(jnp.float32)
            normed[b, 0:OWN, columns_of(g)] = (states[g] * factor * gain).astype(jnp.bfloat16)
        normed_copy(b).start()

    def batch(b, carry):
        @pl.when(seg > 0)
        def _():
            for g in range(PARTS):
                z_copy(b, g).wait_recv()
            normalize(b)

        normed_copy(b).wait_recv()
        for n in range(FH // TILE):
            cols = slice(n * TILE, (n + 1) * TILE)
            rows = normed[b]
            gate = jnp.dot(rows, weights[0, :, cols], preferred_element_type=jnp.float32)
            lift = jnp.dot(rows, weights[1, :, cols], preferred_element_type=jnp.float32)
            hidden[:, cols] = (gate / (1.0 + jnp.exp(-gate)) * lift).astype(jnp.bfloat16)

        def finish(g):
            share_copy(b, g).wait_recv()
            whole = partial[g] + other[b, g].astype(jnp.float32)
            leaving[b, g] = (arrived[b, g].astype(jnp.float32) + whole).astype(jnp.bfloat16)

            @pl.when(seg < 3)
            def _():
                z_copy(b, g).start()

        for g in range(PARTS):
            for half in range(2):
                part = slice(TILE * half, TILE * (half + 1))
                out = lax.dot_general(
                    hidden[...], weights[2, PART * g + TILE * half : PART * g + TILE * (half + 1), :],
                    (((1,), (1,)), ((), ())), preferred_element_type=jnp.float32,
                )
                partial[g, :, part] = out[0:OWN]
                share[b, g, :, part] = out[OWN:].astype(jnp.bfloat16)
            share_copy(b, g).start()
            if g > 0:
                finish(g - 1)
        finish(PARTS - 1)

        @pl.when(seg == 3)
        def _():
            for half in range(2):
                for g in range(PARTS):
                    rows = leaving[b, g, ROWS * half : ROWS * (half + 1)].astype(jnp.float32)
                    mean = jnp.mean(rows.reshape(2, 16, PART), axis=1)
                    cond_ref[2 * b + half, 0:2, columns_of(g)] = mean.astype(jnp.bfloat16).astype(jnp.float32)
                for target in range(3):
                    cond_copy(2 * b + half, target).start()

        return carry

    @pl.when(seg == 0)
    def _():
        for b in range(BATCHES):
            for g in range(PARTS):
                arrived[b, g] = first[b, :, columns_of(g)]
            normalize(b)

    finish_gather()
    lax.fori_loop(0, BATCHES, batch, 0)

    for chunk in chunks:
        for number in range(20):
            sent(chunk, number)
    for b in range(BATCHES):
        normed_copy(b).wait_send()
        for g in range(PARTS):
            share_copy(b, g).wait_send()

    @pl.when(seg < 3)
    def _():
        for b in range(BATCHES):
            for g in range(PARTS):
                z_copy(b, g).wait_send()

    for j in range(MICRO):
        sibling_copy(j, x_ref.at[pl.ds(0, ROWS), :], slot_of(j, there)).wait_send()

        @pl.when(seg < 3)
        def _(j=j):
            cond_copy(j, 0).wait_recv()

        @pl.when(seg == 3)
        def _(j=j):
            for target in range(3):
                cond_copy(j, target).wait_send()

    last = sibling_copy(4, wc_ref, there_rows)
    last.wait_recv()
    last.wait_send()


def trunk(trunk_in, norm_gain, w_gate, w_up, w_down_t, w_cond):
    anywhere = pl.BlockSpec(memory_space=pl.ANY)
    vmem = pl.BlockSpec(memory_space=pltpu.VMEM)
    dma = pltpu.SemaphoreType.DMA
    bf16 = jnp.bfloat16
    return pl.pallas_call(
        trunk_kernel,
        out_shape=(
            jax.ShapeDtypeStruct((MICRO, 2, D), jnp.float32),
            jax.ShapeDtypeStruct((D, w_cond.shape[1]), bf16),
        ),
        in_specs=[anywhere, vmem, anywhere, anywhere, anywhere, anywhere],
        out_specs=(vmem, anywhere),
        scratch_shapes=[
            pltpu.VMEM((3, D, FH), bf16),
            pltpu.VMEM((BATCHES, OWN, D), bf16),
            pltpu.VMEM((BATCHES, PARTS, OWN, PART), bf16),
            pltpu.VMEM((BATCHES, PARTS, OWN, PART), bf16),
            pltpu.VMEM((BATCHES, 2 * OWN, D), bf16),
            pltpu.VMEM((2 * OWN, FH), bf16),
            pltpu.VMEM((PARTS, OWN, PART), jnp.float32),
            pltpu.VMEM((BATCHES, PARTS, OWN, PART), bf16),
            pltpu.VMEM((BATCHES, PARTS, OWN, PART), bf16),
            dma((8,)),
            dma((6, 20)),
            dma((6, 20)),
            dma((7,)),
            dma((7,)),
            dma((BATCHES, PARTS)),
            dma((BATCHES, PARTS)),
            dma((BATCHES, PARTS)),
            dma((BATCHES, PARTS)),
            dma((MICRO, 3)),
            dma((MICRO,)),
        ],
        compiler_params=pltpu.CompilerParams(
            collective_id=0, has_side_effects=True, vmem_limit_bytes=52 * 2**20
        ),
    )(trunk_in, norm_gain, w_gate, w_up, w_down_t, w_cond)


def mish_parts(values):
    small = jnp.exp(-jnp.abs(values))
    right = values > 0
    top = jnp.where(right, 1.0 + 2.0 * small, small * (small + 2.0))
    rest = jnp.where(right, 2.0 * small * small, 2.0)
    return small, right, top, rest


def mish_value(values):
    _, _, top, rest = mish_parts(values)
    return values * (top / (top + rest))


def mish_slope(values):
    small, right, top, rest = mish_parts(values)
    inverse = 1.0 / (top + rest)
    logistic = jnp.where(right, 1.0, small) / (1.0 + small)
    return top * inverse + values * logistic * (rest * (2.0 * top + rest)) * (inverse * inverse)


FLATS = 16
STEPS = 64
C = 256
BLOCK = 256
ROWS_A = 320
ROWS_B = 192


def finish_kernel(
    cond_ref, wcond_ref, wc_ref, noise_in, actions_in, tsteps_ref, advantage_ref, roots_ref, table_ref,
    win_in, wres_in, wmid_ref, wout_in, wtime_ref,
    full_a, full_b, act_all, film_all, gcond_ref,
    noise_ref, actions_ref, keep_ref, blend_ref, adv_ref, time_ref, wide_in, wide_res, wide_out, win_ref, wres_ref,
    wout_ref, wout_t_ref, npad, cols, pad, mid, back, pre, res, unit1, act1, slope1, unit2, slope2, block, d_block, d_pred,
    d_second, d_first, film, d_film, sum1, sum2, inv1, inv2, mean1, mean2,
    cond_sib, film_ref, film_sib, film_out, film_z,
    grads_a, grads_b, mp_a, mp_b, zo_a, zo_b, zi_a, zi_b, xo_a, xi_a, yi_a, xi_b, yi_b,
    ms_sem, mr_sem, zs_sem, zr_sem, xs_sem, xr_sem, ys_sem, yr_sem,
):
    dp, seg, core = lax.axis_index("dp"), lax.axis_index("segment"), lax.axis_index("mp")
    y, x = dp // SIDE, dp % SIDE
    sibling = 1 - core

    def x_peer(step):
        return {"dp": y * SIDE + (x + step) % SIDE}

    def y_peer(step):
        return {"dp": ((y + step) % SIDE) * SIDE + x}

    def z_peer(step):
        return {"segment": (seg + step) % SIDE}

    barrier = pltpu.get_barrier_semaphore()
    pl.semaphore_signal(barrier, inc=1, device_id={"mp": sibling}, device_id_type=MESH)
    for step in range(1, SIDE):
        for peer in (x_peer, y_peer, z_peer):
            pl.semaphore_signal(barrier, inc=1, device_id=peer(step), device_id_type=MESH)

    def copy(src, dst, out_sem, in_sem, peer):
        return pltpu.make_async_remote_copy(
            src_ref=src, dst_ref=dst, send_sem=out_sem, recv_sem=in_sem, device_id=peer, device_id_type=MESH
        )

    started = []

    def launch(src, dst, out_sem, in_sem, peer):
        one = copy(src, dst, out_sem, in_sem, peer)
        one.start()
        started.append(one)

    def arrive(dst, in_sem):
        copy(dst, dst, ms_sem.at[0], in_sem, {"mp": sibling}).wait_recv()

    def to_sibling(number, src, dst):
        launch(src, dst, ms_sem.at[number], mr_sem.at[number], {"mp": sibling})

    def scatter(out_sem, in_sem, number, src, dst, me, peer):
        for step in range(1, SIDE):
            launch(
                src.at[(me + step) % SIDE], dst.at[me], out_sem.at[number, step - 1], in_sem.at[number, step - 1], peer(step)
            )

    def spread(out_sem, in_sem, number, slots, me, peer):
        for step in range(1, SIDE):
            launch(slots.at[me], slots.at[me], out_sem.at[number, step - 1], in_sem.at[number, step - 1], peer(step))

    def gathered(in_sem, number, slots, me):
        for step in range(1, SIDE):
            arrive(slots.at[(me - step + SIDE) % SIDE], in_sem.at[number, step - 1])

    def added(slots):
        pieces = [slots[k].astype(jnp.float32) for k in range(SIDE)]
        return (pieces[0] + pieces[1]) + (pieces[2] + pieces[3])

    here = pl.ds(pl.multiple_of(core * HALF, 128), HALF)
    there = pl.ds(pl.multiple_of(sibling * HALF, 128), HALF)
    bf16, f32 = jnp.bfloat16, jnp.float32

    def rows_of(f, size=STEPS):
        return pl.ds(pl.multiple_of(f * size, size), size)

    def one(f):
        return pl.ds(f, 1)

    def each(body, count=FLATS):
        def step(f, carry):
            body(f)
            return carry

        lax.fori_loop(0, count, step, 0, unroll=8 if count == FLATS else 4)

    lanes = lax.broadcasted_iota(jnp.int32, (C, C), 1)
    row_ids = lax.broadcasted_iota(jnp.int32, (C, C), 0)
    same = jnp.where(lanes // 32 == row_ids // 32, 1.0 / 2048.0, 0.0).astype(bf16)

    def group_mean(values):
        high = values.astype(bf16)
        rest = values - high.astype(f32)
        middle = rest.astype(bf16)
        low = (rest - middle.astype(f32)).astype(bf16)
        count = values.shape[0]
        sums = jnp.dot(jnp.concatenate([high, middle, low], axis=0), same, preferred_element_type=f32)
        return sums[0:count] + (sums[count : 2 * count] + sums[2 * count : 3 * count])

    def dot(left, right):
        return jnp.dot(left, right, preferred_element_type=f32)

    begin = 4 * seg + 2 * core
    sample_at = lax.broadcasted_iota(jnp.int32, (8, 16), 1)

    def column(ref):
        pieces = []
        for sample in range(2):
            chosen = jnp.where(sample_at == begin + sample, ref[...].astype(f32), 0.0)
            pieces.append(jnp.sum(chosen, axis=1, keepdims=True))
        return jnp.broadcast_to(jnp.concatenate(pieces, axis=0), (FLATS, 128))

    steps_at = column(tsteps_ref)
    lane_at = lax.broadcasted_iota(jnp.int32, (FLATS, 128), 1).astype(f32)
    picked = jnp.where(steps_at == lane_at, 1.0, 0.0)
    keep_ref[...] = jnp.broadcast_to(jnp.sum(picked * roots_ref[0:1], axis=1, keepdims=True), (FLATS, 128))
    blend_ref[...] = jnp.broadcast_to(jnp.sum(picked * roots_ref[1:2], axis=1, keepdims=True), (FLATS, 128))
    adv_ref[...] = column(advantage_ref)
    time_ref[...] = dot(picked.astype(bf16), table_ref[...]).astype(bf16)
    for sample in range(2):
        actions_ref[sample] = jnp.zeros((STEPS, 128), f32)
        actions_ref[sample, :, 0:14] = actions_in[sample].astype(f32)

    def widen(f):
        noise_ref[rows_of(f)] = jnp.zeros((STEPS, 128), f32)
        noise_ref[rows_of(f), 0:14] = noise_in[rows_of(f)].astype(f32)

    each(widen)
    wide_in[...] = jnp.zeros_like(wide_in)
    wide_in[0:70] = win_in[...].astype(f32)
    win_ref[...] = wide_in[...].astype(bf16)
    wide_res[...] = jnp.zeros_like(wide_res)
    wide_res[70:84] = wres_in[...].astype(f32)
    wres_ref[...] = wide_res[...].astype(bf16)
    wide_out[...] = jnp.zeros_like(wide_out)
    wide_out[0:14] = wout_in[...].astype(f32)
    wout_t_ref[...] = wide_out[...].astype(bf16)
    wout_ref[...] = wide_out[...].T.astype(bf16)

    npad[...] = jnp.zeros_like(npad)
    pad[...] = jnp.zeros_like(pad)

    def make_cols(f):
        noisy = keep_ref[one(f)] * actions_ref[f // 8] + blend_ref[one(f)] * noise_ref[rows_of(f)]
        noisy = noisy.astype(bf16).astype(f32)
        npad[f, 8:72] = noisy
        total = pltpu.roll(noisy, 70, 1)
        for tap in range(5):
            total = total + pltpu.roll(npad[f, 6 + tap : 70 + tap], 14 * tap, 1)
        cols[rows_of(f)] = total.astype(bf16)

    each(make_cols)

    pl.semaphore_wait(barrier, 10)
    to_sibling(3, cond_ref.at[:, :, there], cond_sib)

    time_film = dot(time_ref[...], wtime_ref[...])
    own_pair = jnp.concatenate([mish_value(cond_ref[seg]), jnp.zeros((6, D), f32)], axis=0)
    film_cond = dot(own_pair.astype(bf16), wcond_ref[...])
    top = jnp.broadcast_to(film_cond[0:1], (8, 2 * C))
    low = jnp.broadcast_to(film_cond[1:2], (8, 2 * C))
    film[...] = jnp.concatenate([top, low], axis=0) + time_film

    def first_conv(b):
        rows = rows_of(b, BLOCK)
        out = dot(cols[rows], win_ref[...])
        pre[rows] = out
        res[rows] = dot(cols[rows], wres_ref[...])

    each(first_conv, 4)

    arrive(cond_sib, mr_sem.at[3])
    pairs = [cond_ref[j, 0:2, here] for j in range(MICRO)] + [cond_sib[j, 0:2] for j in range(MICRO)]
    act_all[y, x] = mish_value(jnp.concatenate(pairs, axis=0)).astype(bf16)
    spread(xs_sem, xr_sem, 0, act_all.at[y], x, x_peer)

    def centre(inverse):
        def total(f):
            sum1[one(f)] = jnp.sum(pre[rows_of(f)], axis=0, keepdims=True)

        each(total)
        mean1[...] = group_mean(sum1[...])

        def moved(f):
            left = pre[rows_of(f)] - mean1[one(f)]
            pre[rows_of(f)] = left
            sum1[one(f)] = jnp.sum(left * left, axis=0, keepdims=True)

        each(moved)
        inverse[...] = lax.rsqrt(group_mean(sum1[...]) + 1e-05)

    def mish_both(values):
        small, right, above, rest = mish_parts(values)
        inverse = 1.0 / (above + rest)
        logistic = jnp.where(right, 1.0, small) / (1.0 + small)
        ratio = above * inverse
        value = values * ratio
        return value, ratio + values * logistic * (rest * (2.0 * above + rest)) * (inverse * inverse)

    centre(inv1)

    def first_act(f):
        unit = pre[rows_of(f)] * inv1[one(f)]
        value, slope = mish_both(unit)
        unit1[rows_of(f)] = unit
        act1[rows_of(f)] = value
        slope1[rows_of(f)] = slope
        changed = film[one(f), 0:C] * value + film[one(f), C:]
        pad[f, 8:72] = changed.astype(bf16).astype(f32)
        for tap in range(5):
            mid[rows_of(f), C * tap : C * (tap + 1)] = pad[f, 6 + tap : 70 + tap].astype(bf16)

    each(first_act)

    gathered(xr_sem, 0, act_all.at[y], x)
    spread(ys_sem, yr_sem, 0, act_all, y, y_peer)

    def second_conv(b):
        rows = rows_of(b, BLOCK)
        pre[rows] = dot(mid[rows], wmid_ref[...])

    each(second_conv, 4)
    centre(inv2)

    def second_act(f):
        unit = pre[rows_of(f)] * inv2[one(f)]
        value, slope = mish_both(unit)
        unit2[rows_of(f)] = unit
        slope2[rows_of(f)] = slope
        block[rows_of(f)] = (value + res[rows_of(f)]).astype(bf16)

    each(second_act)

    def errors(f, total):
        rows = rows_of(f)
        error = dot(block[rows], wout_ref[...]) - noise_ref[rows]
        d_pred[rows] = (adv_ref[one(f)] * error * (2.0 / 896.0)).astype(bf16)
        return total + error * error

    err = lax.fori_loop(0, FLATS, errors, jnp.zeros((STEPS, 128), f32), unroll=8)
    err_sum = jnp.sum(err) * (1.0 / 896.0)

    def from_pred(b):
        rows = rows_of(b, BLOCK)
        out = dot(d_pred[rows], wout_t_ref[...])
        pre[rows] = out
        d_block[rows] = out.astype(bf16)

    each(from_pred, 4)

    def act_back(scale, unit, slope):
        def totals(f):
            grad = scale(f) * slope[rows_of(f)]
            pre[rows_of(f)] = grad
            sum1[one(f)] = jnp.sum(grad, axis=0, keepdims=True)
            sum2[one(f)] = jnp.sum(grad * unit[rows_of(f)], axis=0, keepdims=True)

        each(totals)
        means = group_mean(jnp.concatenate([sum1[...], sum2[...]], axis=0))
        mean1[...] = means[0:FLATS]
        mean2[...] = means[FLATS:]

    act_back(lambda f: pre[rows_of(f)], unit2, slope2)

    def second_back(f):
        grad = inv2[one(f)] * (pre[rows_of(f)] - mean1[one(f)] - unit2[rows_of(f)] * mean2[one(f)])
        rounded = grad.astype(bf16)
        d_second[rows_of(f)] = rounded
        pad[f, 8:72] = rounded.astype(f32)
        for tap in range(5):
            back[rows_of(f), C * tap : C * (tap + 1)] = pad[f, 10 - tap : 74 - tap].astype(bf16)

    each(second_back)

    def over_rows(left, right):
        return lax.dot_general(left, right, (((0,), (0,)), ((), ())), preferred_element_type=f32)

    for tap in range(5):
        grad = over_rows(d_second[...], mid[:, C * tap : C * (tap + 1)]).astype(bf16)
        for s in range(4):
            for half in range(2):
                begin = 64 * (2 * tap + half)
                grads_a[s, begin : begin + 64] = grad[64 * s : 64 * (s + 1), 128 * half : 128 * (half + 1)]

    def ours(rows):
        return pl.ds(pl.multiple_of(core * rows, 16), rows)

    def theirs(rows):
        return pl.ds(pl.multiple_of(sibling * rows, 16), rows)

    def to_segments(number, grads, landed, out, slots, rows):
        out[...] = (grads[:, ours(rows), :].astype(f32) + landed[...].astype(f32)).astype(bf16)
        scatter(zs_sem, zr_sem, number, out, slots, seg, z_peer)
        slots[seg] = out[seg]

    def to_row(number, got, out, slots):
        out[...] = added(got).astype(bf16).reshape(out.shape)
        scatter(xs_sem, xr_sem, number, out, slots, x, x_peer)
        slots[x] = out[x]

    def to_column(number, got, slots):
        slots[y] = added(got).astype(bf16)
        spread(ys_sem, yr_sem, number, slots, y, y_peer)

    to_sibling(1, grads_a.at[:, theirs(ROWS_A), :], mp_a)

    def mid_back(b):
        rows = rows_of(b, BLOCK)
        pre[rows] = sum(
            lax.dot_general(
                back[rows, C * tap : C * (tap + 1)], wmid_ref[C * tap : C * (tap + 1)], (((1,), (1,)), ((), ())),
                preferred_element_type=f32,
            )
            for tap in range(5)
        )

    each(mid_back, 4)

    arrive(mp_a, mr_sem.at[1])
    to_segments(1, grads_a, mp_a, zo_a, zi_a, ROWS_A)

    def film_back(f):
        grad = pre[rows_of(f)]
        d_film[one(f), 0:C] = jnp.sum(grad * act1[rows_of(f)], axis=0, keepdims=True)
        d_film[one(f), C:] = jnp.sum(grad, axis=0, keepdims=True)

    each(film_back)
    film_ref[...] = jnp.zeros_like(film_ref)
    film_ref[0:1] = jnp.sum(d_film[0:8], axis=0, keepdims=True)
    film_ref[1:2] = jnp.sum(d_film[8:16], axis=0, keepdims=True)

    to_sibling(0, film_ref, film_sib)

    act_back(lambda f: pre[rows_of(f)] * film[one(f), 0:C], unit1, slope1)

    arrive(film_sib, mr_sem.at[0])
    film_out[...] = jnp.zeros_like(film_out)
    for s in range(SIDE):
        film_out[s, 0:2] = film_ref[0:2, 128 * s : 128 * (s + 1)]
        film_out[s, 2:4] = film_sib[0:2, 128 * s : 128 * (s + 1)]
    scatter(zs_sem, zr_sem, 0, film_out, film_z, seg, z_peer)
    film_z[seg] = film_out[seg]

    def first_back(f):
        grad = inv1[one(f)] * (pre[rows_of(f)] - mean1[one(f)] - unit1[rows_of(f)] * mean2[one(f)])
        d_first[rows_of(f)] = grad.astype(bf16)

    each(first_back)

    lane = lax.broadcasted_iota(jnp.int32, (C, 128), 1)
    inner = over_rows(d_first[...], cols[...])
    skip = over_rows(d_block[...], cols[...])
    out = pltpu.roll(over_rows(block[...], d_pred[...]), 84, 1)
    joined = jnp.where(lane < 70, inner, jnp.where(lane < 84, skip, jnp.where(lane < 98, out, err_sum))).astype(bf16)
    timed = over_rows(time_ref[...], d_film[...].astype(bf16)).astype(bf16)
    for s in range(4):
        grads_b[s, 0:64] = joined[64 * s : 64 * (s + 1)]
        grads_b[s, 64:320] = timed[:, 128 * s : 128 * (s + 1)]
        grads_b[s, 320:384] = jnp.zeros((64, 128), bf16)
    to_sibling(2, grads_b.at[:, theirs(ROWS_B), :], mp_b)

    gathered(zr_sem, 1, zi_a, seg)
    to_row(2, zi_a, xo_a, xi_a)
    arrive(mp_b, mr_sem.at[2])
    to_segments(2, grads_b, mp_b, zo_b, zi_b, ROWS_B)

    gathered(zr_sem, 0, film_z, seg)
    pairs = [film_z[j, 0:2] for j in range(MICRO)] + [film_z[j, 2:4] for j in range(MICRO)]
    film_all[y, x] = jnp.concatenate(pairs, axis=0).astype(bf16)
    spread(xs_sem, xr_sem, 1, film_all.at[y], x, x_peer)

    gathered(xr_sem, 2, xi_a, x)
    to_column(2, xi_a, yi_a)
    gathered(zr_sem, 2, zi_b, seg)
    xi_b[x] = added(zi_b).astype(bf16)
    spread(xs_sem, xr_sem, 3, xi_b, x, x_peer)
    gathered(xr_sem, 1, film_all.at[y], x)
    spread(ys_sem, yr_sem, 1, film_all, y, y_peer)
    gathered(yr_sem, 2, yi_a, y)
    full_a[core, x] = added(yi_a).astype(bf16)
    spread(xs_sem, xr_sem, 4, full_a.at[core], x, x_peer)
    gathered(xr_sem, 3, xi_b, x)
    to_column(3, xi_b, yi_b)

    low = jnp.where(core == 0, film_ref[0:2], film_sib[0:2])
    high = jnp.where(core == 0, film_sib[0:2], film_ref[0:2])
    film_rows = jnp.concatenate([low, high, jnp.zeros((12, 512), jnp.float32)], axis=0).astype(jnp.bfloat16)
    own_cond, sib_cond = cond_ref[seg, 0:2, here], cond_sib[seg, 0:2]
    cond_rows = jnp.concatenate(
        [jnp.where(core == 0, own_cond, sib_cond), jnp.where(core == 0, sib_cond, own_cond)], axis=0
    )
    back = lax.dot_general(film_rows, wc_ref[...], (((1,), (1,)), ((), ())), preferred_element_type=jnp.float32)
    gcond_ref[...] = back[0:4] * mish_slope(cond_rows)

    gathered(xr_sem, 4, full_a.at[core], x)
    to_sibling(4, full_a.at[core], full_a.at[core])
    gathered(yr_sem, 3, yi_b, y)
    full_b[core] = added(yi_b).astype(bf16)
    to_sibling(5, full_b.at[core], full_b.at[core])
    gathered(yr_sem, 0, act_all, y)
    gathered(yr_sem, 1, film_all, y)
    arrive(full_a.at[sibling], mr_sem.at[4])
    arrive(full_b.at[sibling], mr_sem.at[5])
    for sent_copy in started:
        sent_copy.wait_send()


def unpack_kernel(full_a, full_b, act_all, film_all, back_ref, gin, gmid, gres, gout, gtime, gwc, gcond, loss):
    f32 = jnp.float32
    flat_a = full_a[...].astype(f32).reshape(640, 128)
    for q in range(10):
        gmid[:, 128 * q : 128 * (q + 1)] = flat_a[64 * q : 64 * (q + 1)]
    flat_b = full_b[...].astype(f32).reshape(384, 128)
    joined = flat_b[0:64]
    turned = joined.T
    gin[...] = joined[:, 0:70]
    gres[...] = turned[70:84]
    gout[...] = turned[84:98]
    loss[...] = joined[0:1, 98:99] * (1.0 / 2048.0)
    gtime[...] = flat_b[64:320]
    gcond[...] = back_ref[...]
    gwc[...] = lax.dot_general(
        act_all[...].reshape(256, HALF), film_all[...].reshape(256, 128), (((0,), (0,)), ((), ())),
        preferred_element_type=f32,
    )


def step_tables():
    table = schedule()
    roots = np.zeros((8, 128))
    roots[0, :TSTEPS], roots[1, :TSTEPS] = np.sqrt(table), np.sqrt(1.0 - table)
    half = C // 2
    angles = np.arange(TSTEPS)[:, None] * np.exp(-math.log(10000.0) * np.arange(half) / (half - 1))[None]
    embedded = np.concatenate([np.sin(angles), np.cos(angles)], axis=1)
    times = np.zeros((128, C))
    times[:TSTEPS] = embedded * np.tanh(np.log1p(np.exp(embedded)))
    return jnp.asarray(roots, jnp.float32), jnp.asarray(times, jnp.float32).astype(jnp.bfloat16)


def finish(cond, w_cond_full, w_cond, noise, actions, tsteps, advantage, w_in, w_res, w_mid, w_out, w_time):
    bf16, f32 = jnp.bfloat16, jnp.float32
    roots, times = step_tables()
    vmem = pl.BlockSpec(memory_space=pltpu.VMEM)
    flat_rows = FLATS * STEPS
    big, small = pltpu.VMEM((flat_rows, C), f32), pltpu.VMEM((FLATS, C), f32)
    big16 = pltpu.VMEM((flat_rows, C), bf16)
    rows_a, rows_b = pltpu.VMEM((SIDE, ROWS_A, 128), bf16), pltpu.VMEM((SIDE, ROWS_B, 128), bf16)
    part_a = pltpu.VMEM((SIDE, ROWS_A // SIDE, 128), bf16)
    dma = pltpu.SemaphoreType.DMA
    return pl.pallas_call(
        finish_kernel,
        out_shape=(
            jax.ShapeDtypeStruct((2, SIDE, ROWS_A // SIDE, 128), bf16),
            jax.ShapeDtypeStruct((2, ROWS_B, 128), bf16),
            jax.ShapeDtypeStruct((SIDE, SIDE, 16, HALF), bf16),
            jax.ShapeDtypeStruct((SIDE, SIDE, 16, 128), bf16),
            jax.ShapeDtypeStruct((4, HALF), f32),
        ),
        in_specs=[vmem] * 14,
        out_specs=(vmem,) * 5,
        scratch_shapes=[
            pltpu.VMEM((flat_rows, 128), f32),
            pltpu.VMEM((2, STEPS, 128), f32),
            pltpu.VMEM((FLATS, 128), f32),
            pltpu.VMEM((FLATS, 128), f32),
            pltpu.VMEM((FLATS, 128), f32),
            pltpu.VMEM((FLATS, C), bf16),
            pltpu.VMEM((128, C), f32),
            pltpu.VMEM((128, C), f32),
            pltpu.VMEM((128, C), f32),
            pltpu.VMEM((128, C), bf16),
            pltpu.VMEM((128, C), bf16),
            pltpu.VMEM((C, 128), bf16),
            pltpu.VMEM((128, C), bf16),
            pltpu.VMEM((FLATS, 80, 128), f32),
            pltpu.VMEM((flat_rows, 128), bf16),
            pltpu.VMEM((FLATS, 80, C), f32),
            pltpu.VMEM((flat_rows, 5 * C), bf16),
            pltpu.VMEM((flat_rows, 5 * C), bf16),
            big, big, big, big, big, big, big,
            big16, big16,
            pltpu.VMEM((flat_rows, 128), bf16),
            big16, big16,
            pltpu.VMEM((FLATS, 2 * C), f32),
            pltpu.VMEM((FLATS, 2 * C), f32),
            small, small, small, small, small, small,
            pltpu.VMEM((MICRO, 2, HALF), f32),
            pltpu.VMEM((8, 512), f32),
            pltpu.VMEM((8, 512), f32),
            pltpu.VMEM((SIDE, 8, 128), f32),
            pltpu.VMEM((SIDE, 8, 128), f32),
            pltpu.VMEM((SIDE, 2 * ROWS_A, 128), bf16),
            pltpu.VMEM((SIDE, 2 * ROWS_B, 128), bf16),
            rows_a, rows_b, rows_a, rows_b, rows_a, rows_b,
            part_a, part_a, part_a, rows_b, rows_b,
            dma((6,)), dma((6,)),
            dma((3, 3)), dma((3, 3)),
            dma((5, 3)), dma((5, 3)),
            dma((4, 3)), dma((4, 3)),
        ],
        compiler_params=pltpu.CompilerParams(
            collective_id=1, has_side_effects=True, vmem_limit_bytes=48 * 2**20
        ),
    )(
        cond, w_cond_full, w_cond, noise, actions, tsteps, advantage, roots, times, w_in, w_res, w_mid, w_out, w_time
    )


def unpack(*arrays):
    f32 = jnp.float32
    vmem = pl.BlockSpec(memory_space=pltpu.VMEM)
    shapes = ((64, 70), (64, 1280), (14, 64), (14, 64), (256, 128), (HALF, 128), (4, HALF), (1, 1))
    return pl.pallas_call(
        unpack_kernel,
        out_shape=tuple(jax.ShapeDtypeStruct(shape, f32) for shape in shapes),
        in_specs=[vmem] * 5,
        out_specs=(vmem,) * 8,
        compiler_params=pltpu.CompilerParams(vmem_limit_bytes=32 * 2**20),
    )(*arrays)


def body(
    trunk_in, norm_gain, w_gate, w_up, w_down, w_cond, w_time, w_in, w_mid, w_res, w_out,
    tsteps, advantage, actions, noise,
):
    cond_all, w_cond_full = trunk(trunk_in, norm_gain, w_gate[0], w_up[0], w_down[0].T, w_cond)
    begin = 4 * lax.axis_index("segment") + 2 * lax.axis_index("mp")

    def own(values):
        return lax.dynamic_slice_in_dim(values, begin, 2, 0)

    parts = finish(
        cond_all, w_cond_full, w_cond, own(noise).reshape(FLATS * STEPS, 14), own(actions), tsteps.T, advantage.T,
        w_in, w_res, w_mid, w_out.T, w_time,
    )
    gin, gmid, gres, gout, gtime, gwc, gcond, loss = unpack(*parts)
    return gin.T, gmid.T, gres, gout.T, gtime, gwc, gcond, loss.reshape(1)


def solution(mesh):
    in_specs = (
        P("dp", "mp"),
        P("segment", None),
        P("segment", "dp", "mp"),
        P("segment", "dp", "mp"),
        P("segment", "mp", "dp"),
        P("mp", None),
        P(),
        P(),
        P(),
        P(),
        P(),
        P("dp", None),
        P("dp", None),
        P("dp", None, None),
        P("dp", None, None, None),
    )
    out_specs = (
        P(None, "segment"),
        P(None, "segment"),
        P(None, "segment"),
        P("segment", None),
        P(None, "segment"),
        P("mp", "segment"),
        P(("dp", "segment"), "mp"),
        P(),
    )
    return jax.shard_map(body, mesh=mesh, in_specs=in_specs, out_specs=out_specs, check_vma=False)
```
